512 devices in a mesh: tm: 16 (over y, core), head: 8 (over z), dp: 4 (over x).
Axes of the slice: x: 4, y: 8, z: 8, core: 2. Of those that a mesh axis runs over, the one named last changes fastest.
Arguments:
- frames: bfloat16 [4, 4096, 1280], P('dp', 'tm'), may hold values from -42 to 42
- masked: int32 [4, 4096], P('dp', 'tm'), may hold values from 0 to 1, as said below
- kept_counts: int32 [4, 16], P('dp', 'tm'), may hold values from 64 to 128, as said below
- teacher_qkv: bfloat16 [1280, 3, 1280], P('dp', None, 'head'), may hold values from -0.15625 to 0.15625
- student_gain: float32 [1280], replicated, may hold values from 0.1 to 1.9
- w_up: bfloat16 [1280, 5120], P('dp', 'head'), may hold values from -0.15625 to 0.15625
- w_down: bfloat16 [1280, 5120], P('dp', 'head'), may hold values from -0.078125 to 0.078125
Outputs:
- targets: bfloat16 [4, 4096, 1280], P('dp', 'tm', 'head')
- grad_up: float32 [1280, 5120], P('dp', 'head')
- grad_down: float32 [1280, 5120], P('dp', 'head')
The draws below stay inside these ranges and needn't reach their ends.
Inputs may be any that keep to these rules, and one draw needn't show every extreme that they name: `masked`: shard t of a sequence keeps exactly kept_counts of its 256 frames. `kept_counts`: every sequence has a shard that keeps 128 frames, and its shards keep 1536 frames together.
All inputs are finite; a program needn't handle non-finite values.
Results may differ from the reference program's by a relative error of at most 0.02.
Values may be sent and summed in bfloat16 or wider, within the bound.
A program may use at most 64 MiB of HBM per device.

```python
import math
import jax
import jax.numpy as jnp
from jax import lax

D = 1280
FF = 5120
HEADS = 16
HEAD_DIM = 80
T_DEV = 256
LEN = 4096
SEQS = 4
CAP = 128


def shard_counts(key):
    shards = LEN // T_DEV
    half = shards // 2
    key_spread, key_order = jax.random.split(jax.random.fold_in(key, 11))
    spread = jax.random.randint(key_spread, (SEQS, half), 0, T_DEV // 8 + 1)
    spread = spread.at[:, 0].set(T_DEV // 8)
    middle = 3 * T_DEV // 8
    counts = jnp.concatenate([middle + spread, middle - spread], axis=1)
    orders = jax.vmap(lambda sub: jax.random.permutation(sub, shards))(jax.random.split(key_order, SEQS))
    return jnp.take_along_axis(counts, orders, axis=1).astype(jnp.int32)


def draw_kept_counts(key, part):
    return shard_counts(key)


def draw_masked(key, part):
    counts = shard_counts(key)
    key = jax.random.fold_in(key, 5)
    shards = LEN // T_DEV
    ranks = jax.vmap(lambda sub: jax.random.permutation(sub, T_DEV))(jax.random.split(key, SEQS * shards))
    ranks = ranks.reshape(SEQS, shards, T_DEV)
    kept = ranks < counts[:, :, None]
    return jnp.where(kept, 0, 1).reshape(SEQS, LEN).astype(jnp.int32)


def draw_frames(key, part):
    key = jax.random.fold_in(key, 1)
    key_base = jax.random.fold_in(key, 0)
    values = jax.random.truncated_normal(key_base, -4.0, 4.0, (SEQS, LEN, D))
    return values.astype(jnp.float32).astype(jnp.bfloat16)


def levels(rng, dims, pieces, least, largest):
    level = 1.0
    for axis_at, shards_of in pieces:
        heights = jax.random.uniform(jax.random.fold_in(jax.random.fold_in(rng, 6), axis_at), (shards_of,), jnp.float32, least / len(pieces), largest / len(pieces))
        level = level * jnp.repeat(jnp.exp(heights), dims[axis_at] // shards_of).reshape((-1,) + (1,) * (len(dims) - 1 - axis_at))
    return level


def scatter_about(rng, dims, width, reach, cuts=(), kind=jnp.bfloat16):
    level = levels(rng, dims, cuts, -0.22, 0.18) if cuts else 1.0
    drawn = jax.random.normal(rng, dims, jnp.float32) * width * level
    return jnp.minimum(jnp.maximum(drawn, -reach), reach).astype(kind)


def setup_inputs(seed: int = 0) -> dict:
    splits = jax.random.split(jax.random.key(seed), 8)
    return {
        "frames": draw_frames(jax.random.fold_in(splits[7], 71), 0),
        "masked": draw_masked(jax.random.fold_in(splits[7], 71), 0),
        "kept_counts": draw_kept_counts(jax.random.fold_in(splits[7], 71), 0),
        "teacher_qkv": scatter_about(splits[3], (D, 3, D), D ** -0.5, 0.15625, ((0, 4), (2, 8))),
        "student_gain": jnp.clip(1.0 + 0.18 * jax.random.normal(splits[4], (D,), jnp.float32), 0.1, 1.9),
        "w_up": scatter_about(splits[5], (D, FF), D ** -0.5, 0.15625, ((0, 4), (1, 8))),
        "w_down": scatter_about(splits[6], (D, FF), FF ** -0.5, 0.078125, ((0, 4), (1, 8))),
    }


def gelu_exact(values):
    return jax.nn.gelu(values, approximate=False)

def teacher_context(sequence, teacher_qkv):
    qkv = jnp.einsum('td,dke->tke', sequence.astype(jnp.float32), teacher_qkv.astype(jnp.float32)).astype(jnp.bfloat16)
    query = qkv[:, 0].reshape(LEN, HEADS, HEAD_DIM)
    keys = qkv[:, 1].reshape(LEN, HEADS, HEAD_DIM)
    values = qkv[:, 2].reshape(LEN, HEADS, HEAD_DIM)
    scale = HEAD_DIM ** (-0.5)

    def one_head(operands):
        head_query, head_keys, head_values = operands
        scores = jnp.dot(head_query, head_keys.T, preferred_element_type=jnp.float32) * scale
        top = lax.optimization_barrier(jnp.max(scores, axis=1, keepdims=True))
        weights = jnp.exp(scores - top)
        total = lax.optimization_barrier(jnp.sum(weights, axis=1, keepdims=True))
        numer = jnp.dot(weights.astype(jnp.bfloat16), head_values, preferred_element_type=jnp.float32)
        return numer / total
    heads_out = lax.map(one_head, (query.transpose(1, 0, 2), keys.transpose(1, 0, 2), values.transpose(1, 0, 2)))
    return heads_out.transpose(1, 0, 2).reshape(LEN, D)

def reference(frames, masked, kept_counts, teacher_qkv, student_gain, w_up, w_down):
    target_list = []
    sum_up = jnp.zeros((D, FF), jnp.float32)
    sum_down = jnp.zeros((D, FF), jnp.float32)
    for seq in range(SEQS):
        sequence = frames[seq]
        context = teacher_context(sequence, teacher_qkv)
        mean = lax.optimization_barrier(jnp.mean(context, axis=0))
        var = lax.optimization_barrier(jnp.mean(context * context, axis=0)) - mean * mean
        target = (context - mean) * lax.rsqrt(var + 1e-05)
        target_list.append(target.astype(jnp.bfloat16))
        keep = (1 - masked[seq]).reshape(LEN // T_DEV, T_DEV)
        shard_x = sequence.reshape(LEN // T_DEV, T_DEV, D)
        shard_t = target.reshape(LEN // T_DEV, T_DEV, D)

        def shard_step(carry, operands):
            acc_up, acc_down = carry
            keep_row, rows_x, rows_t, count = operands
            index = jnp.nonzero(keep_row, size=CAP, fill_value=0)[0].astype(jnp.int32)
            valid = jnp.arange(CAP, dtype=jnp.int32) < count
            chosen = jnp.take(rows_x, index, axis=0).astype(jnp.float32)
            aim = jnp.take(rows_t, index, axis=0)
            centre = lax.optimization_barrier(jnp.mean(chosen, axis=1, keepdims=True))
            spread = lax.optimization_barrier(jnp.mean((chosen - centre) ** 2, axis=1, keepdims=True))
            normed = ((chosen - centre) * lax.rsqrt(spread + 1e-05) * student_gain).astype(jnp.bfloat16)
            pre = jnp.dot(normed, w_up, preferred_element_type=jnp.float32)
            act = gelu_exact(pre).astype(jnp.bfloat16)
            pred = jnp.dot(act, w_down.T, preferred_element_type=jnp.float32)
            cot = (jnp.where(valid[:, None], pred - aim, 0.0) * (2.0 / math.sqrt(D))).astype(jnp.bfloat16)
            d_act = jnp.dot(cot, w_down, preferred_element_type=jnp.float32)
            d_pre = jax.vjp(gelu_exact, pre)[1](d_act)[0].astype(jnp.bfloat16)
            g_down = jnp.dot(cot.T, act, preferred_element_type=jnp.float32).astype(jnp.bfloat16)
            g_up = jnp.dot(normed.T, d_pre, preferred_element_type=jnp.float32).astype(jnp.bfloat16)
            return ((acc_up + g_up.astype(jnp.float32), acc_down + g_down.astype(jnp.float32)), None)
        (sum_up, sum_down), unused = lax.scan(shard_step, (sum_up, sum_down), (keep, shard_x, shard_t, kept_counts[seq]))
    targets = jnp.stack(target_list)
    return (targets, sum_up, sum_down)
```

```python
import math

import jax
import jax.numpy as jnp
from jax import lax
from jax.experimental import pallas as pl
from jax.experimental.pallas import tpu as pltpu
from jax.sharding import PartitionSpec as P

BF16 = jnp.bfloat16
F32 = jnp.float32
MESH = pl.DeviceIdType.MESH

D = 1280
HEAD = 80
FRAMES = 256
SLOTS = 128
CHANNELS = 160
HIDDEN = 640
SHARD = 320
NX, NY, NZ = 4, 8, 8
NT = 2 * NY
PIECE = 208
STACK = NY * PIECE
LENGTH = NT * FRAMES
SCALE = HEAD**-0.5


def dot(a, b, dims):
    return lax.dot_general(a, b, (dims, ((), ())), preferred_element_type=F32)


class Names:
    def __init__(self):
        self.index = {}

    def __call__(self, name):
        return self.index.setdefault(name, len(self.index))


def kernel(
    frames_ref,
    masked_ref,
    counts_ref,
    gain_ref,
    wt_ref,
    up_ref,
    down_ref,
    target_ref,
    gup_ref,
    gdown_ref,
    wbuf,
    upbuf,
    downbuf,
    kv,
    normed_ref,
    normed_t,
    act_ref,
    slope_ref,
    dpre_ref,
    psend,
    precv,
    cot,
    stats,
    abuf,
    bbuf,
    g32,
    gs,
    rsb,
    fown,
    foth,
    local_sem,
    send_sem,
    recv_sem,
):
    t = lax.axis_index("tm")
    x = lax.axis_index("dp")
    z = lax.axis_index("head")
    y, c = t // 2, t % 2
    other = 1 - c
    partner = {"tm": y * 2 + other}

    def at_x(step):
        return lax.rem(x + step + NX, NX)

    def at_y(step):
        return lax.rem(y + step + NY, NY)

    def at_z(step):
        return lax.rem(z + step + NZ, NZ)

    barrier = pltpu.get_barrier_semaphore()
    peers = [partner]
    for step in range(1, NY):
        for core in range(2):
            peers.append({"tm": at_y(step) * 2 + core})
    for step in range(1, NX):
        for core in range(2):
            peers.append({"dp": at_x(step), "tm": y * 2 + core})
    for step in range(1, NZ):
        peers.append({"head": at_z(step)})
    for peer in peers:
        pl.semaphore_signal(barrier, inc=1, device_id=peer, device_id_type=MESH)
    pl.semaphore_wait(barrier, len(peers))

    names = Names()
    sent = []

    def describe(src, dst, device, name, out):
        return pltpu.make_async_remote_copy(
            src_ref=src,
            dst_ref=dst,
            send_sem=send_sem.at[out],
            recv_sem=recv_sem.at[name],
            device_id=device,
            device_id_type=MESH,
        )

    def send(src, dst, device, name):
        copy = describe(src, dst, device, names(name), len(sent))
        copy.start()
        sent.append(copy)

    def wait(dst, name):
        describe(dst, dst, partner, names(name), 0).wait_recv()

    def place_w(shard, row, rows):
        return wbuf.at[shard, pl.ds(row, rows), :]

    def place_up(shard, row, rows):
        return upbuf.at[pl.ds(shard * SHARD + row, rows), :]

    def place_down(shard, row, rows):
        return downbuf.at[pl.ds(shard * SHARD + row, rows), :]

    class Gather:
        def __init__(self, name, src, place, half, first, sem):
            self.name, self.src, self.place = name, src, place
            self.half, self.first = half, first
            self.mine, self.theirs = c * half, other * half
            self.own = pltpu.make_async_copy(src, place(x, 0, 2 * half), local_sem.at[sem])

        def start(self):
            self.own.start()
            mine = self.src.at[pl.ds(self.mine, self.half), :]
            there = self.place(x, self.mine, self.half)
            send(mine, there, {"dp": at_x(1)}, self.name + "R0")
            send(mine, there, {"dp": at_x(-1)}, self.name + "L0")

        def relay(self):
            n, first = self.half, self.first
            block = self.place(at_x(-1), self.mine, n)
            wait(block, self.name + "R0")
            part = self.place(at_x(-1), self.mine, first)
            send(part, part, {"dp": at_x(1)}, self.name + "R1")
            send(block, block, partner, self.name + "P0")
            block = self.place(at_x(1), self.mine, n)
            wait(block, self.name + "L0")
            part = self.place(at_x(1), self.mine + first, n - first)
            send(part, part, {"dp": at_x(-1)}, self.name + "L1")
            send(block, block, partner, self.name + "P1")

        def finish(self):
            n, first = self.half, self.first
            far = at_x(2)
            part = self.place(far, self.mine, first)
            wait(part, self.name + "R1")
            send(part, part, partner, self.name + "P2")
            part = self.place(far, self.mine + first, n - first)
            wait(part, self.name + "L1")
            send(part, part, partner, self.name + "P3")
            self.own.wait()
            wait(self.place(at_x(-1), self.theirs, n), self.name + "P0")
            wait(self.place(at_x(1), self.theirs, n), self.name + "P1")
            wait(self.place(far, self.theirs, first), self.name + "P2")
            wait(self.place(far, self.theirs + first, n - first), self.name + "P3")

    teacher = Gather("w", wt_ref, place_w, 240, 128, 0)
    upward = Gather("u", up_ref, place_up, 160, 80, 1)
    downward = Gather("d", down_ref, place_down, 160, 80, 2)

    teacher.start()

    keep = 1 - masked_ref[...]
    keep = keep.astype(F32)
    before = lax.broadcasted_iota(jnp.int32, (FRAMES, FRAMES), 0)
    after = lax.broadcasted_iota(jnp.int32, (FRAMES, FRAMES), 1)
    upper = jnp.where(before <= after, 1.0, 0.0).astype(BF16)
    rank = dot(jnp.broadcast_to(keep, (16, FRAMES)).astype(BF16), upper, ((1,), (0,)))[0:1]
    slot = lax.broadcasted_iota(jnp.int32, (SLOTS, FRAMES), 0).astype(F32)
    pick = jnp.where(rank - 1.0 == slot, jnp.broadcast_to(keep, (SLOTS, FRAMES)), 0.0).astype(BF16)
    chosen = dot(pick, frames_ref[...], ((1,), (0,)))
    centre = jnp.mean(chosen, axis=1, keepdims=True)
    chosen = chosen - centre
    spread = jnp.mean(chosen * chosen, axis=1, keepdims=True)
    normed = chosen * lax.rsqrt(spread + 1e-5) * gain_ref[...]
    normed_ref[...] = normed.astype(BF16)
    normed_t[...] = normed.T.astype(BF16)

    teacher.relay()
    upward.start()
    teacher.finish()

    qkv = jnp.zeros((3 * CHANNELS, FRAMES), F32)
    for shard in range(NX):
        qkv = qkv + dot(
            wbuf[shard], frames_ref[:, shard * SHARD : (shard + 1) * SHARD], ((1,), (1,))
        )
    qkv = qkv.astype(BF16)
    kv[y, c] = qkv[CHANNELS:]
    query = [qkv[h * HEAD : (h + 1) * HEAD] for h in range(2)]

    def block(source, core, part):
        return kv.at[source, core, pl.ds(part * CHANNELS, CHANNELS), :]

    right, left = {"tm": at_y(1) * 2 + c}, {"tm": at_y(-1) * 2 + c}
    for part, tag in ((0, "k"), (1, "v")):
        mine = block(y, c, part)
        send(mine, mine, right, tag + "R0")
        send(mine, mine, left, tag + "L0")
        send(mine, mine, partner, tag + "P0")

    best = [jnp.full((1, FRAMES), -jnp.inf, F32) for _ in range(2)]
    accum = [jnp.zeros((HEAD + 16, FRAMES), F32) for _ in range(2)]

    def attend(blocks):
        for h in range(2):
            keys = jnp.concatenate(
                [kv[s, core, h * HEAD : (h + 1) * HEAD, :] for s, core in blocks], axis=1
            )
            low = CHANNELS + h * HEAD
            values = jnp.concatenate(
                [kv[s, core, low : low + HEAD, :] for s, core in blocks], axis=1
            )
            values = jnp.concatenate([values, jnp.ones((16, values.shape[1]), BF16)], axis=0)
            scores = dot(keys, query[h], ((0,), (0,)))
            top = jnp.maximum(best[h], jnp.max(scores, axis=0, keepdims=True))
            fade = jnp.exp((best[h] - top) * SCALE)
            weights = jnp.exp((scores - top) * SCALE).astype(BF16)
            accum[h] = accum[h] * fade + dot(values, weights, ((1,), (0,)))
            best[h] = top

    def forward(step):
        behind, ahead = at_y(-step), at_y(step)
        for part, tag in ((0, "k"), (1, "v")):
            if step < 4 or part == 0:
                here = block(behind, c, part)
                wait(here, f"{tag}R{step - 1}")
                if step < 3 or (step == 3 and part == 0):
                    send(here, here, right, f"{tag}R{step}")
                send(here, here, partner, f"{tag}PR{step}")
            if step < 4 or part == 1:
                here = block(ahead, c, part)
                wait(here, f"{tag}L{step - 1}")
                if step < 3 or (step == 3 and part == 1):
                    send(here, here, left, f"{tag}L{step}")
                send(here, here, partner, f"{tag}PL{step}")

    def shared(step):
        for part, tag in ((0, "k"), (1, "v")):
            if step == 0:
                wait(block(y, other, part), tag + "P0")
                continue
            if step < 4 or part == 0:
                wait(block(at_y(-step), other, part), f"{tag}PR{step}")
            if step < 4 or part == 1:
                wait(block(at_y(step), other, part), f"{tag}PL{step}")

    me = x * 2 + c

    def operand(tag, role, source, target):
        for step in range(1, NX):
            out = len(sent)
            sem = names(f"{tag}{step}0")
            names(f"{tag}{step}1")
            copy = describe(
                source(at_x(step)), target.at[me], {"dp": at_x(step), "tm": y * 2 + role}, sem + c, out
            )
            copy.start()
            sent.append(copy)
        sem = names(f"{tag}00")
        names(f"{tag}01")
        out = len(sent)
        copy = describe(source(x), target.at[me], partner, sem + c, out)

        @pl.when(c == role)
        def _():
            target[me] = source(x)[...]

        @pl.when(c != role)
        def _():
            copy.start()

        sent.append((role, copy))

    def operands_here(tag, target):
        sem = names(f"{tag}00")
        describe(
            target.at[x * 2 + other], target.at[x * 2 + other], partner, sem + other, 0
        ).wait_recv()
        for step in range(1, NX):
            for core in range(2):
                here = target.at[at_x(-step) * 2 + core]
                describe(here, here, partner, names(f"{tag}{step}{core}"), 0).wait_recv()

    attend([(y, c)])
    shared(0)
    attend([(y, other)])
    forward(1)
    upward.relay()
    downward.start()
    attend([(at_y(-1), c), (at_y(1), c)])
    shared(1)
    attend([(at_y(-1), other), (at_y(1), other)])
    forward(2)
    upward.finish()
    attend([(at_y(-2), c), (at_y(2), c)])
    shared(2)

    pre = dot(normed_ref[...], upbuf[...], ((1,), (0,)))
    cumulative = 0.5 * (1.0 + lax.erf(pre * math.sqrt(0.5)))
    act_ref[...] = (pre * cumulative).astype(BF16)
    slope_ref[...] = cumulative + pre * (jnp.exp(-0.5 * pre * pre) * (1.0 / math.sqrt(2 * math.pi)))

    forward(3)
    downward.relay()
    operand("b", 0, lambda to: act_ref, bbuf)
    operand("a", 1, lambda to: normed_t.at[pl.ds(to * SHARD, SHARD), :], abuf)
    attend([(at_y(-2), other), (at_y(2), other)])
    attend([(at_y(-3), c), (at_y(3), c)])
    forward(4)
    downward.finish()

    psend[...] = dot(downbuf[...], act_ref[...], ((1,), (1,))).astype(BF16)
    for step in range(1, NZ):
        to = at_z(step)
        send(
            psend.at[pl.ds(to * CHANNELS, CHANNELS), :],
            precv.at[z],
            {"head": to},
            f"p{step}",
        )
    shared(3)
    attend([(at_y(-3), other), (at_y(3), other), (at_y(4), c)])
    shared(4)
    attend([(at_y(4), other)])

    context = [accum[h][:HEAD] / accum[h][HEAD : HEAD + 1] for h in range(2)]
    lane = lax.broadcasted_iota(jnp.int32, (HEAD, 128), 1)
    columns = jnp.zeros((HEAD, 128), F32)
    for h in range(2):
        first = jnp.sum(context[h], axis=1, keepdims=True)
        second = jnp.sum(context[h] * context[h], axis=1, keepdims=True)
        columns = jnp.where(lane == h, first, jnp.where(lane == 2 + h, second, columns))
    columns = jnp.concatenate([columns, jnp.zeros((128 - HEAD, 128), F32)], axis=0)
    stats[0] = columns.T[0:8]
    for step in range(1, NT):
        send(stats.at[0], stats.at[step], {"tm": lax.rem(t + step, NT)}, f"s{step}")
    total = stats[0]
    for step in range(1, NT):
        wait(stats.at[step], f"s{step}")
        total = total + stats[step]
    columns = jnp.concatenate([total, jnp.zeros((120, 128), F32)], axis=0).T
    parts = []
    for h in range(2):
        mean = columns[:HEAD, h : h + 1] * (1.0 / LENGTH)
        var = columns[:HEAD, 2 + h : 3 + h] * (1.0 / LENGTH) - mean * mean
        parts.append((context[h] - mean) * lax.rsqrt(var + 1e-5))
    target = jnp.concatenate(parts, axis=0).astype(BF16)
    target_ref[...] = target

    aim = dot(target, pick, ((1,), (1,)))
    pred = psend[pl.ds(z * CHANNELS, CHANNELS), :].astype(F32)
    for step in range(1, NZ):
        wait(precv.at[at_z(-step)], f"p{step}")
        pred = pred + precv[at_z(-step)].astype(F32)
    number = lax.broadcasted_iota(jnp.int32, (CHANNELS, SLOTS), 1)
    valid = number < jnp.broadcast_to(counts_ref[...], (CHANNELS, SLOTS))
    gap = jnp.where(valid, pred - aim, 0.0) * (2.0 / math.sqrt(D))
    here = cot.at[pl.ds(z * CHANNELS, CHANNELS), :]
    here[...] = gap.astype(BF16)
    for step in range(1, NZ):
        send(here, here, {"head": at_z(step)}, f"c{step}")
    for step in range(1, NZ):
        wait(cot.at[pl.ds(at_z(-step) * CHANNELS, CHANNELS), :], f"c{step}")

    operand("a", 0, lambda to: cot.at[pl.ds(to * SHARD, SHARD), :], abuf)
    back = dot(cot[...], downbuf[...], ((0,), (0,)))
    dpre_ref[...] = (back * slope_ref[...]).astype(BF16)
    operand("b", 1, lambda to: dpre_ref, bbuf)

    operands_here("a", abuf)
    operands_here("b", bbuf)
    grad = jnp.zeros((SHARD, HIDDEN), F32)
    for pair in range(NX):
        rows = jnp.concatenate([abuf[2 * pair], abuf[2 * pair + 1]], axis=1)
        columns = jnp.concatenate([bbuf[2 * pair], bbuf[2 * pair + 1]], axis=0)
        grad = grad + dot(rows, columns, ((1,), (0,)))
    for band in range(HIDDEN // 128):
        stripe = grad[:, band * 128 : (band + 1) * 128]
        g32[band * SHARD : (band + 1) * SHARD, :] = stripe
        gs[band * SHARD : (band + 1) * SHARD, :] = stripe.astype(BF16)
    rest = STACK - SHARD * HIDDEN // 128
    g32[STACK - rest :, :] = jnp.zeros((rest, 128), F32)
    gs[STACK - rest :, :] = jnp.zeros((rest, 128), BF16)

    for step in range(1, NY):
        to = at_y(step)
        send(gs.at[pl.ds(to * PIECE, PIECE), :], rsb.at[step - 1], {"tm": to * 2 + c}, f"r{step}")
    total = g32[pl.ds(y * PIECE, PIECE), :]
    for step in range(1, NY):
        wait(rsb.at[step - 1], f"r{step}")
        total = total + rsb[step - 1].astype(F32)
    here = fown.at[pl.ds(y * PIECE, PIECE), :]
    here[...] = total.astype(BF16)
    for step in range(1, NY):
        send(here, here, {"tm": at_y(step) * 2 + c}, f"g{step}")
    send(here, foth.at[pl.ds(y * PIECE, PIECE), :], partner, "h0")
    for step in range(1, NY):
        rows = pl.ds(at_y(-step) * PIECE, PIECE)
        wait(fown.at[rows, :], f"g{step}")
        send(fown.at[rows, :], foth.at[rows, :], partner, f"h{step}")
    for step in range(NY):
        wait(foth.at[pl.ds(at_y(-step) * PIECE, PIECE), :], f"h{step}")

    def unstack(source, out):
        for band in range(HIDDEN // 128):
            out[:, band * 128 : (band + 1) * 128] = source[band * SHARD : (band + 1) * SHARD, :]

    @pl.when(c == 0)
    def _():
        unstack(fown, gdown_ref)
        unstack(foth, gup_ref)

    @pl.when(c != 0)
    def _():
        unstack(fown, gup_ref)
        unstack(foth, gdown_ref)

    for copy in sent:
        if isinstance(copy, tuple):
            role, copy = copy

            @pl.when(c != role)
            def _():
                copy.wait_send()
        else:
            copy.wait_send()


def local(frames, masked, kept_counts, teacher_qkv, student_gain, w_up, w_down):
    wt = teacher_qkv.transpose(1, 2, 0).reshape(3 * CHANNELS, SHARD)
    vmem = pl.BlockSpec(memory_space=pltpu.VMEM)
    hbm = pl.BlockSpec(memory_space=pl.ANY)
    target, gup, gdown = pl.pallas_call(
        kernel,
        out_shape=(
            jax.ShapeDtypeStruct((CHANNELS, FRAMES), BF16),
            jax.ShapeDtypeStruct((SHARD, HIDDEN), BF16),
            jax.ShapeDtypeStruct((SHARD, HIDDEN), BF16),
        ),
        in_specs=[vmem, vmem, vmem, vmem, hbm, hbm, hbm],
        out_specs=(vmem, vmem, vmem),
        scratch_shapes=[
            pltpu.VMEM((NX, 3 * CHANNELS, SHARD), BF16),
            pltpu.VMEM((D, HIDDEN), BF16),
            pltpu.VMEM((D, HIDDEN), BF16),
            pltpu.VMEM((NY, 2, 2 * CHANNELS, FRAMES), BF16),
            pltpu.VMEM((SLOTS, D), BF16),
            pltpu.VMEM((D, SLOTS), BF16),
            pltpu.VMEM((SLOTS, HIDDEN), BF16),
            pltpu.VMEM((SLOTS, HIDDEN), F32),
            pltpu.VMEM((SLOTS, HIDDEN), BF16),
            pltpu.VMEM((D, SLOTS), BF16),
            pltpu.VMEM((NZ, CHANNELS, SLOTS), BF16),
            pltpu.VMEM((D, SLOTS), BF16),
            pltpu.VMEM((NT, 8, 128), F32),
            pltpu.VMEM((2 * NX, SHARD, SLOTS), BF16),
            pltpu.VMEM((2 * NX, SLOTS, HIDDEN), BF16),
            pltpu.VMEM((STACK, 128), F32),
            pltpu.VMEM((STACK, 128), BF16),
            pltpu.VMEM((NY - 1, PIECE, 128), BF16),
            pltpu.VMEM((STACK, 128), BF16),
            pltpu.VMEM((STACK, 128), BF16),
            pltpu.SemaphoreType.DMA((3,)),
            pltpu.SemaphoreType.DMA((192,)),
            pltpu.SemaphoreType.DMA((160,)),
        ],
        compiler_params=pltpu.CompilerParams(
            collective_id=0, has_side_effects=True, vmem_limit_bytes=48 * 1024 * 1024
        ),
    )(
        frames[0],
        masked,
        kept_counts,
        student_gain[None],
        wt,
        w_up,
        w_down,
    )
    return target.T[None], gup.astype(F32), gdown.astype(F32)


def solution(mesh):
    placed = (
        P("dp", "tm", None),
        P("dp", "tm"),
        P("dp", "tm"),
        P("dp", None, "head"),
        P(),
        P("dp", "head"),
        P("dp", "head"),
    )
    return jax.shard_map(
        local,
        mesh=mesh,
        in_specs=placed,
        out_specs=(P("dp", "tm", "head"), P("dp", "head"), P("dp", "head")),
        check_vma=False,
    )
```

```python
import math

import jax
import jax.numpy as jnp
from jax import lax
from jax.experimental import pallas as pl
from jax.experimental.pallas import tpu as pltpu
from jax.sharding import PartitionSpec as P

BF16 = jnp.bfloat16
F32 = jnp.float32
MESH = pl.DeviceIdType.MESH

D = 1280
HEAD = 80
FRAMES = 256
SLOTS = 128
CHANNELS = 160
HIDDEN = 640
SHARD = 320
NX, NY, NZ = 4, 8, 8
NT = 2 * NY
PIECE = 208
STACK = NY * PIECE
CHUNKS = ((0, 2, 80), (2, 2, 80), (4, 1, 48))
NEAR = (1, 3, 2)
LENGTH = NT * FRAMES
SCALE = HEAD**-0.5


def dot(a, b, dims):
    return lax.dot_general(a, b, (dims, ((), ())), preferred_element_type=F32)


class Names:
    def __init__(self):
        self.index = {}

    def __call__(self, name):
        return self.index.setdefault(name, len(self.index))


def kernel(
    frames_hbm,
    masked_ref,
    counts_ref,
    gain_ref,
    wt_ref,
    up_ref,
    down_ref,
    target_ref,
    gup_ref,
    gdown_ref,
    frames_ref,
    wbuf,
    upbuf,
    downbuf,
    kv,
    normed_ref,
    normed_t,
    act_ref,
    slope_ref,
    dpre_ref,
    psend,
    precv,
    cot,
    stats,
    abuf,
    bbuf,
    g32,
    gs,
    rsb,
    fown,
    foth,
    local_sem,
    send_sem,
    recv_sem,
):
    t = lax.axis_index("tm")
    x = lax.axis_index("dp")
    z = lax.axis_index("head")
    y, c = t // 2, t % 2
    other = 1 - c
    partner = {"tm": y * 2 + other}

    def at_x(step):
        return lax.rem(x + step + NX, NX)

    def at_y(step):
        return lax.rem(y + step + NY, NY)

    def at_z(step):
        return lax.rem(z + step + NZ, NZ)

    fetch = pltpu.make_async_copy(frames_hbm, frames_ref, local_sem.at[4])
    fetch.start()

    barrier = pltpu.get_barrier_semaphore()
    peers = [partner]
    for step in range(1, NY):
        for core in range(2):
            peers.append({"tm": at_y(step) * 2 + core})
    for step in range(1, NX):
        for core in range(2):
            peers.append({"dp": at_x(step), "tm": y * 2 + core})
    for step in range(1, NZ):
        peers.append({"head": at_z(step)})
    for peer in peers:
        pl.semaphore_signal(barrier, inc=1, device_id=peer, device_id_type=MESH)
    pl.semaphore_wait(barrier, len(peers))

    names = Names()
    sent = []

    def describe(src, dst, device, name, out):
        return pltpu.make_async_remote_copy(
            src_ref=src,
            dst_ref=dst,
            send_sem=send_sem.at[out],
            recv_sem=recv_sem.at[name],
            device_id=device,
            device_id_type=MESH,
        )

    def send(src, dst, device, name):
        copy = describe(src, dst, device, names(name), len(sent))
        copy.start()
        sent.append(copy)

    def wait(dst, name):
        describe(dst, dst, partner, names(name), 0).wait_recv()

    def place_w(shard, row, rows):
        return wbuf.at[shard, pl.ds(row, rows), :]

    def place_up(shard, row, rows):
        return upbuf.at[pl.ds(shard * SHARD + row, rows), :]

    def place_down(shard, row, rows):
        return downbuf.at[pl.ds(shard * SHARD + row, rows), :]

    class Direct:
        def __init__(self, name, src, place, base, half, sem):
            self.name, self.src, self.place, self.half = name, src, place, half
            self.mine, self.theirs = base + c * half, base + other * half
            self.own = pltpu.make_async_copy(
                src.at[pl.ds(base, 2 * half), :], place(x, base, 2 * half), local_sem.at[sem]
            )

        def start(self):
            mine = self.src.at[pl.ds(self.mine, self.half), :]
            there = self.place(x, self.mine, self.half)
            for step in NEAR:
                send(mine, there, {"dp": at_x(step)}, f"{self.name}{step}")
            self.own.start()

        def share(self):
            for step in NEAR:
                block = self.place(at_x(-step), self.mine, self.half)
                wait(block, f"{self.name}{step}")
                send(block, block, partner, f"{self.name}P{step}")

        def finish(self):
            self.own.wait()
            for step in NEAR:
                wait(self.place(at_x(-step), self.theirs, self.half), f"{self.name}P{step}")

    class Relay:
        def __init__(self, name, src, place, half, first, sem):
            self.name, self.src, self.place = name, src, place
            self.half, self.first = half, first
            self.mine, self.theirs = c * half, other * half
            self.own = pltpu.make_async_copy(src, place(x, 0, 2 * half), local_sem.at[sem])

        def start(self):
            mine = self.src.at[pl.ds(self.mine, self.half), :]
            there = self.place(x, self.mine, self.half)
            send(mine, there, {"dp": at_x(1)}, self.name + "R0")
            send(mine, there, {"dp": at_x(-1)}, self.name + "L0")
            self.own.start()

        def relay(self):
            n, first = self.half, self.first
            block = self.place(at_x(-1), self.mine, n)
            wait(block, self.name + "R0")
            part = self.place(at_x(-1), self.mine, first)
            send(part, part, {"dp": at_x(1)}, self.name + "R1")
            send(block, block, partner, self.name + "P0")
            block = self.place(at_x(1), self.mine, n)
            wait(block, self.name + "L0")
            part = self.place(at_x(1), self.mine + first, n - first)
            send(part, part, {"dp": at_x(-1)}, self.name + "L1")
            send(block, block, partner, self.name + "P1")

        def share(self):
            n, first = self.half, self.first
            far = at_x(2)
            part = self.place(far, self.mine, first)
            wait(part, self.name + "R1")
            send(part, part, partner, self.name + "P2")
            part = self.place(far, self.mine + first, n - first)
            wait(part, self.name + "L1")
            send(part, part, partner, self.name + "P3")

        def near(self):
            n = self.half
            self.own.wait()
            wait(self.place(at_x(-1), self.theirs, n), self.name + "P0")
            wait(self.place(at_x(1), self.theirs, n), self.name + "P1")

        def far(self):
            n, first = self.half, self.first
            wait(self.place(at_x(2), self.theirs, first), self.name + "P2")
            wait(self.place(at_x(2), self.theirs + first, n - first), self.name + "P3")

    teacher_kv = Direct("w", wt_ref, place_w, CHANNELS, CHANNELS, 0)
    teacher_q = Direct("q", wt_ref, place_w, 0, HEAD, 3)
    upward = Relay("u", up_ref, place_up, 160, 80, 1)
    downward = Relay("d", down_ref, place_down, 160, 80, 2)

    teacher_kv.start()

    keep = 1 - masked_ref[...]
    keep = keep.astype(F32)
    before = lax.broadcasted_iota(jnp.int32, (FRAMES, FRAMES), 0)
    after = lax.broadcasted_iota(jnp.int32, (FRAMES, FRAMES), 1)
    upper = jnp.where(before <= after, 1.0, 0.0).astype(BF16)
    rank = dot(jnp.broadcast_to(keep, (16, FRAMES)).astype(BF16), upper, ((1,), (0,)))[0:1]
    slot = lax.broadcasted_iota(jnp.int32, (SLOTS, FRAMES), 0).astype(F32)
    pick = jnp.where(rank - 1.0 == slot, jnp.broadcast_to(keep, (SLOTS, FRAMES)), 0.0).astype(BF16)
    fetch.wait()
    chosen = dot(pick, frames_ref[...], ((1,), (0,)))
    centre = jnp.mean(chosen, axis=1, keepdims=True)
    chosen = chosen - centre
    spread = jnp.mean(chosen * chosen, axis=1, keepdims=True)
    normed = chosen * lax.rsqrt(spread + 1e-5) * gain_ref[...].reshape(1, D)
    normed_ref[...] = normed.astype(BF16)
    normed_t[...] = normed.T.astype(BF16)

    def project(low, high):
        out = jnp.zeros((high - low, FRAMES), F32)
        for shard in range(NX):
            out = out + dot(
                wbuf[shard, low:high, :], frames_ref[:, shard * SHARD : (shard + 1) * SHARD], ((1,), (1,))
            )
        return out.astype(BF16)

    def block(source, core, part):
        return kv.at[source, core, pl.ds(part * CHANNELS, CHANNELS), :]

    teacher_kv.share()
    teacher_q.start()
    teacher_kv.finish()
    kv[y, c] = project(CHANNELS, 3 * CHANNELS)
    right, left = {"tm": at_y(1) * 2 + c}, {"tm": at_y(-1) * 2 + c}
    for part, tag in ((0, "k"), (1, "v")):
        mine = block(y, c, part)
        send(mine, mine, right, tag + "R0")
        send(mine, mine, left, tag + "L0")
        send(mine, mine, partner, tag + "P0")
    upward.start()
    teacher_q.share()
    teacher_q.finish()
    downward.start()
    query = project(0, CHANNELS)
    query = [query[h * HEAD : (h + 1) * HEAD] for h in range(2)]

    best = [jnp.full((1, FRAMES), -jnp.inf, F32) for _ in range(2)]
    accum = [jnp.zeros((HEAD + 16, FRAMES), F32) for _ in range(2)]

    def attend(blocks):
        for h in range(2):
            keys = jnp.concatenate(
                [kv[s, core, h * HEAD : (h + 1) * HEAD, :] for s, core in blocks], axis=1
            )
            low = CHANNELS + h * HEAD
            values = jnp.concatenate(
                [kv[s, core, low : low + HEAD, :] for s, core in blocks], axis=1
            )
            values = jnp.concatenate([values, jnp.ones((16, values.shape[1]), BF16)], axis=0)
            scores = dot(keys, query[h], ((0,), (0,)))
            top = jnp.maximum(best[h], jnp.max(scores, axis=0, keepdims=True))
            fade = jnp.exp((best[h] - top) * SCALE)
            weights = jnp.exp((scores - top) * SCALE).astype(BF16)
            accum[h] = accum[h] * fade + dot(values, weights, ((1,), (0,)))
            best[h] = top

    def forward(step):
        behind, ahead = at_y(-step), at_y(step)
        for part, tag in ((0, "k"), (1, "v")):
            if step < 4 or part == 0:
                here = block(behind, c, part)
                wait(here, f"{tag}R{step - 1}")
                if step < 3 or (step == 3 and part == 0):
                    send(here, here, right, f"{tag}R{step}")
                send(here, here, partner, f"{tag}PR{step}")
            if step < 4 or part == 1:
                here = block(ahead, c, part)
                wait(here, f"{tag}L{step - 1}")
                if step < 3 or (step == 3 and part == 1):
                    send(here, here, left, f"{tag}L{step}")
                send(here, here, partner, f"{tag}PL{step}")

    def shared(step):
        for part, tag in ((0, "k"), (1, "v")):
            if step == 0:
                wait(block(y, other, part), tag + "P0")
                continue
            if step < 4 or part == 0:
                wait(block(at_y(-step), other, part), f"{tag}PR{step}")
            if step < 4 or part == 1:
                wait(block(at_y(step), other, part), f"{tag}PL{step}")

    me = x * 2 + c

    def operand(tag, role, source, place):
        for step in NEAR:
            sem = names(f"{tag}{step}0")
            names(f"{tag}{step}1")
            copy = describe(
                source(at_x(step)), place(me), {"dp": at_x(step), "tm": y * 2 + role}, sem + c, len(sent)
            )
            copy.start()
            sent.append(copy)
        sem = names(f"{tag}00")
        names(f"{tag}01")
        copy = describe(source(x), place(me), partner, sem + c, len(sent))

        @pl.when(c == role)
        def _():
            place(me)[...] = source(x)[...]

        @pl.when(c != role)
        def _():
            copy.start()

        sent.append((c != role, copy))

    def operand_here(tag, place):
        here = place(x * 2 + other)
        describe(here, here, partner, names(f"{tag}00") + other, 0).wait_recv()
        for step in NEAR:
            for core in range(2):
                here = place(at_x(-step) * 2 + core)
                describe(here, here, partner, names(f"{tag}{step}{core}"), 0).wait_recv()

    def whole_a(source):
        return abuf.at[source]

    def whole_b(source):
        return bbuf.at[source]

    attend([(y, c)])
    shared(0)
    attend([(y, other)])
    forward(1)
    attend([(at_y(-1), c), (at_y(1), c)])
    shared(1)
    attend([(at_y(-1), other), (at_y(1), other)])
    forward(2)
    upward.relay()
    attend([(at_y(-2), c), (at_y(2), c)])
    shared(2)
    attend([(at_y(-2), other), (at_y(2), other)])
    forward(3)
    downward.relay()
    attend([(at_y(-3), c), (at_y(3), c)])
    upward.share()
    shared(3)
    attend([(at_y(-3), other), (at_y(3), other)])
    forward(4)
    attend([(at_y(4), c)])
    shared(4)
    attend([(at_y(4), other)])

    context = [accum[h][:HEAD] / accum[h][HEAD : HEAD + 1] for h in range(2)]
    lane = lax.broadcasted_iota(jnp.int32, (HEAD, 128), 1)
    columns = jnp.zeros((HEAD, 128), F32)
    for h in range(2):
        first = jnp.sum(context[h], axis=1, keepdims=True)
        second = jnp.sum(context[h] * context[h], axis=1, keepdims=True)
        columns = jnp.where(lane == h, first, jnp.where(lane == 2 + h, second, columns))
    columns = jnp.concatenate([columns, jnp.zeros((128 - HEAD, 128), F32)], axis=0)
    stats[0] = columns.T[0:8]
    for step in range(1, NT):
        send(stats.at[0], stats.at[step], {"tm": lax.rem(t + step, NT)}, f"s{step}")

    downward.share()
    upward.near()
    upward.far()
    pre = dot(normed_ref[...], upbuf[...], ((1,), (0,)))
    cumulative = 0.5 * (1.0 + lax.erf(pre * math.sqrt(0.5)))
    act_ref[...] = (pre * cumulative).astype(BF16)
    slope_ref[...] = cumulative + pre * (jnp.exp(-0.5 * pre * pre) * (1.0 / math.sqrt(2 * math.pi)))

    def predict(shard, step):
        rows = pl.ds(shard * SHARD, SHARD)
        psend[rows, :] = dot(downbuf[rows, :], act_ref[...], ((1,), (1,))).astype(BF16)
        for half in range(2):
            to = shard * 2 + half
            copy = describe(
                psend.at[pl.ds(to * CHANNELS, CHANNELS), :],
                precv.at[z],
                {"head": to},
                names("p0") + lax.rem(to - z + NZ, NZ),
                len(sent),
            )

            @pl.when(to != z)
            def _():
                copy.start()

            sent.append((to != z, copy))

    for step in range(NZ):
        names(f"p{step}")
    downward.near()
    for step in (0, 1, 3):
        predict(at_x(step), step)
    downward.far()
    predict(at_x(2), 2)
    operand("act", 0, lambda to: act_ref, whole_b)
    operand("nrm", 1, lambda to: normed_t.at[pl.ds(to * SHARD, SHARD), :], whole_a)

    total = stats[0]
    for step in range(1, NT):
        wait(stats.at[step], f"s{step}")
        total = total + stats[step]
    columns = jnp.concatenate([total, jnp.zeros((120, 128), F32)], axis=0).T
    parts = []
    for h in range(2):
        mean = columns[:HEAD, h : h + 1] * (1.0 / LENGTH)
        var = columns[:HEAD, 2 + h : 3 + h] * (1.0 / LENGTH) - mean * mean
        parts.append((context[h] - mean) * lax.rsqrt(var + 1e-5))
    target = jnp.concatenate(parts, axis=0).astype(BF16)
    target_ref[...] = target

    aim = dot(target, pick, ((1,), (1,)))
    pred = psend[pl.ds(z * CHANNELS, CHANNELS), :].astype(F32)
    for step in range(1, NZ):
        wait(precv.at[at_z(-step)], f"p{step}")
        pred = pred + precv[at_z(-step)].astype(F32)
    number = lax.broadcasted_iota(jnp.int32, (CHANNELS, SLOTS), 1)
    valid = number < jnp.broadcast_to(counts_ref[...], (CHANNELS, SLOTS))
    gap = jnp.where(valid, pred - aim, 0.0) * (2.0 / math.sqrt(D))
    here = cot.at[pl.ds(z * CHANNELS, CHANNELS), :]
    here[...] = gap.astype(BF16)
    for step in (1, 7, 2, 6, 3, 5, 4):
        send(here, here, {"head": at_z(step)}, f"c{step}")

    for step in range(4 * NX):
        names(f"e{step}")

    def half_a(source, half):
        return abuf.at[source, pl.ds(half * CHANNELS, CHANNELS), :]

    def pass_on(owner):
        to, half = owner // 2, lax.rem(owner, 2)
        source = cot.at[pl.ds(owner * CHANNELS, CHANNELS), :]
        sem = names("e0") + lax.rem(to - x + NX, NX) * 4 + c * 2 + half
        copy = describe(source, half_a(me, half), {"dp": to, "tm": y * 2}, sem, len(sent))
        mine = jnp.logical_and(to == x, c == 0)
        away = jnp.logical_not(mine)

        @pl.when(mine)
        def _():
            half_a(me, half)[...] = source[...]

        @pl.when(away)
        def _():
            copy.start()

        sent.append((away, copy))

    def back_from(owner):
        rows = pl.ds(owner * CHANNELS, CHANNELS)
        return dot(cot[rows, :], downbuf[rows, :], ((0,), (0,)))

    pass_on(z)
    back = back_from(z)
    for step in (1, 7, 2, 6, 3, 5, 4):
        owner = at_z(-step)
        wait(cot.at[pl.ds(owner * CHANNELS, CHANNELS), :], f"c{step}")
        pass_on(owner)
        back = back + back_from(owner)
    dpre_ref[...] = (back * slope_ref[...]).astype(BF16)
    for number, (band, bands, _) in enumerate(CHUNKS):
        columns = pl.ds(band * 128, bands * 128)
        operand(
            f"m{number}",
            1,
            lambda to: dpre_ref.at[:, columns],
            lambda source: bbuf.at[source, :, columns],
        )

    @pl.when(c == 0)
    def _():
        operand_here("act", whole_b)
        for step in (0, *NEAR):
            for core in range(2):
                for half in range(2):
                    here = half_a(at_x(-step) * 2 + core, half)
                    copy = describe(
                        here, here, partner, names("e0") + step * 4 + core * 2 + half, 0
                    )
                    if (step, core) != (0, 0):
                        copy.wait_recv()

    @pl.when(c != 0)
    def _():
        operand_here("nrm", whole_a)

    def eighth(number, which):
        band, _, rows = CHUNKS[number]
        return pl.ds(band * SHARD + which * rows, rows)

    def landing(number, step):
        band, _, rows = CHUNKS[number]
        return rsb.at[step - 1, pl.ds(band * SHARD // NY, rows), :]

    rest = STACK - SHARD * HIDDEN // 128
    g32[STACK - rest :, :] = jnp.zeros((rest, 128), F32)
    gs[STACK - rest :, :] = jnp.zeros((rest, 128), BF16)
    for number, (band, bands, _) in enumerate(CHUNKS):
        columns = pl.ds(band * 128, bands * 128)

        @pl.when(c != 0)
        def _():
            operand_here(f"m{number}", lambda source: bbuf.at[source, :, columns])

        grad = jnp.zeros((SHARD, bands * 128), F32)
        for pair in range(NX):
            rows = jnp.concatenate([abuf[2 * pair], abuf[2 * pair + 1]], axis=1)
            inner = jnp.concatenate([bbuf[2 * pair, :, columns], bbuf[2 * pair + 1, :, columns]], axis=0)
            grad = grad + dot(rows, inner, ((1,), (0,)))
        for at in range(bands):
            stripe = grad[:, at * 128 : (at + 1) * 128]
            low = (band + at) * SHARD
            g32[low : low + SHARD, :] = stripe
            gs[low : low + SHARD, :] = stripe.astype(BF16)
        for step in (1, 7, 2, 6, 3, 5, 4):
            to = at_y(step)
            send(
                gs.at[eighth(number, to), :],
                landing(number, step),
                {"tm": to * 2 + c},
                f"r{number}{step}",
            )

    for number in range(len(CHUNKS)):
        total = g32[eighth(number, y), :]
        for step in range(1, NY):
            wait(landing(number, step), f"r{number}{step}")
            total = total + landing(number, step)[...].astype(F32)
        here = fown.at[eighth(number, y), :]
        here[...] = total.astype(BF16)
        for step in (1, 7, 2, 6, 3, 5, 4):
            send(here, here, {"tm": at_y(step) * 2 + c}, f"g{number}{step}")
        send(here, foth.at[eighth(number, y), :], partner, f"h{number}0")
    for number in range(len(CHUNKS)):
        for step in (1, 7, 2, 6, 3, 5, 4):
            rows = eighth(number, at_y(-step))
            wait(fown.at[rows, :], f"g{number}{step}")
            send(fown.at[rows, :], foth.at[rows, :], partner, f"h{number}{step}")
    for number in range(len(CHUNKS)):
        for step in range(NY):
            wait(foth.at[eighth(number, at_y(-step)), :], f"h{number}{step}")

    def unstack(source, out):
        for band in range(HIDDEN // 128):
            out[:, band * 128 : (band + 1) * 128] = source[band * SHARD : (band + 1) * SHARD, :]

    @pl.when(c == 0)
    def _():
        unstack(fown, gdown_ref)
        unstack(foth, gup_ref)

    @pl.when(c != 0)
    def _():
        unstack(fown, gup_ref)
        unstack(foth, gdown_ref)

    for copy in sent:
        if isinstance(copy, tuple):
            started, copy = copy

            @pl.when(started)
            def _():
                copy.wait_send()
        else:
            copy.wait_send()


def local(frames, masked, kept_counts, teacher_qkv, student_gain, w_up, w_down):
    wt = teacher_qkv.transpose(1, 2, 0).reshape(3 * CHANNELS, SHARD)
    vmem = pl.BlockSpec(memory_space=pltpu.VMEM)
    hbm = pl.BlockSpec(memory_space=pl.ANY)
    target, gup, gdown = pl.pallas_call(
        kernel,
        out_shape=(
            jax.ShapeDtypeStruct((CHANNELS, FRAMES), BF16),
            jax.ShapeDtypeStruct((SHARD, HIDDEN), BF16),
            jax.ShapeDtypeStruct((SHARD, HIDDEN), BF16),
        ),
        in_specs=[hbm, vmem, vmem, vmem, hbm, hbm, hbm],
        out_specs=(vmem, vmem, vmem),
        scratch_shapes=[
            pltpu.VMEM((FRAMES, D), BF16),
            pltpu.VMEM((NX, 3 * CHANNELS, SHARD), BF16),
            pltpu.VMEM((D, HIDDEN), BF16),
            pltpu.VMEM((D, HIDDEN), BF16),
            pltpu.VMEM((NY, 2, 2 * CHANNELS, FRAMES), BF16),
            pltpu.VMEM((SLOTS, D), BF16),
            pltpu.VMEM((D, SLOTS), BF16),
            pltpu.VMEM((SLOTS, HIDDEN), BF16),
            pltpu.VMEM((SLOTS, HIDDEN), F32),
            pltpu.VMEM((SLOTS, HIDDEN), BF16),
            pltpu.VMEM((D, SLOTS), BF16),
            pltpu.VMEM((NZ, CHANNELS, SLOTS), BF16),
            pltpu.VMEM((D, SLOTS), BF16),
            pltpu.VMEM((NT, 8, 128), F32),
            pltpu.VMEM((2 * NX, SHARD, SLOTS), BF16),
            pltpu.VMEM((2 * NX, SLOTS, HIDDEN), BF16),
            pltpu.VMEM((STACK, 128), F32),
            pltpu.VMEM((STACK, 128), BF16),
            pltpu.VMEM((NY - 1, PIECE, 128), BF16),
            pltpu.VMEM((STACK, 128), BF16),
            pltpu.VMEM((STACK, 128), BF16),
            pltpu.SemaphoreType.DMA((5,)),
            pltpu.SemaphoreType.DMA((256,)),
            pltpu.SemaphoreType.DMA((256,)),
        ],
        compiler_params=pltpu.CompilerParams(
            collective_id=0, has_side_effects=True, vmem_limit_bytes=60 * 1024 * 1024
        ),
    )(
        frames[0],
        masked,
        kept_counts,
        student_gain,
        wt,
        w_up,
        w_down,
    )
    return target.T[None], gup.astype(F32), gdown.astype(F32)


def solution(mesh):
    placed = (
        P("dp", "tm", None),
        P("dp", "tm"),
        P("dp", "tm"),
        P("dp", None, "head"),
        P(),
        P("dp", "head"),
        P("dp", "head"),
    )
    return jax.shard_map(
        local,
        mesh=mesh,
        in_specs=placed,
        out_specs=(P("dp", "tm", "head"), P("dp", "head"), P("dp", "head")),
        check_vma=False,
    )
```

```python
import math

import jax
import jax.numpy as jnp
from jax import lax
from jax.experimental import pallas as pl
from jax.experimental.pallas import tpu as pltpu
from jax.sharding import PartitionSpec as P

BF16 = jnp.bfloat16
F32 = jnp.float32
MESH = pl.DeviceIdType.MESH

D = 1280
HEAD = 80
FRAMES = 256
SLOTS = 128
CHANNELS = 160
HIDDEN = 640
SHARD = 320
NX, NY, NZ = 4, 8, 8
NT = 2 * NY
PIECE = 208
STACK = NY * PIECE
CHUNKS = ((0, 2, 80), (2, 2, 80), (4, 1, 48))
NEAR = (1, 3, 2)
LENGTH = NT * FRAMES
SCALE = HEAD**-0.5


def dot(a, b, dims):
    return lax.dot_general(a, b, (dims, ((), ())), preferred_element_type=F32)


class Names:
    def __init__(self):
        self.index = {}

    def __call__(self, name):
        return self.index.setdefault(name, len(self.index))


def kernel(
    frames_hbm,
    masked_ref,
    counts_ref,
    gain_ref,
    wt_ref,
    up_ref,
    down_ref,
    target_ref,
    gup_ref,
    gdown_ref,
    frames_ref,
    wbuf,
    upbuf,
    downbuf,
    kv,
    normed_ref,
    normed_t,
    act_ref,
    slope_ref,
    dpre_ref,
    psend,
    precv,
    cot,
    stats,
    abuf,
    bbuf,
    g32,
    gs,
    rsb,
    fown,
    foth,
    local_sem,
    send_sem,
    recv_sem,
):
    t = lax.axis_index("tm")
    x = lax.axis_index("dp")
    z = lax.axis_index("head")
    y, c = t // 2, t % 2
    other = 1 - c
    partner = {"tm": y * 2 + other}

    def at_x(step):
        return lax.rem(x + step + NX, NX)

    def at_y(step):
        return lax.rem(y + step + NY, NY)

    def at_z(step):
        return lax.rem(z + step + NZ, NZ)

    fetch = pltpu.make_async_copy(frames_hbm, frames_ref, local_sem.at[4])
    fetch.start()

    barrier = pltpu.get_barrier_semaphore()
    peers = [partner]
    for step in range(1, NY):
        for core in range(2):
            peers.append({"tm": at_y(step) * 2 + core})
    for step in range(1, NX):
        for core in range(2):
            peers.append({"dp": at_x(step), "tm": y * 2 + core})
    for step in range(1, NZ):
        peers.append({"head": at_z(step)})
    for peer in peers:
        pl.semaphore_signal(barrier, inc=1, device_id=peer, device_id_type=MESH)
    pl.semaphore_wait(barrier, len(peers))

    names = Names()
    sent = []

    def describe(src, dst, device, name, out):
        return pltpu.make_async_remote_copy(
            src_ref=src,
            dst_ref=dst,
            send_sem=send_sem.at[out],
            recv_sem=recv_sem.at[name],
            device_id=device,
            device_id_type=MESH,
        )

    def send(src, dst, device, name):
        copy = describe(src, dst, device, names(name), len(sent))
        copy.start()
        sent.append(copy)

    done = [0]

    def drain():
        for copy in sent[done[0] :]:
            if isinstance(copy, tuple):
                started, copy = copy

                @pl.when(started)
                def _():
                    copy.wait_send()
            else:
                copy.wait_send()
        done[0] = len(sent)

    def wait(dst, name):
        describe(dst, dst, partner, names(name), 0).wait_recv()

    def place_w(shard, row, rows):
        return wbuf.at[shard, pl.ds(row, rows), :]

    def place_up(shard, row, rows):
        return upbuf.at[pl.ds(shard * SHARD + row, rows), :]

    def place_down(shard, row, rows):
        return downbuf.at[pl.ds(shard * SHARD + row, rows), :]

    class Direct:
        def __init__(self, name, src, place, base, half, sem):
            self.name, self.src, self.place, self.half = name, src, place, half
            self.mine, self.theirs = base + c * half, base + other * half
            self.own = pltpu.make_async_copy(
                src.at[pl.ds(base, 2 * half), :], place(x, base, 2 * half), local_sem.at[sem]
            )

        def start(self):
            mine = self.src.at[pl.ds(self.mine, self.half), :]
            there = self.place(x, self.mine, self.half)
            for step in NEAR:
                send(mine, there, {"dp": at_x(step)}, f"{self.name}{step}")
            self.own.start()

        def share(self):
            for step in NEAR:
                block = self.place(at_x(-step), self.mine, self.half)
                wait(block, f"{self.name}{step}")
                send(block, block, partner, f"{self.name}P{step}")

        def finish(self):
            self.own.wait()
            for step in NEAR:
                wait(self.place(at_x(-step), self.theirs, self.half), f"{self.name}P{step}")

    class Relay:
        def __init__(self, name, src, place, half, first, sem):
            self.name, self.src, self.place = name, src, place
            self.half, self.first = half, first
            self.mine, self.theirs = c * half, other * half
            self.own = pltpu.make_async_copy(src, place(x, 0, 2 * half), local_sem.at[sem])

        def start(self):
            mine = self.src.at[pl.ds(self.mine, self.half), :]
            there = self.place(x, self.mine, self.half)
            send(mine, there, {"dp": at_x(1)}, self.name + "R0")
            send(mine, there, {"dp": at_x(-1)}, self.name + "L0")
            self.own.start()

        def relay(self):
            n, first = self.half, self.first
            block = self.place(at_x(-1), self.mine, n)
            wait(block, self.name + "R0")
            part = self.place(at_x(-1), self.mine, first)
            send(part, part, {"dp": at_x(1)}, self.name + "R1")
            send(block, block, partner, self.name + "P0")
            block = self.place(at_x(1), self.mine, n)
            wait(block, self.name + "L0")
            part = self.place(at_x(1), self.mine + first, n - first)
            send(part, part, {"dp": at_x(-1)}, self.name + "L1")
            send(block, block, partner, self.name + "P1")

        def share(self):
            n, first = self.half, self.first
            far = at_x(2)
            part = self.place(far, self.mine, first)
            wait(part, self.name + "R1")
            send(part, part, partner, self.name + "P2")
            part = self.place(far, self.mine + first, n - first)
            wait(part, self.name + "L1")
            send(part, part, partner, self.name + "P3")

        def near(self):
            n = self.half
            self.own.wait()
            wait(self.place(at_x(-1), self.theirs, n), self.name + "P0")
            wait(self.place(at_x(1), self.theirs, n), self.name + "P1")

        def far(self):
            n, first = self.half, self.first
            wait(self.place(at_x(2), self.theirs, first), self.name + "P2")
            wait(self.place(at_x(2), self.theirs + first, n - first), self.name + "P3")

    teacher_kv = Direct("w", wt_ref, place_w, CHANNELS, CHANNELS, 0)
    teacher_q = Direct("q", wt_ref, place_w, 0, HEAD, 3)
    upward = Relay("u", up_ref, place_up, 160, 80, 1)
    downward = Relay("d", down_ref, place_down, 160, 80, 2)

    teacher_kv.start()

    keep = 1 - masked_ref[...]
    keep = keep.astype(F32)
    before = lax.broadcasted_iota(jnp.int32, (FRAMES, FRAMES), 0)
    after = lax.broadcasted_iota(jnp.int32, (FRAMES, FRAMES), 1)
    upper = jnp.where(before <= after, 1.0, 0.0).astype(BF16)
    rank = dot(jnp.broadcast_to(keep, (16, FRAMES)).astype(BF16), upper, ((1,), (0,)))[0:1]
    slot = lax.broadcasted_iota(jnp.int32, (SLOTS, FRAMES), 0).astype(F32)
    pick = jnp.where(rank - 1.0 == slot, jnp.broadcast_to(keep, (SLOTS, FRAMES)), 0.0).astype(BF16)
    fetch.wait()
    chosen = dot(pick, frames_ref[...], ((1,), (0,)))
    centre = jnp.mean(chosen, axis=1, keepdims=True)
    chosen = chosen - centre
    spread = jnp.mean(chosen * chosen, axis=1, keepdims=True)
    normed = chosen * lax.rsqrt(spread + 1e-5) * gain_ref[...].reshape(1, D)
    normed_ref[...] = normed.astype(BF16)
    normed_t[...] = normed.T.astype(BF16)

    def project(low, high):
        out = jnp.zeros((high - low, FRAMES), F32)
        for shard in range(NX):
            out = out + dot(
                wbuf[shard, low:high, :], frames_ref[:, shard * SHARD : (shard + 1) * SHARD], ((1,), (1,))
            )
        return out.astype(BF16)

    def block(source, core, part):
        return kv.at[source, core, pl.ds(part * CHANNELS, CHANNELS), :]

    teacher_kv.share()
    teacher_q.start()
    teacher_kv.finish()
    kv[y, c] = project(CHANNELS, 3 * CHANNELS)
    right, left = {"tm": at_y(1) * 2 + c}, {"tm": at_y(-1) * 2 + c}
    for part, tag in ((0, "k"), (1, "v")):
        mine = block(y, c, part)
        send(mine, mine, right, tag + "R0")
        send(mine, mine, left, tag + "L0")
        send(mine, mine, partner, tag + "P0")
    upward.start()
    teacher_q.share()
    teacher_q.finish()
    downward.start()
    query = project(0, CHANNELS)
    query = [query[h * HEAD : (h + 1) * HEAD] for h in range(2)]

    best = [jnp.full((1, FRAMES), -jnp.inf, F32) for _ in range(2)]
    accum = [jnp.zeros((HEAD + 16, FRAMES), F32) for _ in range(2)]

    def attend(blocks):
        for h in range(2):
            keys = jnp.concatenate(
                [kv[s, core, h * HEAD : (h + 1) * HEAD, :] for s, core in blocks], axis=1
            )
            low = CHANNELS + h * HEAD
            values = jnp.concatenate(
                [kv[s, core, low : low + HEAD, :] for s, core in blocks], axis=1
            )
            values = jnp.concatenate([values, jnp.ones((16, values.shape[1]), BF16)], axis=0)
            scores = dot(keys, query[h], ((0,), (0,)))
            top = jnp.maximum(best[h], jnp.max(scores, axis=0, keepdims=True))
            fade = jnp.exp((best[h] - top) * SCALE)
            weights = jnp.exp((scores - top) * SCALE).astype(BF16)
            accum[h] = accum[h] * fade + dot(values, weights, ((1,), (0,)))
            best[h] = top

    def forward(step):
        behind, ahead = at_y(-step), at_y(step)
        for part, tag in ((0, "k"), (1, "v")):
            if step < 4 or part == 0:
                here = block(behind, c, part)
                wait(here, f"{tag}R{step - 1}")
                if step < 3 or (step == 3 and part == 0):
                    send(here, here, right, f"{tag}R{step}")
                send(here, here, partner, f"{tag}PR{step}")
            if step < 4 or part == 1:
                here = block(ahead, c, part)
                wait(here, f"{tag}L{step - 1}")
                if step < 3 or (step == 3 and part == 1):
                    send(here, here, left, f"{tag}L{step}")
                send(here, here, partner, f"{tag}PL{step}")

    def shared(step):
        for part, tag in ((0, "k"), (1, "v")):
            if step == 0:
                wait(block(y, other, part), tag + "P0")
                continue
            if step < 4 or part == 0:
                wait(block(at_y(-step), other, part), f"{tag}PR{step}")
            if step < 4 or part == 1:
                wait(block(at_y(step), other, part), f"{tag}PL{step}")

    me = x * 2 + c

    def operand(tag, role, source, place):
        for step in NEAR:
            sem = names(f"{tag}{step}0")
            names(f"{tag}{step}1")
            copy = describe(
                source(at_x(step)), place(me), {"dp": at_x(step), "tm": y * 2 + role}, sem + c, len(sent)
            )
            copy.start()
            sent.append(copy)
        sem = names(f"{tag}00")
        names(f"{tag}01")
        copy = describe(source(x), place(me), partner, sem + c, len(sent))

        @pl.when(c == role)
        def _():
            place(me)[...] = source(x)[...]

        @pl.when(c != role)
        def _():
            copy.start()

        sent.append((c != role, copy))

    def operand_here(tag, place):
        here = place(x * 2 + other)
        describe(here, here, partner, names(f"{tag}00") + other, 0).wait_recv()
        for step in NEAR:
            for core in range(2):
                here = place(at_x(-step) * 2 + core)
                describe(here, here, partner, names(f"{tag}{step}{core}"), 0).wait_recv()

    def whole_a(source):
        return abuf.at[source]

    def whole_b(source):
        return bbuf.at[source]

    attend([(y, c)])
    shared(0)
    attend([(y, other)])
    forward(1)
    attend([(at_y(-1), c), (at_y(1), c)])
    shared(1)
    attend([(at_y(-1), other), (at_y(1), other)])
    upward.relay()
    forward(2)
    attend([(at_y(-2), c), (at_y(2), c)])
    shared(2)
    attend([(at_y(-2), other), (at_y(2), other)])
    downward.relay()
    forward(3)
    upward.share()
    attend([(at_y(-3), c), (at_y(3), c)])

    upward.near()
    upward.far()
    pre = dot(normed_ref[...], upbuf[...], ((1,), (0,)))
    cumulative = 0.5 * (1.0 + lax.erf(pre * math.sqrt(0.5)))
    act_ref[...] = (pre * cumulative).astype(BF16)
    slope_ref[...] = cumulative + pre * (jnp.exp(-0.5 * pre * pre) * (1.0 / math.sqrt(2 * math.pi)))

    operand("act", 0, lambda to: act_ref, whole_b)
    shared(3)
    attend([(at_y(-3), other), (at_y(3), other)])
    forward(4)
    attend([(at_y(4), c)])

    def predict(shard, step):
        rows = pl.ds(shard * SHARD, SHARD)
        psend[rows, :] = dot(downbuf[rows, :], act_ref[...], ((1,), (1,))).astype(BF16)
        for half in range(2):
            to = shard * 2 + half
            copy = describe(
                psend.at[pl.ds(to * CHANNELS, CHANNELS), :],
                precv.at[z],
                {"head": to},
                names("p0") + lax.rem(to - z + NZ, NZ),
                len(sent),
            )

            @pl.when(to != z)
            def _():
                copy.start()

            sent.append((to != z, copy))

    for step in range(NZ):
        names(f"p{step}")
    downward.share()
    downward.near()
    for step in (0, 1, 3):
        predict(at_x(step), step)
    shared(4)
    attend([(at_y(4), other)])

    context = [accum[h][:HEAD] / accum[h][HEAD : HEAD + 1] for h in range(2)]
    lane = lax.broadcasted_iota(jnp.int32, (HEAD, 128), 1)
    columns = jnp.zeros((HEAD, 128), F32)
    for h in range(2):
        first = jnp.sum(context[h], axis=1, keepdims=True)
        second = jnp.sum(context[h] * context[h], axis=1, keepdims=True)
        columns = jnp.where(lane == h, first, jnp.where(lane == 2 + h, second, columns))
    columns = jnp.concatenate([columns, jnp.zeros((128 - HEAD, 128), F32)], axis=0)
    stats[0] = columns.T[0:8]
    for step in range(1, NT):
        send(stats.at[0], stats.at[step], {"tm": lax.rem(t + step, NT)}, f"s{step}")
    downward.far()
    predict(at_x(2), 2)
    operand("nrm", 1, lambda to: normed_t.at[pl.ds(to * SHARD, SHARD), :], whole_a)
    drain()


    total = stats[0]
    for step in range(1, NT):
        wait(stats.at[step], f"s{step}")
        total = total + stats[step]
    columns = jnp.concatenate([total, jnp.zeros((120, 128), F32)], axis=0).T
    parts = []
    for h in range(2):
        mean = columns[:HEAD, h : h + 1] * (1.0 / LENGTH)
        var = columns[:HEAD, 2 + h : 3 + h] * (1.0 / LENGTH) - mean * mean
        parts.append((context[h] - mean) * lax.rsqrt(var + 1e-5))
    target = jnp.concatenate(parts, axis=0).astype(BF16)
    target_ref[...] = target

    aim = dot(target, pick, ((1,), (1,)))
    pred = psend[pl.ds(z * CHANNELS, CHANNELS), :].astype(F32)
    for step in range(1, NZ):
        wait(precv.at[at_z(-step)], f"p{step}")
        pred = pred + precv[at_z(-step)].astype(F32)
    number = lax.broadcasted_iota(jnp.int32, (CHANNELS, SLOTS), 1)
    valid = number < jnp.broadcast_to(counts_ref[...], (CHANNELS, SLOTS))
    gap = jnp.where(valid, pred - aim, 0.0) * (2.0 / math.sqrt(D))
    here = cot.at[pl.ds(z * CHANNELS, CHANNELS), :]
    here[...] = gap.astype(BF16)
    for step in (1, 7, 2, 6, 3, 5, 4):
        send(here, here, {"head": at_z(step)}, f"c{step}")

    for step in range(4 * NX):
        names(f"e{step}")

    def half_a(source, half):
        return abuf.at[source, pl.ds(half * CHANNELS, CHANNELS), :]

    def pass_on(owner):
        to, half = owner // 2, lax.rem(owner, 2)
        source = cot.at[pl.ds(owner * CHANNELS, CHANNELS), :]
        sem = names("e0") + lax.rem(to - x + NX, NX) * 4 + c * 2 + half
        copy = describe(source, half_a(me, half), {"dp": to, "tm": y * 2}, sem, len(sent))
        mine = jnp.logical_and(to == x, c == 0)
        away = jnp.logical_not(mine)

        @pl.when(mine)
        def _():
            half_a(me, half)[...] = source[...]

        @pl.when(away)
        def _():
            copy.start()

        sent.append((away, copy))

    def back_from(owner):
        rows = pl.ds(owner * CHANNELS, CHANNELS)
        return dot(cot[rows, :], downbuf[rows, :], ((0,), (0,)))

    pass_on(z)
    back = back_from(z)
    drain()
    for step in (1, 7, 2, 6, 3, 5, 4):
        owner = at_z(-step)
        wait(cot.at[pl.ds(owner * CHANNELS, CHANNELS), :], f"c{step}")
        pass_on(owner)
        back = back + back_from(owner)
    dpre_ref[...] = (back * slope_ref[...]).astype(BF16)
    for number, (band, bands, _) in enumerate(CHUNKS):
        columns = pl.ds(band * 128, bands * 128)
        operand(
            f"m{number}",
            1,
            lambda to, columns=columns: dpre_ref.at[:, columns],
            lambda source, columns=columns: bbuf.at[source, :, columns],
        )
    drain()

    @pl.when(c == 0)
    def _():
        operand_here("act", whole_b)
        for step in (0, *NEAR):
            for core in range(2):
                for half in range(2):
                    here = half_a(at_x(-step) * 2 + core, half)
                    copy = describe(
                        here, here, partner, names("e0") + step * 4 + core * 2 + half, 0
                    )
                    if (step, core) != (0, 0):
                        copy.wait_recv()

    @pl.when(c != 0)
    def _():
        operand_here("nrm", whole_a)

    def eighth(number, which):
        band, _, rows = CHUNKS[number]
        return pl.ds(band * SHARD + which * rows, rows)

    def landing(number, slot):
        band, _, rows = CHUNKS[number]
        return rsb.at[slot, pl.ds(band * SHARD // NY, rows), :]

    def on_y(step):
        return {"tm": at_y(step) * 2 + c}

    even = lax.rem(y, 2) == 0
    side = 1 - 2 * lax.rem(y, 2)

    def reduce_first(number):
        band, bands, _ = CHUNKS[number]
        columns = pl.ds(band * 128, bands * 128)

        @pl.when(c != 0)
        def _():
            operand_here(f"m{number}", lambda source: bbuf.at[source, :, columns])

        grad = jnp.zeros((SHARD, bands * 128), F32)
        for pair in range(NX):
            rows = jnp.concatenate([abuf[2 * pair], abuf[2 * pair + 1]], axis=1)
            inner = jnp.concatenate([bbuf[2 * pair, :, columns], bbuf[2 * pair + 1, :, columns]], axis=0)
            grad = grad + dot(rows, inner, ((1,), (0,)))
        for at in range(bands):
            stripe = grad[:, at * 128 : (at + 1) * 128]
            low = (band + at) * SHARD
            g32[low : low + SHARD, :] = stripe
            gs[low : low + SHARD, :] = stripe.astype(BF16)
        for slot, step, piece in (
            (0, 1, at_y(3)),
            (1, -1, at_y(-3)),
            (2, 2 * side, at_y(4)),
            (3, 1, at_y(1)),
            (4, -1, at_y(-1)),
        ):
            send(gs.at[eighth(number, piece), :], landing(number, slot), on_y(step), f"r{number}{slot}")

    def reduce_second(number):
        for slot in range(3):
            wait(landing(number, slot), f"r{number}{slot}")
        far = landing(number, 2)[...].astype(F32)
        for slot, step, mine in ((5, 2, even), (6, -2, jnp.logical_not(even))):
            total = g32[eighth(number, at_y(step)), :] + landing(number, slot - 5)[...].astype(F32)
            total = total + jnp.where(mine, far, 0.0)
            out = landing(number, slot - 5 + 7)
            out[...] = total.astype(BF16)
            send(out, landing(number, slot), on_y(step), f"r{number}{slot}")

    def reduce_last(number):
        total = g32[eighth(number, y), :]
        for slot in (3, 4, 5, 6):
            wait(landing(number, slot), f"r{number}{slot}")
            total = total + landing(number, slot)[...].astype(F32)
        here = fown.at[eighth(number, y), :]
        here[...] = total.astype(BF16)
        for step in (2, -2, 1, -1):
            send(here, here, on_y(step), f"g{number}{step}")
        send(here, foth.at[eighth(number, y), :], partner, f"h{number}0")

    def gathered(number, step):
        rows = eighth(number, at_y(-step))
        wait(fown.at[rows, :], f"g{number}{step}")
        return rows

    def hand_over(number, step, rows):
        send(fown.at[rows, :], foth.at[rows, :], partner, f"h{number}{step}")

    def gather_first(number):
        for step in (2, -2):
            rows = gathered(number, step)
            near = 1 if step > 0 else -1
            send(fown.at[rows, :], fown.at[rows, :], on_y(near), f"g{number}{3 * near}")
            hand_over(number, step, rows)
        rows = eighth(number, at_y(-2 * side))
        send(fown.at[rows, :], fown.at[rows, :], on_y(2 * side), f"g{number}4")
        for step in (1, -1):
            hand_over(number, step, gathered(number, step))

    def gather_last(number):
        for step in (3, -3, 4):
            hand_over(number, step, gathered(number, step))

    rest = STACK - SHARD * HIDDEN // 128
    g32[STACK - rest :, :] = jnp.zeros((rest, 128), F32)
    gs[STACK - rest :, :] = jnp.zeros((rest, 128), BF16)
    reduce_first(0)
    reduce_first(1)
    reduce_second(0)
    reduce_first(2)
    reduce_second(1)
    reduce_last(0)
    reduce_second(2)
    reduce_last(1)
    gather_first(0)
    reduce_last(2)
    gather_first(1)
    gather_last(0)
    gather_first(2)
    gather_last(1)
    gather_last(2)
    drain()
    for number in range(len(CHUNKS)):
        for step in (0, 1, -1, 2, -2, 3, -3, 4):
            wait(foth.at[eighth(number, at_y(-step)), :], f"h{number}{step}")

    def unstack(source, out):
        for band in range(HIDDEN // 128):
            out[:, band * 128 : (band + 1) * 128] = source[band * SHARD : (band + 1) * SHARD, :]

    @pl.when(c == 0)
    def _():
        unstack(fown, gdown_ref)
        unstack(foth, gup_ref)

    @pl.when(c != 0)
    def _():
        unstack(fown, gup_ref)
        unstack(foth, gdown_ref)

    drain()


def widen(target_ref, gup_ref, gdown_ref, target_out, gup_out, gdown_out):
    target_out[...] = target_ref[...]
    gup_out[...] = gup_ref[...].astype(F32)
    gdown_out[...] = gdown_ref[...].astype(F32)


def local(frames, masked, kept_counts, teacher_qkv, student_gain, w_up, w_down):
    wt = teacher_qkv.transpose(1, 2, 0).reshape(3 * CHANNELS, SHARD)
    vmem = pl.BlockSpec(memory_space=pltpu.VMEM)
    hbm = pl.BlockSpec(memory_space=pl.ANY)
    target, gup, gdown = pl.pallas_call(
        kernel,
        out_shape=(
            jax.ShapeDtypeStruct((CHANNELS, FRAMES), BF16),
            jax.ShapeDtypeStruct((SHARD, HIDDEN), BF16),
            jax.ShapeDtypeStruct((SHARD, HIDDEN), BF16),
        ),
        in_specs=[hbm, vmem, vmem, vmem, hbm, hbm, hbm],
        out_specs=(vmem, vmem, vmem),
        scratch_shapes=[
            pltpu.VMEM((FRAMES, D), BF16),
            pltpu.VMEM((NX, 3 * CHANNELS, SHARD), BF16),
            pltpu.VMEM((D, HIDDEN), BF16),
            pltpu.VMEM((D, HIDDEN), BF16),
            pltpu.VMEM((NY, 2, 2 * CHANNELS, FRAMES), BF16),
            pltpu.VMEM((SLOTS, D), BF16),
            pltpu.VMEM((D, SLOTS), BF16),
            pltpu.VMEM((SLOTS, HIDDEN), BF16),
            pltpu.VMEM((SLOTS, HIDDEN), F32),
            pltpu.VMEM((SLOTS, HIDDEN), BF16),
            pltpu.VMEM((D, SLOTS), BF16),
            pltpu.VMEM((NZ, CHANNELS, SLOTS), BF16),
            pltpu.VMEM((D, SLOTS), BF16),
            pltpu.VMEM((NT, 8, 128), F32),
            pltpu.VMEM((2 * NX, SHARD, SLOTS), BF16),
            pltpu.VMEM((2 * NX, SLOTS, HIDDEN), BF16),
            pltpu.VMEM((STACK, 128), F32),
            pltpu.VMEM((STACK, 128), BF16),
            pltpu.VMEM((NY + 1, PIECE, 128), BF16),
            pltpu.VMEM((STACK, 128), BF16),
            pltpu.VMEM((STACK, 128), BF16),
            pltpu.SemaphoreType.DMA((5,)),
            pltpu.SemaphoreType.DMA((256,)),
            pltpu.SemaphoreType.DMA((256,)),
        ],
        compiler_params=pltpu.CompilerParams(
            collective_id=0, has_side_effects=True, vmem_limit_bytes=60 * 1024 * 1024
        ),
    )(
        frames[0],
        masked,
        kept_counts,
        student_gain,
        wt,
        w_up,
        w_down,
    )
    target, gup, gdown = pl.pallas_call(
        widen,
        out_shape=(
            jax.ShapeDtypeStruct((CHANNELS, FRAMES), BF16),
            jax.ShapeDtypeStruct((SHARD, HIDDEN), F32),
            jax.ShapeDtypeStruct((SHARD, HIDDEN), F32),
        ),
        in_specs=[vmem] * 3,
        out_specs=(vmem, vmem, vmem),
    )(target, gup, gdown)
    return target.T[None], gup, gdown


def solution(mesh):
    placed = (
        P("dp", "tm", None),
        P("dp", "tm"),
        P("dp", "tm"),
        P("dp", None, "head"),
        P(),
        P("dp", "head"),
        P("dp", "head"),
    )
    return jax.shard_map(
        local,
        mesh=mesh,
        in_specs=placed,
        out_specs=(P("dp", "tm", "head"), P("dp", "head"), P("dp", "head")),
        check_vma=False,
    )
```

```python
import math

import jax
import jax.numpy as jnp
from jax import lax
from jax.experimental import pallas as pl
from jax.experimental.pallas import tpu as pltpu
from jax.sharding import PartitionSpec as P

BF16 = jnp.bfloat16
F32 = jnp.float32
MESH = pl.DeviceIdType.MESH

D = 1280
HEAD = 80
FRAMES = 256
SLOTS = 128
CHANNELS = 160
HIDDEN = 640
SHARD = 320
NX, NY, NZ = 4, 8, 8
NT = 2 * NY
PIECE = 208
STACK = NY * PIECE
CHUNKS = ((0, 2, 80), (2, 3, 128))
NEAR = (1, 3, 2)
SENDS, RECEIVES = 13, 67
METER = 5120
LENGTH = NT * FRAMES
SCALE = HEAD**-0.5


def dot(a, b, dims):
    return lax.dot_general(a, b, (dims, ((), ())), preferred_element_type=F32)


class Names:
    def __init__(self):
        self.index = {}

    def __call__(self, name):
        return self.index.setdefault(name, len(self.index))


def kernel(
    frames_hbm,
    masked_ref,
    counts_ref,
    gain_ref,
    wt_ref,
    up_ref,
    down_ref,
    target_ref,
    gup_ref,
    gdown_ref,
    frames_ref,
    wbuf,
    upbuf,
    downbuf,
    kv,
    normed_ref,
    normed_t,
    act_ref,
    slope_ref,
    dpre_ref,
    psend,
    precv,
    cot,
    stats,
    abuf,
    bbuf,
    g32,
    gs,
    rsb,
    fown,
    foth,
    meter,
    local_sem,
    send_sem,
    recv_sem,
):
    t = lax.axis_index("tm")
    x = lax.axis_index("dp")
    z = lax.axis_index("head")
    y, c = t // 2, t % 2
    other = 1 - c
    partner = {"tm": y * 2 + other}

    def at_x(step):
        return lax.rem(x + step + NX, NX)

    def at_y(step):
        return lax.rem(y + step + NY, NY)

    def at_z(step):
        return lax.rem(z + step + NZ, NZ)

    fetch = pltpu.make_async_copy(frames_hbm, frames_ref, local_sem.at[4])
    fetch.start()

    barrier = pltpu.get_barrier_semaphore()
    peers = [partner]
    for step in range(1, NY):
        for core in range(2):
            peers.append({"tm": at_y(step) * 2 + core})
    for step in range(1, NX):
        for core in range(2):
            peers.append({"dp": at_x(step), "tm": y * 2 + core})
    for step in range(1, NZ):
        peers.append({"head": at_z(step)})
    for peer in peers:
        pl.semaphore_signal(barrier, inc=1, device_id=peer, device_id_type=MESH)
    pl.semaphore_wait(barrier, len(peers))

    names, outs = Names(), Names()
    left_here = {}

    def describe(src, dst, device, name, group):
        return pltpu.make_async_remote_copy(
            src_ref=src,
            dst_ref=dst,
            send_sem=send_sem.at[outs(group)],
            recv_sem=recv_sem.at[names(name)],
            device_id=device,
            device_id_type=MESH,
        )

    def send(src, dst, device, name, group):
        describe(src, dst, device, name, group).start()
        count(src, group)

    def count(src, group):
        left_here[group] = left_here.get(group, 0) + math.prod(src.shape) * src.dtype.itemsize // 256

    def wait(dst, name):
        describe(dst, dst, partner, name, "w").wait_recv()

    def pieces(rows):
        return meter.at[pl.ds(0, rows), :]

    def wait_left(group, refs=None):
        refs = pieces(left_here[group]) if refs is None else refs
        describe(refs, refs, partner, "w1", group).wait_send()

    def place_w(shard, row, rows):
        return wbuf.at[shard, pl.ds(row, rows), :]

    def place_up(shard, row, rows):
        return upbuf.at[pl.ds(shard * SHARD + row, rows), :]

    def place_down(shard, row, rows):
        return downbuf.at[pl.ds(shard * SHARD + row, rows), :]

    class Direct:
        def __init__(self, name, src, place, base, half, sem):
            self.name, self.src, self.place, self.half = name, src, place, half
            self.mine, self.theirs = base + c * half, base + other * half
            self.own = pltpu.make_async_copy(
                src.at[pl.ds(base, 2 * half), :], place(x, base, 2 * half), local_sem.at[sem]
            )

        def start(self):
            mine = self.src.at[pl.ds(self.mine, self.half), :]
            there = self.place(x, self.mine, self.half)
            for step in NEAR:
                send(mine, there, {"dp": at_x(step)}, f"{self.name}{step}", "w")
            self.own.start()

        def share(self):
            for step in NEAR:
                block = self.place(at_x(-step), self.mine, self.half)
                wait(block, f"{self.name}{step}")
                send(block, block, partner, f"{self.name}P", "w")

        def finish(self):
            self.own.wait()
            wait(wbuf.at[pl.ds(0, NX - 1), pl.ds(self.theirs, self.half), :], f"{self.name}P")

    class Relay:
        def __init__(self, name, src, place, half, first, sem):
            self.name, self.src, self.place = name, src, place
            self.half, self.first = half, first
            self.mine, self.theirs = c * half, other * half
            self.own = pltpu.make_async_copy(src, place(x, 0, 2 * half), local_sem.at[sem])

        def start(self):
            mine = self.src.at[pl.ds(self.mine, self.half), :]
            there = self.place(x, self.mine, self.half)
            send(mine, there, {"dp": at_x(1)}, self.name + "R0", self.name)
            send(mine, there, {"dp": at_x(-1)}, self.name + "L0", self.name)
            self.own.start()

        def relay(self):
            n, first = self.half, self.first
            block = self.place(at_x(-1), self.mine, n)
            wait(block, self.name + "R0")
            part = self.place(at_x(-1), self.mine, first)
            send(part, part, {"dp": at_x(1)}, self.name + "R1", self.name)
            send(block, block, partner, self.name + "P0", self.name)
            block = self.place(at_x(1), self.mine, n)
            wait(block, self.name + "L0")
            part = self.place(at_x(1), self.mine + first, n - first)
            send(part, part, {"dp": at_x(-1)}, self.name + "L1", self.name)
            send(block, block, partner, self.name + "P0", self.name)

        def share(self):
            n, first = self.half, self.first
            far = at_x(2)
            part = self.place(far, self.mine, first)
            wait(part, self.name + "R1")
            send(part, part, partner, self.name + "P2", self.name)
            part = self.place(far, self.mine + first, n - first)
            wait(part, self.name + "L1")
            send(part, part, partner, self.name + "P2", self.name)

        def near(self):
            self.own.wait()
            wait(self.place(0, 0, 2 * self.half), self.name + "P0")

        def far(self):
            wait(self.place(at_x(2), self.theirs, self.half), self.name + "P2")

    teacher_kv = Direct("w", wt_ref, place_w, CHANNELS, CHANNELS, 0)
    teacher_q = Direct("q", wt_ref, place_w, 0, HEAD, 3)
    upward = Relay("u", up_ref, place_up, 160, 80, 1)
    downward = Relay("d", down_ref, place_down, 160, 80, 2)

    teacher_kv.start()

    keep = 1 - masked_ref[...]
    keep = keep.astype(F32)
    before = lax.broadcasted_iota(jnp.int32, (FRAMES, FRAMES), 0)
    after = lax.broadcasted_iota(jnp.int32, (FRAMES, FRAMES), 1)
    upper = jnp.where(before <= after, 1.0, 0.0).astype(BF16)
    rank = dot(jnp.broadcast_to(keep, (16, FRAMES)).astype(BF16), upper, ((1,), (0,)))[0:1]
    slot = lax.broadcasted_iota(jnp.int32, (SLOTS, FRAMES), 0).astype(F32)
    pick = jnp.where(rank - 1.0 == slot, jnp.broadcast_to(keep, (SLOTS, FRAMES)), 0.0).astype(BF16)
    fetch.wait()
    chosen = dot(pick, frames_ref[...], ((1,), (0,)))
    centre = jnp.mean(chosen, axis=1, keepdims=True)
    chosen = chosen - centre
    spread = jnp.mean(chosen * chosen, axis=1, keepdims=True)
    normed = chosen * lax.rsqrt(spread + 1e-5) * gain_ref[...].reshape(1, D)
    normed_ref[...] = normed.astype(BF16)
    normed_t[...] = normed.T.astype(BF16)

    def project(low, high):
        out = jnp.zeros((high - low, FRAMES), F32)
        for shard in range(NX):
            out = out + dot(
                wbuf[shard, low:high, :], frames_ref[:, shard * SHARD : (shard + 1) * SHARD], ((1,), (1,))
            )
        return out.astype(BF16)

    def block(source, core, part):
        return kv.at[source, core, pl.ds(part * CHANNELS, CHANNELS), :]

    teacher_kv.share()
    teacher_q.start()
    teacher_kv.finish()
    kv[y, c] = project(CHANNELS, 3 * CHANNELS)
    right, left = {"tm": at_y(1) * 2 + c}, {"tm": at_y(-1) * 2 + c}
    for part, tag in ((0, "k"), (1, "v")):
        mine = block(y, c, part)
        send(mine, mine, right, tag + "R0", tag)
        send(mine, mine, left, tag + "L0", tag)
        send(mine, mine, partner, "s0", tag)
    upward.start()
    teacher_q.share()
    teacher_q.finish()
    downward.start()
    query = project(0, CHANNELS)
    query = [query[h * HEAD : (h + 1) * HEAD] for h in range(2)]

    best = [jnp.full((1, FRAMES), -jnp.inf, F32) for _ in range(2)]
    accum = [jnp.zeros((HEAD + 16, FRAMES), F32) for _ in range(2)]

    def attend(blocks):
        for h in range(2):
            keys = jnp.concatenate(
                [kv[s, core, h * HEAD : (h + 1) * HEAD, :] for s, core in blocks], axis=1
            )
            low = CHANNELS + h * HEAD
            values = jnp.concatenate(
                [kv[s, core, low : low + HEAD, :] for s, core in blocks], axis=1
            )
            values = jnp.concatenate([values, jnp.ones((16, values.shape[1]), BF16)], axis=0)
            scores = dot(keys, query[h], ((0,), (0,)))
            top = jnp.maximum(best[h], jnp.max(scores, axis=0, keepdims=True))
            fade = jnp.exp((best[h] - top) * SCALE)
            weights = jnp.exp((scores - top) * SCALE).astype(BF16)
            accum[h] = accum[h] * fade + dot(values, weights, ((1,), (0,)))
            best[h] = top

    def forward(step):
        behind, ahead = at_y(-step), at_y(step)
        for part, tag in ((0, "k"), (1, "v")):
            if step < 4 or part == 0:
                here = block(behind, c, part)
                wait(here, f"{tag}R{step - 1}")
                if step < 3 or (step == 3 and part == 0):
                    send(here, here, right, f"{tag}R{step}", tag)
                send(here, here, partner, f"s{step}", tag)
            if step < 4 or part == 1:
                here = block(ahead, c, part)
                wait(here, f"{tag}L{step - 1}")
                if step < 3 or (step == 3 and part == 1):
                    send(here, here, left, f"{tag}L{step}", tag)
                send(here, here, partner, f"s{step}", tag)

    def shared(step):
        wait(kv.at[y, other] if step in (0, 4) else kv.at[y], f"s{step}")

    me = x * 2 + c

    def operand(tag, role, source, place):
        for step in NEAR:
            send(source(at_x(step)), place(me), {"dp": at_x(step), "tm": y * 2 + role}, tag, "o" + tag[0])

        @pl.when(c == role)
        def _():
            place(me)[...] = source(x)[...]

        copy = describe(source(x), place(me), partner, tag, "partner")

        @pl.when(c != role)
        def _():
            copy.start()

        count(source(x), f"partner{1 - role}")

    def whole_a(source):
        return abuf.at[source]

    def whole_b(source):
        return bbuf.at[source]

    attend([(y, c)])
    shared(0)
    attend([(y, other)])
    forward(1)
    attend([(at_y(-1), c), (at_y(1), c)])
    shared(1)
    attend([(at_y(-1), other), (at_y(1), other)])
    upward.relay()
    forward(2)
    attend([(at_y(-2), c), (at_y(2), c)])
    shared(2)
    attend([(at_y(-2), other), (at_y(2), other)])
    downward.relay()
    forward(3)
    upward.share()
    attend([(at_y(-3), c), (at_y(3), c)])

    upward.near()
    upward.far()
    pre = dot(normed_ref[...], upbuf[...], ((1,), (0,)))
    cumulative = 0.5 * (1.0 + lax.erf(pre * math.sqrt(0.5)))
    act_ref[...] = (pre * cumulative).astype(BF16)
    slope_ref[...] = cumulative + pre * (jnp.exp(-0.5 * pre * pre) * (1.0 / math.sqrt(2 * math.pi)))

    operand("act", 0, lambda to: act_ref, whole_b)
    shared(3)
    attend([(at_y(-3), other), (at_y(3), other)])
    forward(4)
    attend([(at_y(4), c)])

    def predict(shard, step):
        rows = pl.ds(shard * SHARD, SHARD)
        psend[rows, :] = dot(downbuf[rows, :], act_ref[...], ((1,), (1,))).astype(BF16)
        for half in range(2):
            to = shard * 2 + half
            source = psend.at[pl.ds(to * CHANNELS, CHANNELS), :]
            copy = describe(source, precv.at[lax.rem(to - z + NZ, NZ)], {"head": to}, "p", "p")

            @pl.when(to != z)
            def _():
                copy.start()

    downward.share()
    downward.near()
    for step in (0, 1, 3):
        predict(at_x(step), step)
    shared(4)
    attend([(at_y(4), other)])

    context = [accum[h][:HEAD] / accum[h][HEAD : HEAD + 1] for h in range(2)]
    lane = lax.broadcasted_iota(jnp.int32, (HEAD, 128), 1)
    columns = jnp.zeros((HEAD, 128), F32)
    for h in range(2):
        first = jnp.sum(context[h], axis=1, keepdims=True)
        second = jnp.sum(context[h] * context[h], axis=1, keepdims=True)
        columns = jnp.where(lane == h, first, jnp.where(lane == 2 + h, second, columns))
    columns = jnp.concatenate([columns, jnp.zeros((128 - HEAD, 128), F32)], axis=0)
    stats[0] = columns.T[0:8]
    for step in range(1, NT):
        send(stats.at[0], stats.at[step], {"tm": lax.rem(t + step, NT)}, "stats", "z")
    downward.far()
    predict(at_x(2), 2)
    operand("nrm", 1, lambda to: normed_t.at[pl.ds(to * SHARD, SHARD), :], whole_a)


    wait(stats.at[pl.ds(1, NT - 1)], "stats")
    total = stats[0]
    for step in range(1, NT):
        total = total + stats[step]
    columns = jnp.concatenate([total, jnp.zeros((120, 128), F32)], axis=0).T
    parts = []
    for h in range(2):
        mean = columns[:HEAD, h : h + 1] * (1.0 / LENGTH)
        var = columns[:HEAD, 2 + h : 3 + h] * (1.0 / LENGTH) - mean * mean
        parts.append((context[h] - mean) * lax.rsqrt(var + 1e-5))
    target = jnp.concatenate(parts, axis=0).astype(BF16)
    target_ref[...] = target

    aim = dot(target, pick, ((1,), (1,)))
    wait(precv.at[pl.ds(1, NZ - 1)], "p")
    pred = psend[pl.ds(z * CHANNELS, CHANNELS), :].astype(F32)
    for step in range(1, NZ):
        pred = pred + precv[step].astype(F32)
    number = lax.broadcasted_iota(jnp.int32, (CHANNELS, SLOTS), 1)
    valid = number < jnp.broadcast_to(counts_ref[...], (CHANNELS, SLOTS))
    gap = jnp.where(valid, pred - aim, 0.0) * (2.0 / math.sqrt(D))
    here = cot.at[pl.ds(z * CHANNELS, CHANNELS), :]
    here[...] = gap.astype(BF16)
    for step in (1, 7, 2, 6, 3, 5, 4):
        send(here, here, {"head": at_z(step)}, f"c{step}", "z")

    def half_a(source, half):
        return abuf.at[source, pl.ds(half * CHANNELS, CHANNELS), :]

    def pass_on(owner):
        to, half = owner // 2, lax.rem(owner, 2)
        source = cot.at[pl.ds(owner * CHANNELS, CHANNELS), :]
        copy = describe(source, half_a(me, half), {"dp": to, "tm": y * 2}, "e", "e")
        mine = jnp.logical_and(to == x, c == 0)
        away = jnp.logical_not(mine)

        @pl.when(mine)
        def _():
            half_a(me, half)[...] = source[...]

        @pl.when(away)
        def _():
            copy.start()

    def back_from(owner):
        rows = pl.ds(owner * CHANNELS, CHANNELS)
        return dot(cot[rows, :], downbuf[rows, :], ((0,), (0,)))

    pass_on(z)
    back = back_from(z)
    for step in (1, 7, 2, 6, 3, 5, 4):
        owner = at_z(-step)
        wait(cot.at[pl.ds(owner * CHANNELS, CHANNELS), :], f"c{step}")
        pass_on(owner)
        back = back + back_from(owner)
    dpre_ref[...] = (back * slope_ref[...]).astype(BF16)
    for number, (band, bands, _) in enumerate(CHUNKS):
        columns = pl.ds(band * 128, bands * 128)
        operand(
            f"m{number}",
            1,
            lambda to, columns=columns: dpre_ref.at[:, columns],
            lambda source, columns=columns: bbuf.at[source, :, columns],
        )

    @pl.when(c == 0)
    def _():
        wait(bbuf.at[pl.ds(0, 2 * NX - 1)], "act")
        wait(abuf.at[pl.ds(0, 2 * NX - 1)], "e")

    @pl.when(c != 0)
    def _():
        wait(abuf.at[pl.ds(0, 2 * NX - 1)], "nrm")

    def eighth(number, which):
        band, _, rows = CHUNKS[number]
        return pl.ds(band * SHARD + which * rows, rows)

    def landing(number, slot):
        band, _, rows = CHUNKS[number]
        return rsb.at[slot, pl.ds(band * SHARD // NY, rows), :]

    def on_y(step):
        return {"tm": at_y(step) * 2 + c}

    even = lax.rem(y, 2) == 0
    side = 1 - 2 * lax.rem(y, 2)

    def reduce_first(number):
        band, bands, _ = CHUNKS[number]
        columns = pl.ds(band * 128, bands * 128)

        @pl.when(c != 0)
        def _():
            wait(bbuf.at[pl.ds(0, 2 * NX - 1), :, columns], f"m{number}")

        grad = jnp.zeros((SHARD, bands * 128), F32)
        for pair in range(NX):
            rows = jnp.concatenate([abuf[2 * pair], abuf[2 * pair + 1]], axis=1)
            inner = jnp.concatenate([bbuf[2 * pair, :, columns], bbuf[2 * pair + 1, :, columns]], axis=0)
            grad = grad + dot(rows, inner, ((1,), (0,)))
        for at in range(bands):
            stripe = grad[:, at * 128 : (at + 1) * 128]
            low = (band + at) * SHARD
            g32[low : low + SHARD, :] = stripe
            gs[low : low + SHARD, :] = stripe.astype(BF16)
        for slot, step, piece in (
            (0, 1, at_y(3)),
            (1, -1, at_y(-3)),
            (2, 2 * side, at_y(4)),
            (3, 1, at_y(1)),
            (4, -1, at_y(-1)),
        ):
            send(
                gs.at[eighth(number, piece), :],
                landing(number, slot),
                on_y(step),
                f"r{number}{slot // 3}",
                "y",
            )

    def reduce_second(number):
        wait(landing(number, pl.ds(0, 3)), f"r{number}0")
        far = landing(number, 2)[...].astype(F32)
        for slot, step, mine in ((5, 2, even), (6, -2, jnp.logical_not(even))):
            total = g32[eighth(number, at_y(step)), :] + landing(number, slot - 5)[...].astype(F32)
            total = total + jnp.where(mine, far, 0.0)
            out = landing(number, slot - 5 + 7)
            out[...] = total.astype(BF16)
            send(out, landing(number, slot), on_y(step), f"r{number}1", "y")

    def reduce_last(number):
        total = g32[eighth(number, y), :]
        wait(landing(number, pl.ds(3, 4)), f"r{number}1")
        for slot in (3, 4, 5, 6):
            total = total + landing(number, slot)[...].astype(F32)
        here = fown.at[eighth(number, y), :]
        here[...] = total.astype(BF16)
        for step, tag in ((2, "a"), (-2, "b"), (1, "c"), (-1, "c")):
            send(here, here, on_y(step), f"g{number}{tag}", "y")
        hand_over(number, eighth(number, y))

    def hand_over(number, rows):
        send(fown.at[rows, :], foth.at[rows, :], partner, f"h{number}", "y")

    def gather_first(number):
        size = CHUNKS[number][2]
        for step, tag in ((2, "a"), (-2, "b")):
            rows = eighth(number, at_y(-step))
            wait(fown.at[rows, :], f"g{number}{tag}")
            send(fown.at[rows, :], fown.at[rows, :], on_y(step // 2), f"g{number}d", "y")
            hand_over(number, rows)
        rows = eighth(number, at_y(-2 * side))
        send(fown.at[rows, :], fown.at[rows, :], on_y(2 * side), f"g{number}d", "y")
        wait(pieces(2 * size), f"g{number}c")
        for step in (1, -1):
            hand_over(number, eighth(number, at_y(-step)))

    def gather_last(number):
        wait(pieces(3 * CHUNKS[number][2]), f"g{number}d")
        for step in (3, -3, 4):
            hand_over(number, eighth(number, at_y(-step)))

    rest = STACK - SHARD * HIDDEN // 128
    g32[STACK - rest :, :] = jnp.zeros((rest, 128), F32)
    gs[STACK - rest :, :] = jnp.zeros((rest, 128), BF16)
    reduce_first(0)
    reduce_first(1)
    reduce_second(0)
    reduce_second(1)
    reduce_last(0)
    reduce_last(1)
    gather_first(0)
    gather_first(1)
    gather_last(0)
    gather_last(1)
    for number, (band, _, rows) in enumerate(CHUNKS):
        wait(foth.at[pl.ds(band * SHARD, NY * rows), :], f"h{number}")

    def unstack(source, out):
        for band in range(HIDDEN // 128):
            out[:, band * 128 : (band + 1) * 128] = source[band * SHARD : (band + 1) * SHARD, :]

    @pl.when(c == 0)
    def _():
        unstack(fown, gdown_ref)
        unstack(foth, gup_ref)

    @pl.when(c != 0)
    def _():
        unstack(fown, gup_ref)
        unstack(foth, gdown_ref)

    wait_left("w", wbuf.at[pl.ds(0, NX - 1)])
    wait_left("p", pieces((NZ - 1) * CHANNELS))
    for group in ("u", "d", "k", "v", "z", "y", "oa", "on", "om"):
        wait_left(group)

    @pl.when(c == 0)
    def _():
        wait_left("partner", pieces(left_here["partner0"]))
        wait_left("e", pieces((NZ - 2) * CHANNELS))

    @pl.when(c != 0)
    def _():
        wait_left("partner", pieces(left_here["partner1"]))
        wait_left("e", pieces(NZ * CHANNELS))

    assert len(names.index) <= RECEIVES and len(outs.index) <= SENDS


def widen(target_ref, gup_ref, gdown_ref, target_out, gup_out, gdown_out):
    target_out[...] = target_ref[...]
    gup_out[...] = gup_ref[...].astype(F32)
    gdown_out[...] = gdown_ref[...].astype(F32)


def local(frames, masked, kept_counts, teacher_qkv, student_gain, w_up, w_down):
    wt = teacher_qkv.transpose(1, 2, 0).reshape(3 * CHANNELS, SHARD)
    vmem = pl.BlockSpec(memory_space=pltpu.VMEM)
    hbm = pl.BlockSpec(memory_space=pltpu.HBM)
    target, gup, gdown = pl.pallas_call(
        kernel,
        out_shape=(
            jax.ShapeDtypeStruct((CHANNELS, FRAMES), BF16),
            jax.ShapeDtypeStruct((SHARD, HIDDEN), BF16),
            jax.ShapeDtypeStruct((SHARD, HIDDEN), BF16),
        ),
        in_specs=[hbm, vmem, vmem, vmem, hbm, hbm, hbm],
        out_specs=(vmem, vmem, vmem),
        scratch_shapes=[
            pltpu.VMEM((FRAMES, D), BF16),
            pltpu.VMEM((NX, 3 * CHANNELS, SHARD), BF16),
            pltpu.VMEM((D, HIDDEN), BF16),
            pltpu.VMEM((D, HIDDEN), BF16),
            pltpu.VMEM((NY, 2, 2 * CHANNELS, FRAMES), BF16),
            pltpu.VMEM((SLOTS, D), BF16),
            pltpu.VMEM((D, SLOTS), BF16),
            pltpu.VMEM((SLOTS, HIDDEN), BF16),
            pltpu.VMEM((SLOTS, HIDDEN), F32),
            pltpu.VMEM((SLOTS, HIDDEN), BF16),
            pltpu.VMEM((D, SLOTS), BF16),
            pltpu.VMEM((NZ, CHANNELS, SLOTS), BF16),
            pltpu.VMEM((D, SLOTS), BF16),
            pltpu.VMEM((NT, 8, 128), F32),
            pltpu.VMEM((2 * NX, SHARD, SLOTS), BF16),
            pltpu.VMEM((2 * NX, SLOTS, HIDDEN), BF16),
            pltpu.VMEM((STACK, 128), F32),
            pltpu.VMEM((STACK, 128), BF16),
            pltpu.VMEM((NY + 1, PIECE, 128), BF16),
            pltpu.VMEM((STACK, 128), BF16),
            pltpu.VMEM((STACK, 128), BF16),
            pltpu.VMEM((METER, 128), BF16),
            pltpu.SemaphoreType.DMA((5,)),
            pltpu.SemaphoreType.DMA((SENDS,)),
            pltpu.SemaphoreType.DMA((RECEIVES,)),
        ],
        compiler_params=pltpu.CompilerParams(
            collective_id=0, has_side_effects=True, vmem_limit_bytes=32 * 1024 * 1024
        ),
    )(
        frames[0],
        masked,
        kept_counts,
        student_gain,
        wt,
        w_up,
        w_down,
    )
    target, gup, gdown = pl.pallas_call(
        widen,
        out_shape=(
            jax.ShapeDtypeStruct((CHANNELS, FRAMES), BF16),
            jax.ShapeDtypeStruct((SHARD, HIDDEN), F32),
            jax.ShapeDtypeStruct((SHARD, HIDDEN), F32),
        ),
        in_specs=[vmem] * 3,
        out_specs=(vmem, vmem, vmem),
    )(target, gup, gdown)
    return target.T[None], gup, gdown


def solution(mesh):
    placed = (
        P("dp", "tm", None),
        P("dp", "tm"),
        P("dp", "tm"),
        P("dp", None, "head"),
        P(),
        P("dp", "head"),
        P("dp", "head"),
    )
    return jax.shard_map(
        local,
        mesh=mesh,
        in_specs=placed,
        out_specs=(P("dp", "tm", "head"), P("dp", "head"), P("dp", "head")),
        check_vma=False,
    )
```

```python
import math

import jax
import jax.numpy as jnp
from jax import lax
from jax.experimental import pallas as pl
from jax.experimental.pallas import tpu as pltpu
from jax.sharding import PartitionSpec as P

BF16 = jnp.bfloat16
F32 = jnp.float32
MESH = pl.DeviceIdType.MESH

D = 1280
HEAD = 80
FRAMES = 256
SLOTS = 128
CHANNELS = 160
HIDDEN = 640
SHARD = 320
NX, NY, NZ = 4, 8, 8
NT = 2 * NY
PIECE = 208
STACK = NY * PIECE
CHUNKS = ((0, 2, 80), (2, 3, 128))
NEAR = (1, 3, 2)
SENDS, RECEIVES = 13, 67
METER = 5120
LENGTH = NT * FRAMES
SCALE = HEAD**-0.5


def dot(a, b, dims):
    return lax.dot_general(a, b, (dims, ((), ())), preferred_element_type=F32)


class Names:
    def __init__(self):
        self.index = {}

    def __call__(self, name):
        return self.index.setdefault(name, len(self.index))


def kernel(
    frames_hbm,
    masked_ref,
    counts_ref,
    gain_ref,
    wt_ref,
    up_ref,
    down_ref,
    target_ref,
    gup_ref,
    gdown_ref,
    frames_ref,
    wbuf,
    upbuf,
    downbuf,
    kv,
    normed_ref,
    normed_t,
    act_ref,
    slope_ref,
    dpre_ref,
    psend,
    precv,
    cot,
    stats,
    abuf,
    bbuf,
    g32,
    gs,
    rsb,
    fown,
    foth,
    meter,
    local_sem,
    send_sem,
    recv_sem,
):
    t = lax.axis_index("tm")
    x = lax.axis_index("dp")
    z = lax.axis_index("head")
    y, c = t // 2, t % 2
    other = 1 - c
    partner = {"tm": y * 2 + other}

    def at_x(step):
        return lax.rem(x + step + NX, NX)

    def at_y(step):
        return lax.rem(y + step + NY, NY)

    def at_z(step):
        return lax.rem(z + step + NZ, NZ)

    fetch = pltpu.make_async_copy(frames_hbm, frames_ref, local_sem.at[4])
    fetch.start()

    barrier = pltpu.get_barrier_semaphore()
    peers = [partner]
    for step in range(1, NY):
        for core in range(2):
            peers.append({"tm": at_y(step) * 2 + core})
    for step in range(1, NX):
        for core in range(2):
            peers.append({"dp": at_x(step), "tm": y * 2 + core})
    for step in range(1, NZ):
        peers.append({"head": at_z(step)})
    for peer in peers:
        pl.semaphore_signal(barrier, inc=1, device_id=peer, device_id_type=MESH)
    pl.semaphore_wait(barrier, len(peers))

    names, outs = Names(), Names()
    left_here = {}

    def describe(src, dst, device, name, group):
        return pltpu.make_async_remote_copy(
            src_ref=src,
            dst_ref=dst,
            send_sem=send_sem.at[outs(group)],
            recv_sem=recv_sem.at[names(name)],
            device_id=device,
            device_id_type=MESH,
        )

    def send(src, dst, device, name, group):
        describe(src, dst, device, name, group).start()
        count(src, group)

    def count(src, group):
        left_here[group] = left_here.get(group, 0) + math.prod(src.shape) * src.dtype.itemsize // 256

    def wait(dst, name):
        describe(dst, dst, partner, name, "w").wait_recv()

    def pieces(rows):
        return meter.at[pl.ds(0, rows), :]

    def wait_left(group, refs=None):
        refs = pieces(left_here[group]) if refs is None else refs
        describe(refs, refs, partner, "w1", group).wait_send()

    def place_w(shard, row, rows):
        return wbuf.at[shard, pl.ds(row, rows), :]

    def place_up(shard, row, rows):
        return upbuf.at[pl.ds(shard * SHARD + row, rows), :]

    def place_down(shard, row, rows):
        return downbuf.at[pl.ds(shard * SHARD + row, rows), :]

    class Direct:
        def __init__(self, name, src, place, base, half, sem):
            self.name, self.src, self.place, self.half = name, src, place, half
            self.mine, self.theirs = base + c * half, base + other * half
            self.own = pltpu.make_async_copy(
                src.at[pl.ds(base, 2 * half), :], place(x, base, 2 * half), local_sem.at[sem]
            )

        def start(self):
            mine = self.src.at[pl.ds(self.mine, self.half), :]
            there = self.place(x, self.mine, self.half)
            for step in NEAR:
                send(mine, there, {"dp": at_x(step)}, f"{self.name}{step}", "w")
            self.own.start()

        def share(self):
            for step in NEAR:
                block = self.place(at_x(-step), self.mine, self.half)
                wait(block, f"{self.name}{step}")
                send(block, block, partner, f"{self.name}P", "w")

        def finish(self):
            self.own.wait()
            wait(wbuf.at[pl.ds(0, NX - 1), pl.ds(self.theirs, self.half), :], f"{self.name}P")

    class Relay:
        def __init__(self, name, src, place, half, first, sem):
            self.name, self.src, self.place = name, src, place
            self.half, self.first = half, first
            self.mine, self.theirs = c * half, other * half
            self.own = pltpu.make_async_copy(src, place(x, 0, 2 * half), local_sem.at[sem])

        def start(self):
            mine = self.src.at[pl.ds(self.mine, self.half), :]
            there = self.place(x, self.mine, self.half)
            send(mine, there, {"dp": at_x(1)}, self.name + "R0", self.name)
            send(mine, there, {"dp": at_x(-1)}, self.name + "L0", self.name)
            self.own.start()

        def relay(self):
            n, first = self.half, self.first
            block = self.place(at_x(-1), self.mine, n)
            wait(block, self.name + "R0")
            part = self.place(at_x(-1), self.mine, first)
            send(part, part, {"dp": at_x(1)}, self.name + "R1", self.name)
            send(block, block, partner, self.name + "P0", self.name)
            block = self.place(at_x(1), self.mine, n)
            wait(block, self.name + "L0")
            part = self.place(at_x(1), self.mine + first, n - first)
            send(part, part, {"dp": at_x(-1)}, self.name + "L1", self.name)
            send(block, block, partner, self.name + "P0", self.name)

        def share(self):
            n, first = self.half, self.first
            far = at_x(2)
            part = self.place(far, self.mine, first)
            wait(part, self.name + "R1")
            send(part, part, partner, self.name + "P2", self.name)
            part = self.place(far, self.mine + first, n - first)
            wait(part, self.name + "L1")
            send(part, part, partner, self.name + "P2", self.name)

        def near(self):
            self.own.wait()
            wait(self.place(0, 0, 2 * self.half), self.name + "P0")

        def far(self):
            wait(self.place(at_x(2), self.theirs, self.half), self.name + "P2")

    teacher_kv = Direct("w", wt_ref, place_w, CHANNELS, CHANNELS, 0)
    teacher_q = Direct("q", wt_ref, place_w, 0, HEAD, 3)
    upward = Relay("u", up_ref, place_up, 160, 80, 1)
    downward = Relay("d", down_ref, place_down, 160, 80, 2)

    teacher_kv.start()
    teacher_q.start()

    keep = 1 - masked_ref[...]
    keep = keep.astype(F32)
    before = lax.broadcasted_iota(jnp.int32, (FRAMES, FRAMES), 0)
    after = lax.broadcasted_iota(jnp.int32, (FRAMES, FRAMES), 1)
    upper = jnp.where(before <= after, 1.0, 0.0).astype(BF16)
    rank = dot(jnp.broadcast_to(keep, (16, FRAMES)).astype(BF16), upper, ((1,), (0,)))[0:1]
    slot = lax.broadcasted_iota(jnp.int32, (SLOTS, FRAMES), 0).astype(F32)
    pick = jnp.where(rank - 1.0 == slot, jnp.broadcast_to(keep, (SLOTS, FRAMES)), 0.0).astype(BF16)
    fetch.wait()
    chosen = dot(pick, frames_ref[...], ((1,), (0,)))
    centre = jnp.mean(chosen, axis=1, keepdims=True)
    chosen = chosen - centre
    spread = jnp.mean(chosen * chosen, axis=1, keepdims=True)
    normed = chosen * lax.rsqrt(spread + 1e-5) * gain_ref[...].reshape(1, D)
    normed_ref[...] = normed.astype(BF16)
    normed_t[...] = normed.T.astype(BF16)

    def project(low, high):
        out = jnp.zeros((high - low, FRAMES), F32)
        for shard in range(NX):
            out = out + dot(
                wbuf[shard, low:high, :], frames_ref[:, shard * SHARD : (shard + 1) * SHARD], ((1,), (1,))
            )
        return out.astype(BF16)

    def block(source, core, part):
        return kv.at[source, core, pl.ds(part * CHANNELS, CHANNELS), :]

    teacher_kv.share()
    upward.start()
    downward.start()
    teacher_kv.finish()
    kv[y, c] = project(CHANNELS, 3 * CHANNELS)
    right, left = {"tm": at_y(1) * 2 + c}, {"tm": at_y(-1) * 2 + c}
    for part, tag in ((0, "k"), (1, "v")):
        mine = block(y, c, part)
        send(mine, mine, right, tag + "R0", tag)
        send(mine, mine, left, tag + "L0", tag)
        send(mine, mine, partner, "s0", tag)
    teacher_q.share()
    teacher_q.finish()
    query = project(0, CHANNELS)
    query = [query[h * HEAD : (h + 1) * HEAD] for h in range(2)]

    best = [jnp.full((1, FRAMES), -jnp.inf, F32) for _ in range(2)]
    accum = [jnp.zeros((HEAD + 16, FRAMES), F32) for _ in range(2)]

    def attend(blocks):
        for h in range(2):
            keys = jnp.concatenate(
                [kv[s, core, h * HEAD : (h + 1) * HEAD, :] for s, core in blocks], axis=1
            )
            low = CHANNELS + h * HEAD
            values = jnp.concatenate(
                [kv[s, core, low : low + HEAD, :] for s, core in blocks], axis=1
            )
            values = jnp.concatenate([values, jnp.ones((16, values.shape[1]), BF16)], axis=0)
            scores = dot(keys, query[h], ((0,), (0,)))
            top = jnp.maximum(best[h], jnp.max(scores, axis=0, keepdims=True))
            fade = jnp.exp((best[h] - top) * SCALE)
            weights = jnp.exp((scores - top) * SCALE).astype(BF16)
            accum[h] = accum[h] * fade + dot(values, weights, ((1,), (0,)))
            best[h] = top

    def forward(step):
        behind, ahead = at_y(-step), at_y(step)
        for part, tag in ((0, "k"), (1, "v")):
            if step < 4 or part == 0:
                here = block(behind, c, part)
                wait(here, f"{tag}R{step - 1}")
                if step < 3 or (step == 3 and part == 0):
                    send(here, here, right, f"{tag}R{step}", tag)
                send(here, here, partner, f"s{step}", tag)
            if step < 4 or part == 1:
                here = block(ahead, c, part)
                wait(here, f"{tag}L{step - 1}")
                if step < 3 or (step == 3 and part == 1):
                    send(here, here, left, f"{tag}L{step}", tag)
                send(here, here, partner, f"s{step}", tag)

    def shared(step):
        wait(kv.at[y, other] if step in (0, 4) else kv.at[y], f"s{step}")

    me = x * 2 + c

    def operand(tag, role, source, place):
        for step in NEAR:
            send(source(at_x(step)), place(me), {"dp": at_x(step), "tm": y * 2 + role}, tag, "o" + tag[0])

        @pl.when(c == role)
        def _():
            place(me)[...] = source(x)[...]

        copy = describe(source(x), place(me), partner, tag, "partner")

        @pl.when(c != role)
        def _():
            copy.start()

        count(source(x), f"partner{1 - role}")

    def whole_a(source):
        return abuf.at[source]

    def whole_b(source):
        return bbuf.at[source]

    attend([(y, c)])
    shared(0)
    attend([(y, other)])
    def predict(shard, step):
        rows = pl.ds(shard * SHARD, SHARD)
        psend[rows, :] = dot(downbuf[rows, :], act_ref[...], ((1,), (1,))).astype(BF16)
        for half in range(2):
            to = shard * 2 + half
            source = psend.at[pl.ds(to * CHANNELS, CHANNELS), :]
            copy = describe(source, precv.at[lax.rem(to - z + NZ, NZ)], {"head": to}, "p", "p")

            @pl.when(to != z)
            def _():
                copy.start()

    forward(1)
    upward.relay()
    attend([(at_y(-1), c), (at_y(1), c)])
    shared(1)
    attend([(at_y(-1), other), (at_y(1), other)])
    downward.relay()
    forward(2)
    attend([(at_y(-2), c), (at_y(2), c)])
    shared(2)
    attend([(at_y(-2), other), (at_y(2), other)])
    upward.share()
    forward(3)
    attend([(at_y(-3), c), (at_y(3), c)])

    upward.near()
    upward.far()
    pre = dot(normed_ref[...], upbuf[...], ((1,), (0,)))
    cumulative = 0.5 * (1.0 + lax.erf(pre * math.sqrt(0.5)))
    act_ref[...] = (pre * cumulative).astype(BF16)
    slope_ref[...] = cumulative + pre * (jnp.exp(-0.5 * pre * pre) * (1.0 / math.sqrt(2 * math.pi)))

    operand("act", 0, lambda to: act_ref, whole_b)
    shared(3)
    attend([(at_y(-3), other), (at_y(3), other)])
    downward.share()
    forward(4)

    downward.near()
    for step in (0, 1, 3):
        predict(at_x(step), step)
    attend([(at_y(4), c)])
    downward.far()
    predict(at_x(2), 2)
    shared(4)
    attend([(at_y(4), other)])

    context = [accum[h][:HEAD] / accum[h][HEAD : HEAD + 1] for h in range(2)]
    lane = lax.broadcasted_iota(jnp.int32, (HEAD, 128), 1)
    columns = jnp.zeros((HEAD, 128), F32)
    for h in range(2):
        first = jnp.sum(context[h], axis=1, keepdims=True)
        second = jnp.sum(context[h] * context[h], axis=1, keepdims=True)
        columns = jnp.where(lane == h, first, jnp.where(lane == 2 + h, second, columns))
    columns = jnp.concatenate([columns, jnp.zeros((128 - HEAD, 128), F32)], axis=0)
    stats[0] = columns.T[0:8]
    for step in range(1, NT):
        send(stats.at[0], stats.at[step], {"tm": lax.rem(t + step, NT)}, "stats", "z")


    wait(precv.at[pl.ds(1, NZ - 1)], "p")
    pred = psend[pl.ds(z * CHANNELS, CHANNELS), :].astype(F32)
    for step in range(1, NZ):
        pred = pred + precv[step].astype(F32)
    context = jnp.concatenate(context, axis=0)
    centre = jnp.mean(context, axis=1, keepdims=True)
    raw = dot((context - centre).astype(BF16), pick, ((1,), (1,)))
    number = lax.broadcasted_iota(jnp.int32, (CHANNELS, SLOTS), 1)
    valid = number < jnp.broadcast_to(counts_ref[...], (CHANNELS, SLOTS))

    wait(stats.at[pl.ds(1, NT - 1)], "stats")
    total = stats[0]
    for step in range(1, NT):
        total = total + stats[step]
    columns = jnp.concatenate([total, jnp.zeros((120, 128), F32)], axis=0).T
    means, scales = [], []
    for h in range(2):
        mean = columns[:HEAD, h : h + 1] * (1.0 / LENGTH)
        var = columns[:HEAD, 2 + h : 3 + h] * (1.0 / LENGTH) - mean * mean
        means.append(mean)
        scales.append(lax.rsqrt(var + 1e-5))
    mean, scale = jnp.concatenate(means, axis=0), jnp.concatenate(scales, axis=0)

    aim = (raw + (centre - mean)) * scale
    gap = jnp.where(valid, pred - aim, 0.0) * (2.0 / math.sqrt(D))
    here = cot.at[pl.ds(z * CHANNELS, CHANNELS), :]
    here[...] = gap.astype(BF16)
    for step in (4, 3, 5, 2, 6, 1, 7):
        send(here, here, {"head": at_z(step)}, f"c{step}", "z")

    target_ref[...] = ((context - mean) * scale).astype(BF16)

    def half_a(source, half):
        return abuf.at[source, pl.ds(half * CHANNELS, CHANNELS), :]

    def pass_on(owner):
        to, half = owner // 2, lax.rem(owner, 2)
        source = cot.at[pl.ds(owner * CHANNELS, CHANNELS), :]
        copy = describe(source, half_a(me, half), {"dp": to, "tm": y * 2}, "e", "e")
        mine = jnp.logical_and(to == x, c == 0)
        away = jnp.logical_not(mine)

        @pl.when(mine)
        def _():
            half_a(me, half)[...] = source[...]

        @pl.when(away)
        def _():
            copy.start()

    def back_from(owner):
        rows = pl.ds(owner * CHANNELS, CHANNELS)
        return dot(cot[rows, :], downbuf[rows, :], ((0,), (0,)))

    operand("nrm", 1, lambda to: normed_t.at[pl.ds(to * SHARD, SHARD), :], whole_a)
    pass_on(z)
    back = back_from(z)
    for step in (1, 7, 2, 6, 3, 5, 4):
        owner = at_z(-step)
        wait(cot.at[pl.ds(owner * CHANNELS, CHANNELS), :], f"c{step}")
        pass_on(owner)
        back = back + back_from(owner)
    dpre_ref[...] = (back * slope_ref[...]).astype(BF16)
    for number, (band, bands, _) in enumerate(CHUNKS):
        columns = pl.ds(band * 128, bands * 128)
        operand(
            f"m{number}",
            1,
            lambda to, columns=columns: dpre_ref.at[:, columns],
            lambda source, columns=columns: bbuf.at[source, :, columns],
        )

    @pl.when(c == 0)
    def _():
        wait(bbuf.at[pl.ds(0, 2 * NX - 1)], "act")
        wait(abuf.at[pl.ds(0, 2 * NX - 1)], "e")

    @pl.when(c != 0)
    def _():
        wait(abuf.at[pl.ds(0, 2 * NX - 1)], "nrm")

    def eighth(number, which):
        band, _, rows = CHUNKS[number]
        return pl.ds(band * SHARD + which * rows, rows)

    def landing(number, slot):
        band, _, rows = CHUNKS[number]
        return rsb.at[slot, pl.ds(band * SHARD // NY, rows), :]

    def on_y(step):
        return {"tm": at_y(step) * 2 + c}

    even = lax.rem(y, 2) == 0
    side = 1 - 2 * lax.rem(y, 2)

    def reduce_first(number):
        band, bands, _ = CHUNKS[number]
        columns = pl.ds(band * 128, bands * 128)

        @pl.when(c != 0)
        def _():
            wait(bbuf.at[pl.ds(0, 2 * NX - 1), :, columns], f"m{number}")

        grad = jnp.zeros((SHARD, bands * 128), F32)
        for pair in range(NX):
            rows = jnp.concatenate([abuf[2 * pair], abuf[2 * pair + 1]], axis=1)
            inner = jnp.concatenate([bbuf[2 * pair, :, columns], bbuf[2 * pair + 1, :, columns]], axis=0)
            grad = grad + dot(rows, inner, ((1,), (0,)))
        for at in range(bands):
            stripe = grad[:, at * 128 : (at + 1) * 128]
            low = (band + at) * SHARD
            g32[low : low + SHARD, :] = stripe
            gs[low : low + SHARD, :] = stripe.astype(BF16)
        for slot, step, piece in (
            (0, 1, at_y(3)),
            (1, -1, at_y(-3)),
            (2, 2 * side, at_y(4)),
            (3, 1, at_y(1)),
            (4, -1, at_y(-1)),
        ):
            send(
                gs.at[eighth(number, piece), :],
                landing(number, slot),
                on_y(step),
                f"r{number}{slot // 3}",
                "y",
            )

    def reduce_second(number):
        wait(landing(number, pl.ds(0, 3)), f"r{number}0")
        far = landing(number, 2)[...].astype(F32)
        for slot, step, mine in ((5, 2, even), (6, -2, jnp.logical_not(even))):
            total = g32[eighth(number, at_y(step)), :] + landing(number, slot - 5)[...].astype(F32)
            total = total + jnp.where(mine, far, 0.0)
            out = landing(number, slot - 5 + 7)
            out[...] = total.astype(BF16)
            send(out, landing(number, slot), on_y(step), f"r{number}1", "y")

    def reduce_last(number):
        total = g32[eighth(number, y), :]
        wait(landing(number, pl.ds(3, 4)), f"r{number}1")
        for slot in (3, 4, 5, 6):
            total = total + landing(number, slot)[...].astype(F32)
        here = fown.at[eighth(number, y), :]
        here[...] = total.astype(BF16)
        for step, tag in ((2, "a"), (-2, "b"), (1, "c"), (-1, "c")):
            send(here, here, on_y(step), f"g{number}{tag}", "y")
        hand_over(number, eighth(number, y))

    def hand_over(number, rows):
        send(fown.at[rows, :], foth.at[rows, :], partner, f"h{number}", "y")

    def gather_first(number):
        size = CHUNKS[number][2]
        for step, tag in ((2, "a"), (-2, "b")):
            rows = eighth(number, at_y(-step))
            wait(fown.at[rows, :], f"g{number}{tag}")
            send(fown.at[rows, :], fown.at[rows, :], on_y(step // 2), f"g{number}d", "y")
            hand_over(number, rows)
        rows = eighth(number, at_y(-2 * side))
        send(fown.at[rows, :], fown.at[rows, :], on_y(2 * side), f"g{number}d", "y")
        wait(pieces(2 * size), f"g{number}c")
        for step in (1, -1):
            hand_over(number, eighth(number, at_y(-step)))

    def gather_last(number):
        wait(pieces(3 * CHUNKS[number][2]), f"g{number}d")
        for step in (3, -3, 4):
            hand_over(number, eighth(number, at_y(-step)))

    rest = STACK - SHARD * HIDDEN // 128
    g32[STACK - rest :, :] = jnp.zeros((rest, 128), F32)
    gs[STACK - rest :, :] = jnp.zeros((rest, 128), BF16)
    reduce_first(0)
    reduce_first(1)
    reduce_second(0)
    reduce_second(1)
    reduce_last(0)
    reduce_last(1)
    gather_first(0)
    gather_first(1)
    gather_last(0)
    gather_last(1)
    for number, (band, _, rows) in enumerate(CHUNKS):
        wait(foth.at[pl.ds(band * SHARD, NY * rows), :], f"h{number}")

    def unstack(source, out):
        for band in range(HIDDEN // 128):
            out[:, band * 128 : (band + 1) * 128] = source[band * SHARD : (band + 1) * SHARD, :]

    @pl.when(c == 0)
    def _():
        unstack(fown, gdown_ref)
        unstack(foth, gup_ref)

    @pl.when(c != 0)
    def _():
        unstack(fown, gup_ref)
        unstack(foth, gdown_ref)

    wait_left("w", wbuf.at[pl.ds(0, NX - 1)])
    wait_left("p", pieces((NZ - 1) * CHANNELS))
    for group in ("u", "d", "k", "v", "z", "y", "oa", "on", "om"):
        wait_left(group)

    @pl.when(c == 0)
    def _():
        wait_left("partner", pieces(left_here["partner0"]))
        wait_left("e", pieces((NZ - 2) * CHANNELS))

    @pl.when(c != 0)
    def _():
        wait_left("partner", pieces(left_here["partner1"]))
        wait_left("e", pieces(NZ * CHANNELS))

    assert len(names.index) <= RECEIVES and len(outs.index) <= SENDS


def widen(target_ref, gup_ref, gdown_ref, target_out, gup_out, gdown_out):
    target_out[...] = target_ref[...]
    gup_out[...] = gup_ref[...].astype(F32)
    gdown_out[...] = gdown_ref[...].astype(F32)


def local(frames, masked, kept_counts, teacher_qkv, student_gain, w_up, w_down):
    wt = teacher_qkv.transpose(1, 2, 0).reshape(3 * CHANNELS, SHARD)
    vmem = pl.BlockSpec(memory_space=pltpu.VMEM)
    hbm = pl.BlockSpec(memory_space=pltpu.HBM)
    target, gup, gdown = pl.pallas_call(
        kernel,
        out_shape=(
            jax.ShapeDtypeStruct((CHANNELS, FRAMES), BF16),
            jax.ShapeDtypeStruct((SHARD, HIDDEN), BF16),
            jax.ShapeDtypeStruct((SHARD, HIDDEN), BF16),
        ),
        in_specs=[hbm, vmem, vmem, vmem, hbm, hbm, hbm],
        out_specs=(vmem, vmem, vmem),
        scratch_shapes=[
            pltpu.VMEM((FRAMES, D), BF16),
            pltpu.VMEM((NX, 3 * CHANNELS, SHARD), BF16),
            pltpu.VMEM((D, HIDDEN), BF16),
            pltpu.VMEM((D, HIDDEN), BF16),
            pltpu.VMEM((NY, 2, 2 * CHANNELS, FRAMES), BF16),
            pltpu.VMEM((SLOTS, D), BF16),
            pltpu.VMEM((D, SLOTS), BF16),
            pltpu.VMEM((SLOTS, HIDDEN), BF16),
            pltpu.VMEM((SLOTS, HIDDEN), F32),
            pltpu.VMEM((SLOTS, HIDDEN), BF16),
            pltpu.VMEM((D, SLOTS), BF16),
            pltpu.VMEM((NZ, CHANNELS, SLOTS), BF16),
            pltpu.VMEM((D, SLOTS), BF16),
            pltpu.VMEM((NT, 8, 128), F32),
            pltpu.VMEM((2 * NX, SHARD, SLOTS), BF16),
            pltpu.VMEM((2 * NX, SLOTS, HIDDEN), BF16),
            pltpu.VMEM((STACK, 128), F32),
            pltpu.VMEM((STACK, 128), BF16),
            pltpu.VMEM((NY + 1, PIECE, 128), BF16),
            pltpu.VMEM((STACK, 128), BF16),
            pltpu.VMEM((STACK, 128), BF16),
            pltpu.VMEM((METER, 128), BF16),
            pltpu.SemaphoreType.DMA((5,)),
            pltpu.SemaphoreType.DMA((SENDS,)),
            pltpu.SemaphoreType.DMA((RECEIVES,)),
        ],
        compiler_params=pltpu.CompilerParams(
            collective_id=0, has_side_effects=True, vmem_limit_bytes=60 * 1024 * 1024
        ),
    )(
        frames[0],
        masked,
        kept_counts,
        student_gain,
        wt,
        w_up,
        w_down,
    )
    target, gup, gdown = pl.pallas_call(
        widen,
        out_shape=(
            jax.ShapeDtypeStruct((CHANNELS, FRAMES), BF16),
            jax.ShapeDtypeStruct((SHARD, HIDDEN), F32),
            jax.ShapeDtypeStruct((SHARD, HIDDEN), F32),
        ),
        in_specs=[vmem] * 3,
        out_specs=(vmem, vmem, vmem),
    )(target, gup, gdown)
    return target.T[None], gup, gdown


def solution(mesh):
    placed = (
        P("dp", "tm", None),
        P("dp", "tm"),
        P("dp", "tm"),
        P("dp", None, "head"),
        P(),
        P("dp", "head"),
        P("dp", "head"),
    )
    return jax.shard_map(
        local,
        mesh=mesh,
        in_specs=placed,
        out_specs=(P("dp", "tm", "head"), P("dp", "head"), P("dp", "head")),
        check_vma=False,
    )
```

```python
import math

import jax
import jax.numpy as jnp
from jax import lax
from jax.experimental import pallas as pl
from jax.experimental.pallas import tpu as pltpu
from jax.sharding import PartitionSpec as P

BF16 = jnp.bfloat16
F32 = jnp.float32
MESH = pl.DeviceIdType.MESH

D = 1280
HEAD = 80
FRAMES = 256
SLOTS = 128
CHANNELS = 160
HIDDEN = 640
SHARD = 320
NX, NY, NZ = 4, 8, 8
NT = 2 * NY
PIECE = 208
STACK = NY * PIECE
CHUNKS = ((0, 2, 80), (2, 3, 128))
NEAR = (1, 3, 2)
SENDS, RECEIVES = 13, 67
METER = 5120
LENGTH = NT * FRAMES
SCALE = HEAD**-0.5


def dot(a, b, dims):
    return lax.dot_general(a, b, (dims, ((), ())), preferred_element_type=F32)


class Names:
    def __init__(self):
        self.index = {}

    def __call__(self, name):
        return self.index.setdefault(name, len(self.index))


def kernel(
    frames_hbm,
    masked_hbm,
    counts_ref,
    gain_hbm,
    wt_ref,
    up_ref,
    down_ref,
    target_hbm,
    gup_hbm,
    gdown_hbm,
    target_ref,
    masked_ref,
    gain_ref,
    frames_ref,
    wbuf,
    upbuf,
    downbuf,
    kv,
    normed_ref,
    normed_t,
    act_ref,
    slope_ref,
    dpre_ref,
    psend,
    precv,
    cot,
    stats,
    abuf,
    bbuf,
    g32,
    gs,
    rsb,
    fown,
    foth,
    meter,
    local_sem,
    send_sem,
    recv_sem,
):
    t = lax.axis_index("tm")
    x = lax.axis_index("dp")
    z = lax.axis_index("head")
    y, c = t // 2, t % 2
    other = 1 - c
    partner = {"tm": y * 2 + other}

    def at_x(step):
        return lax.rem(x + step + NX, NX)

    def at_y(step):
        return lax.rem(y + step + NY, NY)

    def at_z(step):
        return lax.rem(z + step + NZ, NZ)

    own_w = pltpu.make_async_copy(wt_ref, wbuf.at[x], local_sem.at[0])
    own_mask = pltpu.make_async_copy(masked_hbm, masked_ref, local_sem.at[1])
    own_gain = pltpu.make_async_copy(gain_hbm, gain_ref, local_sem.at[2])
    own_frames = pltpu.make_async_copy(frames_hbm, frames_ref, local_sem.at[3])
    own_rows = pl.ds(x * SHARD, SHARD)
    own_up = pltpu.make_async_copy(up_ref, upbuf.at[own_rows, :], local_sem.at[4])
    own_down = pltpu.make_async_copy(down_ref, downbuf.at[own_rows, :], local_sem.at[5])
    for copy in (own_w, own_mask, own_gain, own_frames, own_up, own_down):
        copy.start()

    barrier = pltpu.get_barrier_semaphore()
    peers = [partner]
    for step in range(1, NY):
        for core in range(2):
            peers.append({"tm": at_y(step) * 2 + core})
    for step in range(1, NX):
        for core in range(2):
            peers.append({"dp": at_x(step), "tm": y * 2 + core})
    for step in range(1, NZ):
        peers.append({"head": at_z(step)})
    for peer in peers:
        pl.semaphore_signal(barrier, inc=1, device_id=peer, device_id_type=MESH)
    pl.semaphore_wait(barrier, len(peers))

    names, outs = Names(), Names()
    left_here = {}

    def describe(src, dst, device, name, group):
        return pltpu.make_async_remote_copy(
            src_ref=src,
            dst_ref=dst,
            send_sem=send_sem.at[outs(group)],
            recv_sem=recv_sem.at[names(name)],
            device_id=device,
            device_id_type=MESH,
        )

    def send(src, dst, device, name, group):
        describe(src, dst, device, name, group).start()
        count(src, group)

    def count(src, group):
        left_here[group] = left_here.get(group, 0) + math.prod(src.shape) * src.dtype.itemsize // 256

    def wait(dst, name):
        describe(dst, dst, partner, name, "w").wait_recv()

    def pieces(rows):
        return meter.at[pl.ds(0, rows), :]

    def wait_left(group, refs=None):
        refs = pieces(left_here[group]) if refs is None else refs
        describe(refs, refs, partner, "w1", group).wait_send()

    def place_w(shard, row, rows):
        return wbuf.at[shard, pl.ds(row, rows), :]

    def place_up(shard, row, rows):
        return upbuf.at[pl.ds(shard * SHARD + row, rows), :]

    def place_down(shard, row, rows):
        return downbuf.at[pl.ds(shard * SHARD + row, rows), :]

    class Direct:
        def __init__(self, name, place, base, half):
            self.name, self.place, self.half = name, place, half
            self.mine, self.theirs = base + c * half, base + other * half

        def start(self):
            mine = self.place(x, self.mine, self.half)
            for step in NEAR:
                send(mine, mine, {"dp": at_x(step)}, f"{self.name}{step}", "w")

        def share(self):
            for step in NEAR:
                block = self.place(at_x(-step), self.mine, self.half)
                wait(block, f"{self.name}{step}")
                send(block, block, partner, f"{self.name}P", "w")

        def finish(self):
            wait(wbuf.at[pl.ds(0, NX - 1), pl.ds(self.theirs, self.half), :], f"{self.name}P")

    class Relay:
        def __init__(self, name, place, half, first):
            self.name, self.place = name, place
            self.half, self.first = half, first
            self.mine, self.theirs = c * half, other * half

        def start(self):
            mine = self.place(x, self.mine, self.half)
            send(mine, mine, {"dp": at_x(1)}, self.name + "R0", self.name)
            send(mine, mine, {"dp": at_x(-1)}, self.name + "L0", self.name)

        def relay(self):
            n, first = self.half, self.first
            block = self.place(at_x(-1), self.mine, n)
            wait(block, self.name + "R0")
            part = self.place(at_x(-1), self.mine, first)
            send(part, part, {"dp": at_x(1)}, self.name + "R1", self.name)
            send(block, block, partner, self.name + "P0", self.name)
            block = self.place(at_x(1), self.mine, n)
            wait(block, self.name + "L0")
            part = self.place(at_x(1), self.mine + first, n - first)
            send(part, part, {"dp": at_x(-1)}, self.name + "L1", self.name)
            send(block, block, partner, self.name + "P0", self.name)

        def share(self):
            n, first = self.half, self.first
            far = at_x(2)
            part = self.place(far, self.mine, first)
            wait(part, self.name + "R1")
            send(part, part, partner, self.name + "P2", self.name)
            part = self.place(far, self.mine + first, n - first)
            wait(part, self.name + "L1")
            send(part, part, partner, self.name + "P2", self.name)

        def near(self):
            wait(self.place(0, 0, 2 * self.half), self.name + "P0")

        def far(self):
            wait(self.place(at_x(2), self.theirs, self.half), self.name + "P2")

    teacher_kv = Direct("w", place_w, CHANNELS, CHANNELS)
    teacher_q = Direct("q", place_w, 0, HEAD)
    upward = Relay("u", place_up, 160, 80)
    downward = Relay("d", place_down, 160, 80)

    own_w.wait()
    teacher_kv.start()
    teacher_q.start()

    own_mask.wait()
    keep = 1 - masked_ref[...]
    keep = keep.astype(F32)
    before = lax.broadcasted_iota(jnp.int32, (FRAMES, FRAMES), 0)
    after = lax.broadcasted_iota(jnp.int32, (FRAMES, FRAMES), 1)
    upper = jnp.where(before <= after, 1.0, 0.0).astype(BF16)
    rank = dot(jnp.broadcast_to(keep, (16, FRAMES)).astype(BF16), upper, ((1,), (0,)))[0:1]
    slot = lax.broadcasted_iota(jnp.int32, (SLOTS, FRAMES), 0).astype(F32)
    pick = jnp.where(rank - 1.0 == slot, jnp.broadcast_to(keep, (SLOTS, FRAMES)), 0.0).astype(BF16)
    own_frames.wait()
    own_gain.wait()
    chosen = dot(pick, frames_ref[...], ((1,), (0,)))
    centre = jnp.mean(chosen, axis=1, keepdims=True)
    chosen = chosen - centre
    spread = jnp.mean(chosen * chosen, axis=1, keepdims=True)
    normed = chosen * lax.rsqrt(spread + 1e-5) * gain_ref[...].reshape(1, D)
    normed_ref[...] = normed.astype(BF16)
    normed_t[...] = normed.T.astype(BF16)

    def project(low, high):
        out = jnp.zeros((high - low, FRAMES), F32)
        for shard in range(NX):
            out = out + dot(
                wbuf[shard, low:high, :], frames_ref[:, shard * SHARD : (shard + 1) * SHARD], ((1,), (1,))
            )
        return out.astype(BF16)

    def block(source, core, part):
        return kv.at[source, core, pl.ds(part * CHANNELS, CHANNELS), :]

    teacher_kv.share()
    own_up.wait()
    own_down.wait()
    upward.start()
    downward.start()
    teacher_kv.finish()
    kv[y, c] = project(CHANNELS, 3 * CHANNELS)
    right, left = {"tm": at_y(1) * 2 + c}, {"tm": at_y(-1) * 2 + c}
    for part, tag in ((0, "k"), (1, "v")):
        mine = block(y, c, part)
        send(mine, mine, right, tag + "R0", tag)
        send(mine, mine, left, tag + "L0", tag)
        send(mine, mine, partner, "s0", tag)
    teacher_q.share()
    teacher_q.finish()
    query = project(0, CHANNELS)
    query = [query[h * HEAD : (h + 1) * HEAD] for h in range(2)]

    best = [jnp.full((1, FRAMES), -jnp.inf, F32) for _ in range(2)]
    accum = [jnp.zeros((HEAD + 16, FRAMES), F32) for _ in range(2)]

    def attend(blocks):
        for h in range(2):
            keys = jnp.concatenate(
                [kv[s, core, h * HEAD : (h + 1) * HEAD, :] for s, core in blocks], axis=1
            )
            low = CHANNELS + h * HEAD
            values = jnp.concatenate(
                [kv[s, core, low : low + HEAD, :] for s, core in blocks], axis=1
            )
            values = jnp.concatenate([values, jnp.ones((16, values.shape[1]), BF16)], axis=0)
            scores = dot(keys, query[h], ((0,), (0,)))
            top = jnp.maximum(best[h], jnp.max(scores, axis=0, keepdims=True))
            fade = jnp.exp((best[h] - top) * SCALE)
            weights = jnp.exp((scores - top) * SCALE).astype(BF16)
            accum[h] = accum[h] * fade + dot(values, weights, ((1,), (0,)))
            best[h] = top

    def forward(step):
        behind, ahead = at_y(-step), at_y(step)
        for part, tag in ((0, "k"), (1, "v")):
            if step < 4 or part == 0:
                here = block(behind, c, part)
                wait(here, f"{tag}R{step - 1}")
                if step < 3 or (step == 3 and part == 0):
                    send(here, here, right, f"{tag}R{step}", tag)
                send(here, here, partner, f"s{step}", tag)
            if step < 4 or part == 1:
                here = block(ahead, c, part)
                wait(here, f"{tag}L{step - 1}")
                if step < 3 or (step == 3 and part == 1):
                    send(here, here, left, f"{tag}L{step}", tag)
                send(here, here, partner, f"s{step}", tag)

    def shared(step):
        wait(kv.at[y, other] if step in (0, 4) else kv.at[y], f"s{step}")

    me = x * 2 + c

    def operand(tag, role, source, place):
        for step in NEAR:
            send(source(at_x(step)), place(me), {"dp": at_x(step), "tm": y * 2 + role}, tag, "o" + tag[0])

        @pl.when(c == role)
        def _():
            place(me)[...] = source(x)[...]

        copy = describe(source(x), place(me), partner, tag, "partner")

        @pl.when(c != role)
        def _():
            copy.start()

        count(source(x), f"partner{1 - role}")

    def whole_a(source):
        return abuf.at[source]

    def whole_b(source):
        return bbuf.at[source]

    attend([(y, c)])
    shared(0)
    attend([(y, other)])
    def predict(shard, step):
        rows = pl.ds(shard * SHARD, SHARD)
        psend[rows, :] = dot(downbuf[rows, :], act_ref[...], ((1,), (1,))).astype(BF16)
        for half in range(2):
            to = shard * 2 + half
            source = psend.at[pl.ds(to * CHANNELS, CHANNELS), :]
            copy = describe(source, precv.at[lax.rem(to - z + NZ, NZ)], {"head": to}, "p", "p")

            @pl.when(to != z)
            def _():
                copy.start()

    forward(1)
    upward.relay()
    attend([(at_y(-1), c), (at_y(1), c)])
    shared(1)
    attend([(at_y(-1), other), (at_y(1), other)])
    downward.relay()
    forward(2)
    attend([(at_y(-2), c), (at_y(2), c)])
    shared(2)
    attend([(at_y(-2), other), (at_y(2), other)])
    upward.share()
    forward(3)
    attend([(at_y(-3), c), (at_y(3), c)])

    upward.near()
    upward.far()
    pre = dot(normed_ref[...], upbuf[...], ((1,), (0,)))
    cumulative = 0.5 * (1.0 + lax.erf(pre * math.sqrt(0.5)))
    act_ref[...] = (pre * cumulative).astype(BF16)
    slope_ref[...] = cumulative + pre * (jnp.exp(-0.5 * pre * pre) * (1.0 / math.sqrt(2 * math.pi)))

    operand("act", 0, lambda to: act_ref, whole_b)
    shared(3)
    attend([(at_y(-3), other), (at_y(3), other)])
    downward.share()
    forward(4)

    downward.near()
    for step in (0, 1, 3):
        predict(at_x(step), step)
    attend([(at_y(4), c)])
    downward.far()
    predict(at_x(2), 2)
    shared(4)
    attend([(at_y(4), other)])

    context = [accum[h][:HEAD] / accum[h][HEAD : HEAD + 1] for h in range(2)]
    lane = lax.broadcasted_iota(jnp.int32, (HEAD, 128), 1)
    columns = jnp.zeros((HEAD, 128), F32)
    for h in range(2):
        first = jnp.sum(context[h], axis=1, keepdims=True)
        second = jnp.sum(context[h] * context[h], axis=1, keepdims=True)
        columns = jnp.where(lane == h, first, jnp.where(lane == 2 + h, second, columns))
    columns = jnp.concatenate([columns, jnp.zeros((128 - HEAD, 128), F32)], axis=0)
    stats[0] = columns.T[0:8]
    for step in range(1, NT):
        send(stats.at[0], stats.at[step], {"tm": lax.rem(t + step, NT)}, "stats", "z")


    wait(precv.at[pl.ds(1, NZ - 1)], "p")
    pred = psend[pl.ds(z * CHANNELS, CHANNELS), :].astype(F32)
    for step in range(1, NZ):
        pred = pred + precv[step].astype(F32)
    context = jnp.concatenate(context, axis=0)
    centre = jnp.mean(context, axis=1, keepdims=True)
    raw = dot((context - centre).astype(BF16), pick, ((1,), (1,)))
    number = lax.broadcasted_iota(jnp.int32, (CHANNELS, SLOTS), 1)
    valid = number < jnp.broadcast_to(counts_ref[...], (CHANNELS, SLOTS))

    wait(stats.at[pl.ds(1, NT - 1)], "stats")
    total = stats[0]
    for step in range(1, NT):
        total = total + stats[step]
    columns = jnp.concatenate([total, jnp.zeros((120, 128), F32)], axis=0).T
    means, scales = [], []
    for h in range(2):
        mean = columns[:HEAD, h : h + 1] * (1.0 / LENGTH)
        var = columns[:HEAD, 2 + h : 3 + h] * (1.0 / LENGTH) - mean * mean
        means.append(mean)
        scales.append(lax.rsqrt(var + 1e-5))
    mean, scale = jnp.concatenate(means, axis=0), jnp.concatenate(scales, axis=0)

    aim = (raw + (centre - mean)) * scale
    gap = jnp.where(valid, pred - aim, 0.0) * (2.0 / math.sqrt(D))
    here = cot.at[pl.ds(z * CHANNELS, CHANNELS), :]
    here[...] = gap.astype(BF16)
    for step in (4, 3, 5, 2, 6, 1, 7):
        send(here, here, {"head": at_z(step)}, f"c{step}", "z")

    target_ref[...] = ((context - mean) * scale).astype(BF16)
    target_out = pltpu.make_async_copy(target_ref, target_hbm, local_sem.at[6])
    target_out.start()

    def half_a(source, half):
        return abuf.at[source, pl.ds(half * CHANNELS, CHANNELS), :]

    def pass_on(owner):
        to, half = owner // 2, lax.rem(owner, 2)
        source = cot.at[pl.ds(owner * CHANNELS, CHANNELS), :]
        copy = describe(source, half_a(me, half), {"dp": to, "tm": y * 2}, "e", "e")
        mine = jnp.logical_and(to == x, c == 0)
        away = jnp.logical_not(mine)

        @pl.when(mine)
        def _():
            half_a(me, half)[...] = source[...]

        @pl.when(away)
        def _():
            copy.start()

    def back_from(owner):
        rows = pl.ds(owner * CHANNELS, CHANNELS)
        return dot(cot[rows, :], downbuf[rows, :], ((0,), (0,)))

    operand("nrm", 1, lambda to: normed_t.at[pl.ds(to * SHARD, SHARD), :], whole_a)
    pass_on(z)
    back = back_from(z)
    for step in (1, 7, 2, 6, 3, 5, 4):
        owner = at_z(-step)
        wait(cot.at[pl.ds(owner * CHANNELS, CHANNELS), :], f"c{step}")
        pass_on(owner)
        back = back + back_from(owner)
    dpre_ref[...] = (back * slope_ref[...]).astype(BF16)
    for number, (band, bands, _) in enumerate(CHUNKS):
        columns = pl.ds(band * 128, bands * 128)
        operand(
            f"m{number}",
            1,
            lambda to, columns=columns: dpre_ref.at[:, columns],
            lambda source, columns=columns: bbuf.at[source, :, columns],
        )

    @pl.when(c == 0)
    def _():
        wait(bbuf.at[pl.ds(0, 2 * NX - 1)], "act")
        wait(abuf.at[pl.ds(0, 2 * NX - 1)], "e")

    @pl.when(c != 0)
    def _():
        wait(abuf.at[pl.ds(0, 2 * NX - 1)], "nrm")

    def eighth(number, which):
        band, _, rows = CHUNKS[number]
        return pl.ds(band * SHARD + which * rows, rows)

    def landing(number, slot):
        band, _, rows = CHUNKS[number]
        return rsb.at[slot, pl.ds(band * SHARD // NY, rows), :]

    def on_y(step):
        return {"tm": at_y(step) * 2 + c}

    even = lax.rem(y, 2) == 0
    side = 1 - 2 * lax.rem(y, 2)

    def reduce_first(number):
        band, bands, _ = CHUNKS[number]
        columns = pl.ds(band * 128, bands * 128)

        @pl.when(c != 0)
        def _():
            wait(bbuf.at[pl.ds(0, 2 * NX - 1), :, columns], f"m{number}")

        grad = jnp.zeros((SHARD, bands * 128), F32)
        for pair in range(NX):
            rows = jnp.concatenate([abuf[2 * pair], abuf[2 * pair + 1]], axis=1)
            inner = jnp.concatenate([bbuf[2 * pair, :, columns], bbuf[2 * pair + 1, :, columns]], axis=0)
            grad = grad + dot(rows, inner, ((1,), (0,)))
        for at in range(bands):
            stripe = grad[:, at * 128 : (at + 1) * 128]
            low = (band + at) * SHARD
            g32[low : low + SHARD, :] = stripe
            gs[low : low + SHARD, :] = stripe.astype(BF16)
        for slot, step, piece in (
            (0, 1, at_y(3)),
            (1, -1, at_y(-3)),
            (2, 2 * side, at_y(4)),
            (3, 1, at_y(1)),
            (4, -1, at_y(-1)),
        ):
            send(
                gs.at[eighth(number, piece), :],
                landing(number, slot),
                on_y(step),
                f"r{number}{slot // 3}",
                "y",
            )

    def reduce_second(number):
        wait(landing(number, pl.ds(0, 3)), f"r{number}0")
        far = landing(number, 2)[...].astype(F32)
        for slot, step, mine in ((5, 2, even), (6, -2, jnp.logical_not(even))):
            total = g32[eighth(number, at_y(step)), :] + landing(number, slot - 5)[...].astype(F32)
            total = total + jnp.where(mine, far, 0.0)
            out = landing(number, slot - 5 + 7)
            out[...] = total.astype(BF16)
            send(out, landing(number, slot), on_y(step), f"r{number}1", "y")

    def reduce_last(number):
        total = g32[eighth(number, y), :]
        wait(landing(number, pl.ds(3, 4)), f"r{number}1")
        for slot in (3, 4, 5, 6):
            total = total + landing(number, slot)[...].astype(F32)
        here = fown.at[eighth(number, y), :]
        here[...] = total.astype(BF16)
        for step, tag in ((2, "a"), (-2, "b"), (1, "c"), (-1, "c")):
            send(here, here, on_y(step), f"g{number}{tag}", "y")
        hand_over(number, eighth(number, y))

    def hand_over(number, rows):
        send(fown.at[rows, :], foth.at[rows, :], partner, f"h{number}", "y")

    def gather_first(number):
        size = CHUNKS[number][2]
        for step, tag in ((2, "a"), (-2, "b")):
            rows = eighth(number, at_y(-step))
            wait(fown.at[rows, :], f"g{number}{tag}")
            send(fown.at[rows, :], fown.at[rows, :], on_y(step // 2), f"g{number}d", "y")
            hand_over(number, rows)
        rows = eighth(number, at_y(-2 * side))
        send(fown.at[rows, :], fown.at[rows, :], on_y(2 * side), f"g{number}d", "y")
        wait(pieces(2 * size), f"g{number}c")
        for step in (1, -1):
            hand_over(number, eighth(number, at_y(-step)))

    def gather_last(number):
        wait(pieces(3 * CHUNKS[number][2]), f"g{number}d")
        for step in (3, -3, 4):
            hand_over(number, eighth(number, at_y(-step)))

    rest = STACK - SHARD * HIDDEN // 128
    g32[STACK - rest :, :] = jnp.zeros((rest, 128), F32)
    gs[STACK - rest :, :] = jnp.zeros((rest, 128), BF16)
    reduce_first(0)
    reduce_first(1)
    reduce_second(0)
    reduce_second(1)
    reduce_last(0)
    reduce_last(1)
    gather_first(0)
    gather_first(1)
    gather_last(0)
    gather_last(1)
    def results(number):
        band, _, rows = CHUNKS[number]
        part = pl.ds(band * SHARD, NY * rows)
        pairs = ((gdown_hbm, gup_hbm), (gup_hbm, gdown_hbm))
        return [
            [
                pltpu.make_async_copy(source.at[part, :], out.at[part, :], local_sem.at[7 + 2 * number + at])
                for at, (source, out) in enumerate(zip((fown, foth), pair))
            ]
            for pair in pairs
        ]

    written = [results(number) for number in range(len(CHUNKS))]
    for number, (band, _, rows) in enumerate(CHUNKS):
        wait(foth.at[pl.ds(band * SHARD, NY * rows), :], f"h{number}")
        for core in range(2):

            @pl.when(c == core)
            def _():
                for copy in written[number][core]:
                    copy.start()

    wait_left("w", wbuf.at[pl.ds(0, NX - 1)])
    wait_left("p", pieces((NZ - 1) * CHANNELS))
    for group in ("u", "d", "k", "v", "z", "y", "oa", "on", "om"):
        wait_left(group)

    @pl.when(c == 0)
    def _():
        wait_left("partner", pieces(left_here["partner0"]))
        wait_left("e", pieces((NZ - 2) * CHANNELS))

    @pl.when(c != 0)
    def _():
        wait_left("partner", pieces(left_here["partner1"]))
        wait_left("e", pieces(NZ * CHANNELS))

    target_out.wait()
    for core in range(2):

        @pl.when(c == core)
        def _():
            for number in range(len(CHUNKS)):
                for copy in written[number][core]:
                    copy.wait()

    assert len(names.index) <= RECEIVES and len(outs.index) <= SENDS


def widen(target_in, gup_in, gdown_in, target_out, gup_out, gdown_out, narrow, wide, sems):
    through = pltpu.make_async_copy(target_in, target_out, sems.at[8])
    pieces = []
    for at, (source, out) in enumerate(((gup_in, gup_out), (gdown_in, gdown_out))):
        for half, (band, bands) in enumerate(((0, 3), (3, 2))):
            rows, columns = pl.ds(band * SHARD, bands * SHARD), pl.ds(band * 128, bands * 128)
            here, sem = wide.at[at, :, columns], 2 * at + half
            come = pltpu.make_async_copy(source.at[rows, :], narrow.at[at, rows, :], sems.at[sem])
            go = pltpu.make_async_copy(here, out.at[:, columns], sems.at[4 + sem])
            pieces.append((at, band, bands, come, go))
    for *_, come, _ in pieces:
        come.start()
    through.start()
    for at, band, bands, come, go in pieces:
        come.wait()
        for number in range(band, band + bands):
            wide[at, :, number * 128 : (number + 1) * 128] = narrow[
                at, number * SHARD : (number + 1) * SHARD, :
            ].astype(F32)
        go.start()
    for *_, go in pieces:
        go.wait()
    through.wait()


def local(frames, masked, kept_counts, teacher_qkv, student_gain, w_up, w_down):
    wt = teacher_qkv.transpose(1, 2, 0).reshape(3 * CHANNELS, SHARD)
    vmem = pl.BlockSpec(memory_space=pltpu.VMEM)
    hbm = pl.BlockSpec(memory_space=pltpu.HBM)
    target, gup, gdown = pl.pallas_call(
        kernel,
        out_shape=(
            jax.ShapeDtypeStruct((CHANNELS, FRAMES), BF16),
            jax.ShapeDtypeStruct((STACK, 128), BF16),
            jax.ShapeDtypeStruct((STACK, 128), BF16),
        ),
        in_specs=[hbm, hbm, vmem, hbm, hbm, hbm, hbm],
        out_specs=(hbm, hbm, hbm),
        scratch_shapes=[
            pltpu.VMEM((CHANNELS, FRAMES), BF16),
            pltpu.VMEM((1, FRAMES), jnp.int32),
            pltpu.VMEM((D,), F32),
            pltpu.VMEM((FRAMES, D), BF16),
            pltpu.VMEM((NX, 3 * CHANNELS, SHARD), BF16),
            pltpu.VMEM((D, HIDDEN), BF16),
            pltpu.VMEM((D, HIDDEN), BF16),
            pltpu.VMEM((NY, 2, 2 * CHANNELS, FRAMES), BF16),
            pltpu.VMEM((SLOTS, D), BF16),
            pltpu.VMEM((D, SLOTS), BF16),
            pltpu.VMEM((SLOTS, HIDDEN), BF16),
            pltpu.VMEM((SLOTS, HIDDEN), F32),
            pltpu.VMEM((SLOTS, HIDDEN), BF16),
            pltpu.VMEM((D, SLOTS), BF16),
            pltpu.VMEM((NZ, CHANNELS, SLOTS), BF16),
            pltpu.VMEM((D, SLOTS), BF16),
            pltpu.VMEM((NT, 8, 128), F32),
            pltpu.VMEM((2 * NX, SHARD, SLOTS), BF16),
            pltpu.VMEM((2 * NX, SLOTS, HIDDEN), BF16),
            pltpu.VMEM((STACK, 128), F32),
            pltpu.VMEM((STACK, 128), BF16),
            pltpu.VMEM((NY + 1, PIECE, 128), BF16),
            pltpu.VMEM((STACK, 128), BF16),
            pltpu.VMEM((STACK, 128), BF16),
            pltpu.VMEM((METER, 128), BF16),
            pltpu.SemaphoreType.DMA((11,)),
            pltpu.SemaphoreType.DMA((SENDS,)),
            pltpu.SemaphoreType.DMA((RECEIVES,)),
        ],
        compiler_params=pltpu.CompilerParams(
            collective_id=0, has_side_effects=True, vmem_limit_bytes=60 * 1024 * 1024
        ),
    )(
        frames[0],
        masked,
        kept_counts,
        student_gain,
        wt,
        w_up,
        w_down,
    )
    target, gup, gdown = pl.pallas_call(
        widen,
        out_shape=(
            jax.ShapeDtypeStruct((CHANNELS, FRAMES), BF16),
            jax.ShapeDtypeStruct((SHARD, HIDDEN), F32),
            jax.ShapeDtypeStruct((SHARD, HIDDEN), F32),
        ),
        in_specs=[hbm] * 3,
        out_specs=(hbm, hbm, hbm),
        scratch_shapes=[
            pltpu.VMEM((2, STACK, 128), BF16),
            pltpu.VMEM((2, SHARD, HIDDEN), F32),
            pltpu.SemaphoreType.DMA((9,)),
        ],
        compiler_params=pltpu.CompilerParams(vmem_limit_bytes=60 * 1024 * 1024),
    )(target, gup, gdown)
    return target.T[None], gup, gdown


def solution(mesh):
    placed = (
        P("dp", "tm", None),
        P("dp", "tm"),
        P("dp", "tm"),
        P("dp", None, "head"),
        P(),
        P("dp", "head"),
        P("dp", "head"),
    )
    return jax.shard_map(
        local,
        mesh=mesh,
        in_specs=placed,
        out_specs=(P("dp", "tm", "head"), P("dp", "head"), P("dp", "head")),
        check_vma=False,
    )
```

```python
import math

import jax
import jax.numpy as jnp
from jax import lax
from jax.experimental import pallas as pl
from jax.experimental.pallas import tpu as pltpu
from jax.sharding import PartitionSpec as P

BF16 = jnp.bfloat16
F32 = jnp.float32
MESH = pl.DeviceIdType.MESH

D = 1280
HEAD = 80
FRAMES = 256
SLOTS = 128
CHANNELS = 160
HIDDEN = 640
SHARD = 320
NX, NY, NZ = 4, 8, 8
NT = 2 * NY
PIECE = 208
STACK = NY * PIECE
CHUNKS = ((0, 2, 80), (2, 3, 128))
NEAR = (1, 3, 2)
SENDS, RECEIVES = 13, 67
METER = 5120
LENGTH = NT * FRAMES
SCALE = HEAD**-0.5


def dot(a, b, dims):
    return lax.dot_general(a, b, (dims, ((), ())), preferred_element_type=F32)


class Names:
    def __init__(self):
        self.index = {}

    def __call__(self, name):
        return self.index.setdefault(name, len(self.index))


def kernel(
    frames_hbm,
    masked_hbm,
    counts_ref,
    gain_hbm,
    wt_ref,
    up_ref,
    down_ref,
    target_hbm,
    gup_hbm,
    gdown_hbm,
    target_ref,
    masked_ref,
    gain_ref,
    frames_ref,
    wbuf,
    upbuf,
    downbuf,
    kv,
    normed_ref,
    normed_t,
    act_ref,
    slope_ref,
    dpre_ref,
    psend,
    precv,
    cot,
    stats,
    abuf,
    bbuf,
    g32,
    gs,
    rsb,
    fown,
    foth,
    meter,
    local_sem,
    send_sem,
    recv_sem,
):
    t = lax.axis_index("tm")
    x = lax.axis_index("dp")
    z = lax.axis_index("head")
    y, c = t // 2, t % 2
    other = 1 - c
    partner = {"tm": y * 2 + other}

    def at_x(step):
        return lax.rem(x + step + NX, NX)

    def at_y(step):
        return lax.rem(y + step + NY, NY)

    def at_z(step):
        return lax.rem(z + step + NZ, NZ)

    own_w = pltpu.make_async_copy(wt_ref, wbuf.at[x], local_sem.at[0])
    own_mask = pltpu.make_async_copy(masked_hbm, masked_ref, local_sem.at[1])
    own_gain = pltpu.make_async_copy(gain_hbm, gain_ref, local_sem.at[2])
    own_frames = pltpu.make_async_copy(frames_hbm, frames_ref, local_sem.at[3])
    own_rows = pl.ds(x * SHARD, SHARD)
    own_up = pltpu.make_async_copy(up_ref, upbuf.at[own_rows, :], local_sem.at[4])
    own_down = pltpu.make_async_copy(down_ref, downbuf.at[own_rows, :], local_sem.at[5])
    for copy in (own_w, own_mask, own_gain, own_frames, own_up, own_down):
        copy.start()

    barrier = pltpu.get_barrier_semaphore()
    peers = [partner]
    for step in range(1, NY):
        for core in range(2):
            peers.append({"tm": at_y(step) * 2 + core})
    for step in range(1, NX):
        for core in range(2):
            peers.append({"dp": at_x(step), "tm": y * 2 + core})
    for step in range(1, NZ):
        peers.append({"head": at_z(step)})
    for peer in peers:
        pl.semaphore_signal(barrier, inc=1, device_id=peer, device_id_type=MESH)
    pl.semaphore_wait(barrier, len(peers))

    names, outs = Names(), Names()
    left_here = {}

    def describe(src, dst, device, name, group):
        return pltpu.make_async_remote_copy(
            src_ref=src,
            dst_ref=dst,
            send_sem=send_sem.at[outs(group)],
            recv_sem=recv_sem.at[names(name)],
            device_id=device,
            device_id_type=MESH,
        )

    def send(src, dst, device, name, group):
        describe(src, dst, device, name, group).start()
        count(src, group)

    def count(src, group):
        left_here[group] = left_here.get(group, 0) + math.prod(src.shape) * src.dtype.itemsize // 256

    def wait(dst, name):
        describe(dst, dst, partner, name, "w").wait_recv()

    def pieces(rows):
        return meter.at[pl.ds(0, rows), :]

    def wait_left(group, refs=None):
        refs = pieces(left_here[group]) if refs is None else refs
        describe(refs, refs, partner, "w1", group).wait_send()

    def place_w(shard, row, rows):
        return wbuf.at[shard, pl.ds(row, rows), :]

    def place_up(shard, row, rows):
        return upbuf.at[pl.ds(shard * SHARD + row, rows), :]

    def place_down(shard, row, rows):
        return downbuf.at[pl.ds(shard * SHARD + row, rows), :]

    class Direct:
        def __init__(self, name, place, base, half):
            self.name, self.place, self.half = name, place, half
            self.mine, self.theirs = base + c * half, base + other * half

        def start(self):
            mine = self.place(x, self.mine, self.half)
            for step in NEAR:
                send(mine, mine, {"dp": at_x(step)}, f"{self.name}{step}", "w")

        def share(self):
            for step in NEAR:
                block = self.place(at_x(-step), self.mine, self.half)
                wait(block, f"{self.name}{step}")
                send(block, block, partner, f"{self.name}P", "w")

        def finish(self):
            wait(wbuf.at[pl.ds(0, NX - 1), pl.ds(self.theirs, self.half), :], f"{self.name}P")

    class Relay:
        def __init__(self, name, place, half, first):
            self.name, self.place = name, place
            self.half, self.first = half, first
            self.mine, self.theirs = c * half, other * half

        def start(self):
            mine = self.place(x, self.mine, self.half)
            send(mine, mine, {"dp": at_x(1)}, self.name + "R0", self.name)
            send(mine, mine, {"dp": at_x(-1)}, self.name + "L0", self.name)

        def relay(self):
            n, first = self.half, self.first
            block = self.place(at_x(-1), self.mine, n)
            wait(block, self.name + "R0")
            part = self.place(at_x(-1), self.mine, first)
            send(part, part, {"dp": at_x(1)}, self.name + "R1", self.name)
            send(block, block, partner, self.name + "P0", self.name)
            block = self.place(at_x(1), self.mine, n)
            wait(block, self.name + "L0")
            part = self.place(at_x(1), self.mine + first, n - first)
            send(part, part, {"dp": at_x(-1)}, self.name + "L1", self.name)
            send(block, block, partner, self.name + "P0", self.name)

        def share(self):
            n, first = self.half, self.first
            far = at_x(2)
            part = self.place(far, self.mine, first)
            wait(part, self.name + "R1")
            send(part, part, partner, self.name + "P2", self.name)
            part = self.place(far, self.mine + first, n - first)
            wait(part, self.name + "L1")
            send(part, part, partner, self.name + "P2", self.name)

        def near(self):
            wait(self.place(0, 0, 2 * self.half), self.name + "P0")

        def far(self):
            wait(self.place(at_x(2), self.theirs, self.half), self.name + "P2")

    teacher_kv = Direct("w", place_w, CHANNELS, CHANNELS)
    teacher_q = Direct("q", place_w, 0, HEAD)
    upward = Relay("u", place_up, 160, 80)
    downward = Relay("d", place_down, 160, 80)

    own_w.wait()
    teacher_kv.start()
    teacher_q.start()

    own_mask.wait()
    keep = 1 - masked_ref[...]
    keep = keep.astype(F32)
    before = lax.broadcasted_iota(jnp.int32, (FRAMES, FRAMES), 0)
    after = lax.broadcasted_iota(jnp.int32, (FRAMES, FRAMES), 1)
    upper = jnp.where(before <= after, 1.0, 0.0).astype(BF16)
    rank = dot(jnp.broadcast_to(keep, (16, FRAMES)).astype(BF16), upper, ((1,), (0,)))[0:1]
    slot = lax.broadcasted_iota(jnp.int32, (SLOTS, FRAMES), 0).astype(F32)
    pick = jnp.where(rank - 1.0 == slot, jnp.broadcast_to(keep, (SLOTS, FRAMES)), 0.0).astype(BF16)
    own_frames.wait()
    own_gain.wait()
    chosen = dot(pick, frames_ref[...], ((1,), (0,)))
    centre = jnp.mean(chosen, axis=1, keepdims=True)
    chosen = chosen - centre
    spread = jnp.mean(chosen * chosen, axis=1, keepdims=True)
    normed = chosen * lax.rsqrt(spread + 1e-5) * gain_ref[...].reshape(1, D)
    normed_ref[...] = normed.astype(BF16)
    normed_t[...] = normed.T.astype(BF16)

    def project(low, high):
        out = jnp.zeros((high - low, FRAMES), F32)
        for shard in range(NX):
            out = out + dot(
                wbuf[shard, low:high, :], frames_ref[:, shard * SHARD : (shard + 1) * SHARD], ((1,), (1,))
            )
        return out.astype(BF16)

    def block(source, core, part):
        return kv.at[source, core, pl.ds(part * CHANNELS, CHANNELS), :]

    teacher_kv.share()
    own_up.wait()
    own_down.wait()
    upward.start()
    downward.start()
    teacher_kv.finish()
    kv[y, c] = project(CHANNELS, 3 * CHANNELS)
    right, left = {"tm": at_y(1) * 2 + c}, {"tm": at_y(-1) * 2 + c}
    for part, tag in ((0, "k"), (1, "v")):
        mine = block(y, c, part)
        send(mine, mine, right, tag + "R0", tag)
        send(mine, mine, left, tag + "L0", tag)
        send(mine, mine, partner, "s0", tag)
    teacher_q.share()
    teacher_q.finish()
    query = project(0, CHANNELS)
    query = [query[h * HEAD : (h + 1) * HEAD] for h in range(2)]

    best = [jnp.full((1, FRAMES), -jnp.inf, F32) for _ in range(2)]
    accum = [jnp.zeros((HEAD + 16, FRAMES), F32) for _ in range(2)]

    def attend(blocks):
        for h in range(2):
            keys = jnp.concatenate(
                [kv[s, core, h * HEAD : (h + 1) * HEAD, :] for s, core in blocks], axis=1
            )
            low = CHANNELS + h * HEAD
            values = jnp.concatenate(
                [kv[s, core, low : low + HEAD, :] for s, core in blocks], axis=1
            )
            values = jnp.concatenate([values, jnp.ones((16, values.shape[1]), BF16)], axis=0)
            scores = dot(keys, query[h], ((0,), (0,)))
            top = jnp.maximum(best[h], jnp.max(scores, axis=0, keepdims=True))
            fade = jnp.exp((best[h] - top) * SCALE)
            weights = jnp.exp((scores - top) * SCALE).astype(BF16)
            accum[h] = accum[h] * fade + dot(values, weights, ((1,), (0,)))
            best[h] = top

    def forward(step):
        behind, ahead = at_y(-step), at_y(step)
        for part, tag in ((0, "k"), (1, "v")):
            if step < 4 or part == 0:
                here = block(behind, c, part)
                wait(here, f"{tag}R{step - 1}")
                if step < 3 or (step == 3 and part == 0):
                    send(here, here, right, f"{tag}R{step}", tag)
                send(here, here, partner, f"s{step}", tag)
            if step < 4 or part == 1:
                here = block(ahead, c, part)
                wait(here, f"{tag}L{step - 1}")
                if step < 3 or (step == 3 and part == 1):
                    send(here, here, left, f"{tag}L{step}", tag)
                send(here, here, partner, f"s{step}", tag)

    def shared(step):
        wait(kv.at[y, other] if step in (0, 4) else kv.at[y], f"s{step}")

    me = x * 2 + c

    def operand(tag, role, source, place):
        for step in NEAR:
            send(source(at_x(step)), place(me), {"dp": at_x(step), "tm": y * 2 + role}, tag, "o" + tag[0])

        @pl.when(c == role)
        def _():
            place(me)[...] = source(x)[...]

        copy = describe(source(x), place(me), partner, tag, "partner")

        @pl.when(c != role)
        def _():
            copy.start()

        count(source(x), f"partner{1 - role}")

    def whole_a(source):
        return abuf.at[source]

    def whole_b(source):
        return bbuf.at[source]

    attend([(y, c)])
    shared(0)
    attend([(y, other)])
    def predict(shard, step):
        rows = pl.ds(shard * SHARD, SHARD)
        psend[rows, :] = dot(downbuf[rows, :], act_ref[...], ((1,), (1,))).astype(BF16)
        for half in range(2):
            to = shard * 2 + half
            source = psend.at[pl.ds(to * CHANNELS, CHANNELS), :]
            copy = describe(source, precv.at[lax.rem(to - z + NZ, NZ)], {"head": to}, "p", "p")

            @pl.when(to != z)
            def _():
                copy.start()

    forward(1)
    upward.relay()
    attend([(at_y(-1), c), (at_y(1), c)])
    shared(1)
    attend([(at_y(-1), other), (at_y(1), other)])
    downward.relay()
    forward(2)
    attend([(at_y(-2), c), (at_y(2), c)])
    shared(2)
    attend([(at_y(-2), other), (at_y(2), other)])
    upward.share()
    forward(3)
    attend([(at_y(-3), c), (at_y(3), c)])

    upward.near()
    upward.far()
    pre = dot(normed_ref[...], upbuf[...], ((1,), (0,)))
    cumulative = 0.5 * (1.0 + lax.erf(pre * math.sqrt(0.5)))
    act_ref[...] = (pre * cumulative).astype(BF16)
    slope_ref[...] = cumulative + pre * (jnp.exp(-0.5 * pre * pre) * (1.0 / math.sqrt(2 * math.pi)))

    operand("act", 0, lambda to: act_ref, whole_b)
    shared(3)
    attend([(at_y(-3), other), (at_y(3), other)])
    downward.share()
    forward(4)

    downward.near()
    for step in (0, 1, 3):
        predict(at_x(step), step)
    attend([(at_y(4), c)])
    downward.far()
    predict(at_x(2), 2)
    shared(4)
    attend([(at_y(4), other)])

    context = [accum[h][:HEAD] / accum[h][HEAD : HEAD + 1] for h in range(2)]
    lane = lax.broadcasted_iota(jnp.int32, (HEAD, 128), 1)
    columns = jnp.zeros((HEAD, 128), F32)
    for h in range(2):
        first = jnp.sum(context[h], axis=1, keepdims=True)
        second = jnp.sum(context[h] * context[h], axis=1, keepdims=True)
        columns = jnp.where(lane == h, first, jnp.where(lane == 2 + h, second, columns))
    columns = jnp.concatenate([columns, jnp.zeros((128 - HEAD, 128), F32)], axis=0)
    stats[0] = columns.T[0:8]
    for step in range(1, NT):
        send(stats.at[0], stats.at[step], {"tm": lax.rem(t + step, NT)}, "stats", "z")


    wait(precv.at[pl.ds(1, NZ - 1)], "p")
    pred = psend[pl.ds(z * CHANNELS, CHANNELS), :].astype(F32)
    for step in range(1, NZ):
        pred = pred + precv[step].astype(F32)
    context = jnp.concatenate(context, axis=0)
    centre = jnp.mean(context, axis=1, keepdims=True)
    raw = dot((context - centre).astype(BF16), pick, ((1,), (1,)))
    number = lax.broadcasted_iota(jnp.int32, (CHANNELS, SLOTS), 1)
    valid = number < jnp.broadcast_to(counts_ref[...], (CHANNELS, SLOTS))

    wait(stats.at[pl.ds(1, NT - 1)], "stats")
    total = stats[0]
    for step in range(1, NT):
        total = total + stats[step]
    columns = jnp.concatenate([total, jnp.zeros((120, 128), F32)], axis=0).T
    means, scales = [], []
    for h in range(2):
        mean = columns[:HEAD, h : h + 1] * (1.0 / LENGTH)
        var = columns[:HEAD, 2 + h : 3 + h] * (1.0 / LENGTH) - mean * mean
        means.append(mean)
        scales.append(lax.rsqrt(var + 1e-5))
    mean, scale = jnp.concatenate(means, axis=0), jnp.concatenate(scales, axis=0)

    aim = (raw + (centre - mean)) * scale
    gap = jnp.where(valid, pred - aim, 0.0) * (2.0 / math.sqrt(D))
    here = cot.at[pl.ds(z * CHANNELS, CHANNELS), :]
    here[...] = gap.astype(BF16)
    for step in (4, 3, 5, 2, 6, 1, 7):
        send(here, here, {"head": at_z(step)}, f"c{step}", "z")

    target_ref[...] = ((context - mean) * scale).astype(BF16)
    target_out = pltpu.make_async_copy(target_ref, target_hbm, local_sem.at[6])
    target_out.start()

    def half_a(source, half):
        return abuf.at[source, pl.ds(half * CHANNELS, CHANNELS), :]

    def pass_on(owner):
        to, half = owner // 2, lax.rem(owner, 2)
        source = cot.at[pl.ds(owner * CHANNELS, CHANNELS), :]
        copy = describe(source, half_a(me, half), {"dp": to, "tm": y * 2}, "e", "e")
        mine = jnp.logical_and(to == x, c == 0)
        away = jnp.logical_not(mine)

        @pl.when(mine)
        def _():
            half_a(me, half)[...] = source[...]

        @pl.when(away)
        def _():
            copy.start()

    def back_from(owner):
        rows = pl.ds(owner * CHANNELS, CHANNELS)
        return dot(cot[rows, :], downbuf[rows, :], ((0,), (0,)))

    operand("nrm", 1, lambda to: normed_t.at[pl.ds(to * SHARD, SHARD), :], whole_a)
    pass_on(z)
    back = back_from(z)
    for step in (1, 7, 2, 6, 3, 5, 4):
        owner = at_z(-step)
        wait(cot.at[pl.ds(owner * CHANNELS, CHANNELS), :], f"c{step}")
        pass_on(owner)
        back = back + back_from(owner)
    dpre_ref[...] = (back * slope_ref[...]).astype(BF16)
    for number, (band, bands, _) in enumerate(CHUNKS):
        columns = pl.ds(band * 128, bands * 128)
        operand(
            f"m{number}",
            1,
            lambda to, columns=columns: dpre_ref.at[:, columns],
            lambda source, columns=columns: bbuf.at[source, :, columns],
        )

    @pl.when(c == 0)
    def _():
        wait(bbuf.at[pl.ds(0, 2 * NX - 1)], "act")
        wait(abuf.at[pl.ds(0, 2 * NX - 1)], "e")

    @pl.when(c != 0)
    def _():
        wait(abuf.at[pl.ds(0, 2 * NX - 1)], "nrm")

    def eighth(number, which):
        band, _, rows = CHUNKS[number]
        return pl.ds(band * SHARD + which * rows, rows)

    def landing(number, slot):
        band, _, rows = CHUNKS[number]
        return rsb.at[slot, pl.ds(band * SHARD // NY, rows), :]

    def on_y(step):
        return {"tm": at_y(step) * 2 + c}

    even = lax.rem(y, 2) == 0
    side = 1 - 2 * lax.rem(y, 2)

    def reduce_first(number):
        band, bands, _ = CHUNKS[number]
        columns = pl.ds(band * 128, bands * 128)

        @pl.when(c != 0)
        def _():
            wait(bbuf.at[pl.ds(0, 2 * NX - 1), :, columns], f"m{number}")

        grad = jnp.zeros((SHARD, bands * 128), F32)
        for pair in range(NX):
            rows = jnp.concatenate([abuf[2 * pair], abuf[2 * pair + 1]], axis=1)
            inner = jnp.concatenate([bbuf[2 * pair, :, columns], bbuf[2 * pair + 1, :, columns]], axis=0)
            grad = grad + dot(rows, inner, ((1,), (0,)))
        for at in range(bands):
            stripe = grad[:, at * 128 : (at + 1) * 128]
            low = (band + at) * SHARD
            g32[low : low + SHARD, :] = stripe
            gs[low : low + SHARD, :] = stripe.astype(BF16)
        for slot, step, piece in (
            (0, 1, at_y(3)),
            (1, -1, at_y(-3)),
            (2, 2 * side, at_y(4)),
            (3, 1, at_y(1)),
            (4, -1, at_y(-1)),
        ):
            send(
                gs.at[eighth(number, piece), :],
                landing(number, slot),
                on_y(step),
                f"r{number}{slot // 3}",
                "y",
            )

    def reduce_second(number):
        wait(landing(number, pl.ds(0, 3)), f"r{number}0")
        far = landing(number, 2)[...].astype(F32)
        for slot, step, mine in ((5, 2, even), (6, -2, jnp.logical_not(even))):
            total = g32[eighth(number, at_y(step)), :] + landing(number, slot - 5)[...].astype(F32)
            total = total + jnp.where(mine, far, 0.0)
            out = landing(number, slot - 5 + 7)
            out[...] = total.astype(BF16)
            send(out, landing(number, slot), on_y(step), f"r{number}1", "y")

    def reduce_last(number):
        total = g32[eighth(number, y), :]
        wait(landing(number, pl.ds(3, 4)), f"r{number}1")
        for slot in (3, 4, 5, 6):
            total = total + landing(number, slot)[...].astype(F32)
        here = fown.at[eighth(number, y), :]
        here[...] = total.astype(BF16)
        for step, tag in ((2, "a"), (-2, "b"), (1, "c"), (-1, "c")):
            send(here, here, on_y(step), f"g{number}{tag}", "y")
        hand_over(number, eighth(number, y))

    def hand_over(number, rows):
        send(fown.at[rows, :], foth.at[rows, :], partner, f"h{number}", "y")

    def gather_first(number):
        size = CHUNKS[number][2]
        for step, tag in ((2, "a"), (-2, "b")):
            rows = eighth(number, at_y(-step))
            wait(fown.at[rows, :], f"g{number}{tag}")
            send(fown.at[rows, :], fown.at[rows, :], on_y(step // 2), f"g{number}d", "y")
            hand_over(number, rows)
        rows = eighth(number, at_y(-2 * side))
        send(fown.at[rows, :], fown.at[rows, :], on_y(2 * side), f"g{number}d", "y")
        wait(pieces(2 * size), f"g{number}c")
        for step in (1, -1):
            hand_over(number, eighth(number, at_y(-step)))

    def gather_last(number):
        wait(pieces(3 * CHUNKS[number][2]), f"g{number}d")
        for step in (3, -3, 4):
            hand_over(number, eighth(number, at_y(-step)))

    rest = STACK - SHARD * HIDDEN // 128
    g32[STACK - rest :, :] = jnp.zeros((rest, 128), F32)
    gs[STACK - rest :, :] = jnp.zeros((rest, 128), BF16)
    reduce_first(0)
    reduce_first(1)
    reduce_second(0)
    reduce_second(1)
    reduce_last(0)
    reduce_last(1)
    gather_first(0)
    gather_first(1)
    gather_last(0)
    gather_last(1)
    def results(number):
        band, _, rows = CHUNKS[number]
        part = pl.ds(band * SHARD, NY * rows)
        pairs = ((gdown_hbm, gup_hbm), (gup_hbm, gdown_hbm))
        return [
            [
                pltpu.make_async_copy(source.at[part, :], out.at[part, :], local_sem.at[7 + 2 * number + at])
                for at, (source, out) in enumerate(zip((fown, foth), pair))
            ]
            for pair in pairs
        ]

    written = [results(number) for number in range(len(CHUNKS))]
    for number, (band, _, rows) in enumerate(CHUNKS):
        wait(foth.at[pl.ds(band * SHARD, NY * rows), :], f"h{number}")
        for core in range(2):

            @pl.when(c == core)
            def _():
                for copy in written[number][core]:
                    copy.start()

    wait_left("w", wbuf.at[pl.ds(0, NX - 1)])
    wait_left("p", pieces((NZ - 1) * CHANNELS))
    for group in ("u", "d", "k", "v", "z", "y", "oa", "on", "om"):
        wait_left(group)

    @pl.when(c == 0)
    def _():
        wait_left("partner", pieces(left_here["partner0"]))
        wait_left("e", pieces((NZ - 2) * CHANNELS))

    @pl.when(c != 0)
    def _():
        wait_left("partner", pieces(left_here["partner1"]))
        wait_left("e", pieces(NZ * CHANNELS))

    target_out.wait()
    for core in range(2):

        @pl.when(c == core)
        def _():
            for number in range(len(CHUNKS)):
                for copy in written[number][core]:
                    copy.wait()

    assert len(names.index) <= RECEIVES and len(outs.index) <= SENDS


def widen(target_in, gup_in, gdown_in, target_out, gup_out, gdown_out, target, narrow, wide, sems):
    target_come = pltpu.make_async_copy(target_in, target, sems.at[0])
    target_go = pltpu.make_async_copy(target, target_out, sems.at[1])
    comes = [
        pltpu.make_async_copy(source, narrow.at[at], sems.at[2 + at])
        for at, source in enumerate((gup_in, gdown_in))
    ]
    for come in comes:
        come.start()
    target_come.start()
    goes = []
    for at, out in enumerate((gup_out, gdown_out)):
        comes[at].wait()
        for half in range(2):
            low, rows = half * CHANNELS, pl.ds(half * CHANNELS, CHANNELS)
            for band in range(HIDDEN // 128):
                source = narrow[at, band * SHARD + low : band * SHARD + low + CHANNELS, :]
                wide[at, low : low + CHANNELS, band * 128 : (band + 1) * 128] = source.astype(F32)
            goes.append(
                pltpu.make_async_copy(wide.at[at, rows, :], out.at[rows, :], sems.at[4 + 2 * at + half])
            )
            goes[-1].start()
    target_come.wait()
    target_go.start()
    for go in goes:
        go.wait()
    target_go.wait()


def local(frames, masked, kept_counts, teacher_qkv, student_gain, w_up, w_down):
    wt = teacher_qkv.transpose(1, 2, 0).reshape(3 * CHANNELS, SHARD)
    vmem = pl.BlockSpec(memory_space=pltpu.VMEM)
    hbm = pl.BlockSpec(memory_space=pltpu.HBM)
    target, gup, gdown = pl.pallas_call(
        kernel,
        out_shape=(
            jax.ShapeDtypeStruct((CHANNELS, FRAMES), BF16),
            jax.ShapeDtypeStruct((STACK, 128), BF16),
            jax.ShapeDtypeStruct((STACK, 128), BF16),
        ),
        in_specs=[hbm, hbm, vmem, hbm, hbm, hbm, hbm],
        out_specs=(hbm, hbm, hbm),
        scratch_shapes=[
            pltpu.VMEM((CHANNELS, FRAMES), BF16),
            pltpu.VMEM((1, FRAMES), jnp.int32),
            pltpu.VMEM((D,), F32),
            pltpu.VMEM((FRAMES, D), BF16),
            pltpu.VMEM((NX, 3 * CHANNELS, SHARD), BF16),
            pltpu.VMEM((D, HIDDEN), BF16),
            pltpu.VMEM((D, HIDDEN), BF16),
            pltpu.VMEM((NY, 2, 2 * CHANNELS, FRAMES), BF16),
            pltpu.VMEM((SLOTS, D), BF16),
            pltpu.VMEM((D, SLOTS), BF16),
            pltpu.VMEM((SLOTS, HIDDEN), BF16),
            pltpu.VMEM((SLOTS, HIDDEN), F32),
            pltpu.VMEM((SLOTS, HIDDEN), BF16),
            pltpu.VMEM((D, SLOTS), BF16),
            pltpu.VMEM((NZ, CHANNELS, SLOTS), BF16),
            pltpu.VMEM((D, SLOTS), BF16),
            pltpu.VMEM((NT, 8, 128), F32),
            pltpu.VMEM((2 * NX, SHARD, SLOTS), BF16),
            pltpu.VMEM((2 * NX, SLOTS, HIDDEN), BF16),
            pltpu.VMEM((STACK, 128), F32),
            pltpu.VMEM((STACK, 128), BF16),
            pltpu.VMEM((NY + 1, PIECE, 128), BF16),
            pltpu.VMEM((STACK, 128), BF16),
            pltpu.VMEM((STACK, 128), BF16),
            pltpu.VMEM((METER, 128), BF16),
            pltpu.SemaphoreType.DMA((11,)),
            pltpu.SemaphoreType.DMA((SENDS,)),
            pltpu.SemaphoreType.DMA((RECEIVES,)),
        ],
        compiler_params=pltpu.CompilerParams(
            collective_id=0, has_side_effects=True, vmem_limit_bytes=60 * 1024 * 1024
        ),
    )(
        frames[0],
        masked,
        kept_counts,
        student_gain,
        wt,
        w_up,
        w_down,
    )
    target, gup, gdown = pl.pallas_call(
        widen,
        out_shape=(
            jax.ShapeDtypeStruct((CHANNELS, FRAMES), BF16),
            jax.ShapeDtypeStruct((SHARD, HIDDEN), F32),
            jax.ShapeDtypeStruct((SHARD, HIDDEN), F32),
        ),
        in_specs=[hbm] * 3,
        out_specs=(hbm, hbm, hbm),
        scratch_shapes=[
            pltpu.VMEM((CHANNELS, FRAMES), BF16),
            pltpu.VMEM((2, STACK, 128), BF16),
            pltpu.VMEM((2, SHARD, HIDDEN), F32),
            pltpu.SemaphoreType.DMA((8,)),
        ],
        compiler_params=pltpu.CompilerParams(vmem_limit_bytes=60 * 1024 * 1024),
    )(target, gup, gdown)
    return target.T[None], gup, gdown


def solution(mesh):
    placed = (
        P("dp", "tm", None),
        P("dp", "tm"),
        P("dp", "tm"),
        P("dp", None, "head"),
        P(),
        P("dp", "head"),
        P("dp", "head"),
    )
    return jax.shard_map(
        local,
        mesh=mesh,
        in_specs=placed,
        out_specs=(P("dp", "tm", "head"), P("dp", "head"), P("dp", "head")),
        check_vma=False,
    )
```

```python
import math

import jax
import jax.numpy as jnp
from jax import lax
from jax.experimental import pallas as pl
from jax.experimental.pallas import tpu as pltpu
from jax.sharding import PartitionSpec as P

BF16 = jnp.bfloat16
F32 = jnp.float32
MESH = pl.DeviceIdType.MESH

D = 1280
HEAD = 80
FRAMES = 256
SLOTS = 128
CHANNELS = 160
HIDDEN = 640
SHARD = 320
NX, NY, NZ = 4, 8, 8
NT = 2 * NY
PIECE = 208
STACK = NY * PIECE
CHUNKS = ((0, 2, 80), (2, 3, 128))
NEAR = (1, 3, 2)
SENDS, RECEIVES = 13, 67
METER = 5120
LENGTH = NT * FRAMES
SCALE = HEAD**-0.5


def dot(a, b, dims):
    return lax.dot_general(a, b, (dims, ((), ())), preferred_element_type=F32)


class Names:
    def __init__(self):
        self.index = {}

    def __call__(self, name):
        return self.index.setdefault(name, len(self.index))


def kernel(
    frames_hbm,
    masked_hbm,
    counts_ref,
    gain_hbm,
    wt_ref,
    up_ref,
    down_ref,
    target_hbm,
    gup_hbm,
    gdown_hbm,
    target_ref,
    masked_ref,
    gain_ref,
    frames_ref,
    wbuf,
    upbuf,
    downbuf,
    kv,
    normed_ref,
    normed_t,
    act_ref,
    slope_ref,
    dpre_ref,
    psend,
    precv,
    cot,
    stats,
    abuf,
    bbuf,
    g32,
    gs,
    rsb,
    fown,
    foth,
    meter,
    local_sem,
    send_sem,
    recv_sem,
):
    t = lax.axis_index("tm")
    x = lax.axis_index("dp")
    z = lax.axis_index("head")
    y, c = t // 2, t % 2
    other = 1 - c
    partner = {"tm": y * 2 + other}

    def at_x(step):
        return lax.rem(x + step + NX, NX)

    def at_y(step):
        return lax.rem(y + step + NY, NY)

    def at_z(step):
        return lax.rem(z + step + NZ, NZ)

    own_w = pltpu.make_async_copy(wt_ref, wbuf.at[x], local_sem.at[0])
    own_mask = pltpu.make_async_copy(masked_hbm, masked_ref, local_sem.at[1])
    own_gain = pltpu.make_async_copy(gain_hbm, gain_ref, local_sem.at[2])
    own_frames = pltpu.make_async_copy(frames_hbm, frames_ref, local_sem.at[3])
    own_rows = pl.ds(x * SHARD, SHARD)
    own_up = pltpu.make_async_copy(up_ref, upbuf.at[own_rows, :], local_sem.at[4])
    own_down = pltpu.make_async_copy(down_ref, downbuf.at[own_rows, :], local_sem.at[5])
    for copy in (own_w, own_mask, own_gain, own_frames, own_up, own_down):
        copy.start()

    barrier = pltpu.get_barrier_semaphore()
    peers = [partner]
    for step in range(1, NY):
        for core in range(2):
            peers.append({"tm": at_y(step) * 2 + core})
    for step in range(1, NX):
        for core in range(2):
            peers.append({"dp": at_x(step), "tm": y * 2 + core})
    for step in range(1, NZ):
        peers.append({"head": at_z(step)})
    for peer in peers:
        pl.semaphore_signal(barrier, inc=1, device_id=peer, device_id_type=MESH)
    pl.semaphore_wait(barrier, len(peers))

    names, outs = Names(), Names()
    left_here = {}

    def describe(src, dst, device, name, group):
        return pltpu.make_async_remote_copy(
            src_ref=src,
            dst_ref=dst,
            send_sem=send_sem.at[outs(group)],
            recv_sem=recv_sem.at[names(name)],
            device_id=device,
            device_id_type=MESH,
        )

    def send(src, dst, device, name, group):
        describe(src, dst, device, name, group).start()
        count(src, group)

    def count(src, group):
        left_here[group] = left_here.get(group, 0) + math.prod(src.shape) * src.dtype.itemsize // 256

    def wait(dst, name):
        describe(dst, dst, partner, name, "w").wait_recv()

    def pieces(rows):
        return meter.at[pl.ds(0, rows), :]

    def wait_left(group, refs=None):
        refs = pieces(left_here[group]) if refs is None else refs
        describe(refs, refs, partner, "w1", group).wait_send()

    def place_w(shard, row, rows):
        return wbuf.at[shard, pl.ds(row, rows), :]

    def place_up(shard, row, rows):
        return upbuf.at[pl.ds(shard * SHARD + row, rows), :]

    def place_down(shard, row, rows):
        return downbuf.at[pl.ds(shard * SHARD + row, rows), :]

    class Direct:
        def __init__(self, name, place, base, half):
            self.name, self.place, self.half = name, place, half
            self.mine, self.theirs = base + c * half, base + other * half

        def start(self):
            mine = self.place(x, self.mine, self.half)
            for step in NEAR:
                send(mine, mine, {"dp": at_x(step)}, f"{self.name}{step}", "w")

        def share(self):
            for step in NEAR:
                block = self.place(at_x(-step), self.mine, self.half)
                wait(block, f"{self.name}{step}")
                send(block, block, partner, f"{self.name}P", "w")

        def finish(self):
            wait(wbuf.at[pl.ds(0, NX - 1), pl.ds(self.theirs, self.half), :], f"{self.name}P")

    class Relay:
        def __init__(self, name, place, half, first):
            self.name, self.place = name, place
            self.half, self.first = half, first
            self.mine, self.theirs = c * half, other * half

        def start(self):
            mine = self.place(x, self.mine, self.half)
            send(mine, mine, {"dp": at_x(1)}, self.name + "R0", self.name)
            send(mine, mine, {"dp": at_x(-1)}, self.name + "L0", self.name)

        def relay(self):
            n, first = self.half, self.first
            block = self.place(at_x(-1), self.mine, n)
            wait(block, self.name + "R0")
            part = self.place(at_x(-1), self.mine, first)
            send(part, part, {"dp": at_x(1)}, self.name + "R1", self.name)
            send(block, block, partner, self.name + "P0", self.name)
            block = self.place(at_x(1), self.mine, n)
            wait(block, self.name + "L0")
            part = self.place(at_x(1), self.mine + first, n - first)
            send(part, part, {"dp": at_x(-1)}, self.name + "L1", self.name)
            send(block, block, partner, self.name + "P0", self.name)

        def share(self):
            n, first = self.half, self.first
            far = at_x(2)
            part = self.place(far, self.mine, first)
            wait(part, self.name + "R1")
            send(part, part, partner, self.name + "P2", self.name)
            part = self.place(far, self.mine + first, n - first)
            wait(part, self.name + "L1")
            send(part, part, partner, self.name + "P2", self.name)

        def near(self):
            wait(self.place(0, 0, 2 * self.half), self.name + "P0")

        def far(self):
            wait(self.place(at_x(2), self.theirs, self.half), self.name + "P2")

    teacher_kv = Direct("w", place_w, CHANNELS, CHANNELS)
    teacher_q = Direct("q", place_w, 0, HEAD)
    upward = Relay("u", place_up, 160, 80)
    downward = Relay("d", place_down, 160, 80)

    own_w.wait()
    teacher_kv.start()
    teacher_q.start()

    own_mask.wait()
    keep = 1 - masked_ref[...]
    keep = keep.astype(F32)
    before = lax.broadcasted_iota(jnp.int32, (FRAMES, FRAMES), 0)
    after = lax.broadcasted_iota(jnp.int32, (FRAMES, FRAMES), 1)
    upper = jnp.where(before <= after, 1.0, 0.0).astype(BF16)
    rank = dot(jnp.broadcast_to(keep, (16, FRAMES)).astype(BF16), upper, ((1,), (0,)))[0:1]
    slot = lax.broadcasted_iota(jnp.int32, (SLOTS, FRAMES), 0).astype(F32)
    pick = jnp.where(rank - 1.0 == slot, jnp.broadcast_to(keep, (SLOTS, FRAMES)), 0.0).astype(BF16)
    own_frames.wait()
    own_gain.wait()
    chosen = dot(pick, frames_ref[...], ((1,), (0,)))
    centre = jnp.mean(chosen, axis=1, keepdims=True)
    chosen = chosen - centre
    spread = jnp.mean(chosen * chosen, axis=1, keepdims=True)
    normed = chosen * lax.rsqrt(spread + 1e-5) * gain_ref[...].reshape(1, D)
    normed_ref[...] = normed.astype(BF16)
    normed_t[...] = normed.T.astype(BF16)

    def project(low, high):
        out = jnp.zeros((high - low, FRAMES), F32)
        for shard in range(NX):
            out = out + dot(
                wbuf[shard, low:high, :], frames_ref[:, shard * SHARD : (shard + 1) * SHARD], ((1,), (1,))
            )
        return out.astype(BF16)

    def block(source, core, part):
        return kv.at[source, core, pl.ds(part * CHANNELS, CHANNELS), :]

    teacher_kv.share()
    own_up.wait()
    own_down.wait()
    upward.start()
    downward.start()
    teacher_kv.finish()
    kv[y, c] = project(CHANNELS, 3 * CHANNELS)
    right, left = {"tm": at_y(1) * 2 + c}, {"tm": at_y(-1) * 2 + c}
    for part, tag in ((0, "k"), (1, "v")):
        mine = block(y, c, part)
        send(mine, mine, right, tag + "R0", tag)
        send(mine, mine, left, tag + "L0", tag)
        send(mine, mine, partner, "s0", tag)
    teacher_q.share()
    teacher_q.finish()
    query = project(0, CHANNELS)
    query = [query[h * HEAD : (h + 1) * HEAD] for h in range(2)]

    best = [jnp.full((1, FRAMES), -jnp.inf, F32) for _ in range(2)]
    accum = [jnp.zeros((HEAD + 16, FRAMES), F32) for _ in range(2)]

    def attend(blocks):
        for h in range(2):
            keys = jnp.concatenate(
                [kv[s, core, h * HEAD : (h + 1) * HEAD, :] for s, core in blocks], axis=1
            )
            low = CHANNELS + h * HEAD
            values = jnp.concatenate(
                [kv[s, core, low : low + HEAD, :] for s, core in blocks], axis=1
            )
            values = jnp.concatenate([values, jnp.ones((16, values.shape[1]), BF16)], axis=0)
            scores = dot(keys, query[h], ((0,), (0,)))
            top = jnp.maximum(best[h], jnp.max(scores, axis=0, keepdims=True))
            fade = jnp.exp((best[h] - top) * SCALE)
            weights = jnp.exp((scores - top) * SCALE).astype(BF16)
            accum[h] = accum[h] * fade + dot(values, weights, ((1,), (0,)))
            best[h] = top

    def forward(step):
        behind, ahead = at_y(-step), at_y(step)
        for part, tag in ((0, "k"), (1, "v")):
            if step < 4 or part == 0:
                here = block(behind, c, part)
                wait(here, f"{tag}R{step - 1}")
                if step < 3 or (step == 3 and part == 0):
                    send(here, here, right, f"{tag}R{step}", tag)
                send(here, here, partner, f"s{step}", tag)
            if step < 4 or part == 1:
                here = block(ahead, c, part)
                wait(here, f"{tag}L{step - 1}")
                if step < 3 or (step == 3 and part == 1):
                    send(here, here, left, f"{tag}L{step}", tag)
                send(here, here, partner, f"s{step}", tag)

    def shared(step):
        wait(kv.at[y, other] if step in (0, 4) else kv.at[y], f"s{step}")

    me = x * 2 + c

    def operand(tag, role, source, place):
        for step in NEAR:
            send(source(at_x(step)), place(me), {"dp": at_x(step), "tm": y * 2 + role}, tag, "o" + tag[0])

        @pl.when(c == role)
        def _():
            place(me)[...] = source(x)[...]

        copy = describe(source(x), place(me), partner, tag, "partner")

        @pl.when(c != role)
        def _():
            copy.start()

        count(source(x), f"partner{1 - role}")

    def whole_a(source):
        return abuf.at[source]

    def whole_b(source):
        return bbuf.at[source]

    attend([(y, c)])
    shared(0)
    attend([(y, other)])
    def predict(shard, step):
        rows = pl.ds(shard * SHARD, SHARD)
        psend[rows, :] = dot(downbuf[rows, :], act_ref[...], ((1,), (1,))).astype(BF16)
        for half in range(2):
            to = shard * 2 + half
            source = psend.at[pl.ds(to * CHANNELS, CHANNELS), :]
            copy = describe(source, precv.at[lax.rem(to - z + NZ, NZ)], {"head": to}, "p", "p")

            @pl.when(to != z)
            def _():
                copy.start()

    forward(1)
    upward.relay()
    attend([(at_y(-1), c), (at_y(1), c)])
    shared(1)
    attend([(at_y(-1), other), (at_y(1), other)])
    downward.relay()
    forward(2)
    attend([(at_y(-2), c), (at_y(2), c)])
    shared(2)
    attend([(at_y(-2), other), (at_y(2), other)])
    upward.share()
    forward(3)
    attend([(at_y(-3), c), (at_y(3), c)])

    upward.near()
    upward.far()
    pre = dot(normed_ref[...], upbuf[...], ((1,), (0,)))
    cumulative = 0.5 * (1.0 + lax.erf(pre * math.sqrt(0.5)))
    act_ref[...] = (pre * cumulative).astype(BF16)
    slope_ref[...] = cumulative + pre * (jnp.exp(-0.5 * pre * pre) * (1.0 / math.sqrt(2 * math.pi)))

    operand("act", 0, lambda to: act_ref, whole_b)
    shared(3)
    attend([(at_y(-3), other), (at_y(3), other)])
    downward.share()
    forward(4)

    downward.near()
    for step in (0, 1, 3):
        predict(at_x(step), step)
    attend([(at_y(4), c)])
    downward.far()
    predict(at_x(2), 2)
    shared(4)
    attend([(at_y(4), other)])

    context = [accum[h][:HEAD] / accum[h][HEAD : HEAD + 1] for h in range(2)]
    lane = lax.broadcasted_iota(jnp.int32, (HEAD, 128), 1)
    columns = jnp.zeros((HEAD, 128), F32)
    for h in range(2):
        first = jnp.sum(context[h], axis=1, keepdims=True)
        second = jnp.sum(context[h] * context[h], axis=1, keepdims=True)
        columns = jnp.where(lane == h, first, jnp.where(lane == 2 + h, second, columns))
    columns = jnp.concatenate([columns, jnp.zeros((128 - HEAD, 128), F32)], axis=0)
    stats[0] = columns.T[0:8]
    for step in (8, 7, 9, 6, 10, 5, 11, 4, 12, 3, 13, 2, 14, 15, 1):
        send(stats.at[0], stats.at[step], {"tm": lax.rem(t + step, NT)}, "stats", "z")


    wait(precv.at[pl.ds(1, NZ - 1)], "p")
    pred = psend[pl.ds(z * CHANNELS, CHANNELS), :].astype(F32)
    for step in range(1, NZ):
        pred = pred + precv[step].astype(F32)
    context = jnp.concatenate(context, axis=0)
    centre = jnp.mean(context, axis=1, keepdims=True)
    raw = dot((context - centre).astype(BF16), pick, ((1,), (1,)))
    number = lax.broadcasted_iota(jnp.int32, (CHANNELS, SLOTS), 1)
    valid = number < jnp.broadcast_to(counts_ref[...], (CHANNELS, SLOTS))

    wait(stats.at[pl.ds(1, NT - 1)], "stats")
    total = stats[0]
    for step in range(1, NT):
        total = total + stats[step]
    columns = jnp.concatenate([total, jnp.zeros((120, 128), F32)], axis=0).T
    means, scales = [], []
    for h in range(2):
        mean = columns[:HEAD, h : h + 1] * (1.0 / LENGTH)
        var = columns[:HEAD, 2 + h : 3 + h] * (1.0 / LENGTH) - mean * mean
        means.append(mean)
        scales.append(lax.rsqrt(var + 1e-5))
    mean, scale = jnp.concatenate(means, axis=0), jnp.concatenate(scales, axis=0)

    aim = (raw + (centre - mean)) * scale
    gap = jnp.where(valid, pred - aim, 0.0) * (2.0 / math.sqrt(D))
    here = cot.at[pl.ds(z * CHANNELS, CHANNELS), :]
    here[...] = gap.astype(BF16)
    for step in (4, 3, 5, 2, 6, 1, 7):
        send(here, here, {"head": at_z(step)}, f"c{step}", "z")

    target_ref[...] = ((context - mean) * scale).astype(BF16)
    target_out = pltpu.make_async_copy(target_ref, target_hbm, local_sem.at[6])
    target_out.start()

    def half_a(source, half):
        return abuf.at[source, pl.ds(half * CHANNELS, CHANNELS), :]

    def pass_on(owner):
        to, half = owner // 2, lax.rem(owner, 2)
        source = cot.at[pl.ds(owner * CHANNELS, CHANNELS), :]
        copy = describe(source, half_a(me, half), {"dp": to, "tm": y * 2}, "e", "e")
        mine = jnp.logical_and(to == x, c == 0)
        away = jnp.logical_not(mine)

        @pl.when(mine)
        def _():
            half_a(me, half)[...] = source[...]

        @pl.when(away)
        def _():
            copy.start()

    def back_from(owner):
        rows = pl.ds(owner * CHANNELS, CHANNELS)
        return dot(cot[rows, :], downbuf[rows, :], ((0,), (0,)))

    operand("nrm", 1, lambda to: normed_t.at[pl.ds(to * SHARD, SHARD), :], whole_a)
    pass_on(z)
    back = back_from(z)
    for step in (1, 7, 2, 6, 3, 5, 4):
        owner = at_z(-step)
        wait(cot.at[pl.ds(owner * CHANNELS, CHANNELS), :], f"c{step}")
        pass_on(owner)
        back = back + back_from(owner)
    dpre_ref[...] = (back * slope_ref[...]).astype(BF16)
    for number, (band, bands, _) in enumerate(CHUNKS):
        columns = pl.ds(band * 128, bands * 128)
        operand(
            f"m{number}",
            1,
            lambda to, columns=columns: dpre_ref.at[:, columns],
            lambda source, columns=columns: bbuf.at[source, :, columns],
        )

    @pl.when(c == 0)
    def _():
        wait(bbuf.at[pl.ds(0, 2 * NX - 1)], "act")
        wait(abuf.at[pl.ds(0, 2 * NX - 1)], "e")

    @pl.when(c != 0)
    def _():
        wait(abuf.at[pl.ds(0, 2 * NX - 1)], "nrm")

    def eighth(number, which):
        band, _, rows = CHUNKS[number]
        return pl.ds(band * SHARD + which * rows, rows)

    def landing(number, slot):
        band, _, rows = CHUNKS[number]
        return rsb.at[slot, pl.ds(band * SHARD // NY, rows), :]

    def on_y(step):
        return {"tm": at_y(step) * 2 + c}

    even = lax.rem(y, 2) == 0
    side = 1 - 2 * lax.rem(y, 2)

    def reduce_first(number):
        band, bands, _ = CHUNKS[number]
        columns = pl.ds(band * 128, bands * 128)

        @pl.when(c != 0)
        def _():
            wait(bbuf.at[pl.ds(0, 2 * NX - 1), :, columns], f"m{number}")

        grad = jnp.zeros((SHARD, bands * 128), F32)
        for pair in range(NX):
            rows = jnp.concatenate([abuf[2 * pair], abuf[2 * pair + 1]], axis=1)
            inner = jnp.concatenate([bbuf[2 * pair, :, columns], bbuf[2 * pair + 1, :, columns]], axis=0)
            grad = grad + dot(rows, inner, ((1,), (0,)))
        for at in range(bands):
            stripe = grad[:, at * 128 : (at + 1) * 128]
            low = (band + at) * SHARD
            g32[low : low + SHARD, :] = stripe
            gs[low : low + SHARD, :] = stripe.astype(BF16)
        for slot, step, piece in (
            (0, 1, at_y(3)),
            (1, -1, at_y(-3)),
            (2, 2 * side, at_y(4)),
            (3, 1, at_y(1)),
            (4, -1, at_y(-1)),
        ):
            send(
                gs.at[eighth(number, piece), :],
                landing(number, slot),
                on_y(step),
                f"r{number}{slot // 3}",
                "y",
            )

    def reduce_second(number):
        wait(landing(number, pl.ds(0, 3)), f"r{number}0")
        far = landing(number, 2)[...].astype(F32)
        for slot, step, mine in ((5, 2, even), (6, -2, jnp.logical_not(even))):
            total = g32[eighth(number, at_y(step)), :] + landing(number, slot - 5)[...].astype(F32)
            total = total + jnp.where(mine, far, 0.0)
            out = landing(number, slot - 5 + 7)
            out[...] = total.astype(BF16)
            send(out, landing(number, slot), on_y(step), f"r{number}1", "y")

    def reduce_last(number):
        total = g32[eighth(number, y), :]
        wait(landing(number, pl.ds(3, 4)), f"r{number}1")
        for slot in (3, 4, 5, 6):
            total = total + landing(number, slot)[...].astype(F32)
        here = fown.at[eighth(number, y), :]
        here[...] = total.astype(BF16)
        for step, tag in ((2, "a"), (-2, "b"), (1, "c"), (-1, "c")):
            send(here, here, on_y(step), f"g{number}{tag}", "y")
        hand_over(number, eighth(number, y))

    def hand_over(number, rows):
        send(fown.at[rows, :], foth.at[rows, :], partner, f"h{number}", "y")

    def gather_first(number):
        size = CHUNKS[number][2]
        for step, tag in ((2, "a"), (-2, "b")):
            rows = eighth(number, at_y(-step))
            wait(fown.at[rows, :], f"g{number}{tag}")
            send(fown.at[rows, :], fown.at[rows, :], on_y(step // 2), f"g{number}d", "y")
            hand_over(number, rows)
        rows = eighth(number, at_y(-2 * side))
        send(fown.at[rows, :], fown.at[rows, :], on_y(2 * side), f"g{number}d", "y")
        wait(pieces(2 * size), f"g{number}c")
        for step in (1, -1):
            hand_over(number, eighth(number, at_y(-step)))

    def gather_last(number):
        wait(pieces(3 * CHUNKS[number][2]), f"g{number}d")
        for step in (3, -3, 4):
            hand_over(number, eighth(number, at_y(-step)))

    rest = STACK - SHARD * HIDDEN // 128
    g32[STACK - rest :, :] = jnp.zeros((rest, 128), F32)
    gs[STACK - rest :, :] = jnp.zeros((rest, 128), BF16)
    reduce_first(0)
    reduce_first(1)
    reduce_second(0)
    reduce_second(1)
    reduce_last(0)
    reduce_last(1)
    gather_first(0)
    gather_first(1)
    gather_last(0)
    gather_last(1)
    def results(number):
        band, _, rows = CHUNKS[number]
        part = pl.ds(band * SHARD, NY * rows)
        pairs = ((gdown_hbm, gup_hbm), (gup_hbm, gdown_hbm))
        return [
            [
                pltpu.make_async_copy(source.at[part, :], out.at[part, :], local_sem.at[7 + 2 * number + at])
                for at, (source, out) in enumerate(zip((fown, foth), pair))
            ]
            for pair in pairs
        ]

    written = [results(number) for number in range(len(CHUNKS))]
    for number, (band, _, rows) in enumerate(CHUNKS):
        wait(foth.at[pl.ds(band * SHARD, NY * rows), :], f"h{number}")
        for core in range(2):

            @pl.when(c == core)
            def _():
                for copy in written[number][core]:
                    copy.start()

    wait_left("w", wbuf.at[pl.ds(0, NX - 1)])
    wait_left("p", pieces((NZ - 1) * CHANNELS))
    for group in ("u", "d", "k", "v", "z", "y", "oa", "on", "om"):
        wait_left(group)

    @pl.when(c == 0)
    def _():
        wait_left("partner", pieces(left_here["partner0"]))
        wait_left("e", pieces((NZ - 2) * CHANNELS))

    @pl.when(c != 0)
    def _():
        wait_left("partner", pieces(left_here["partner1"]))
        wait_left("e", pieces(NZ * CHANNELS))

    target_out.wait()
    for core in range(2):

        @pl.when(c == core)
        def _():
            for number in range(len(CHUNKS)):
                for copy in written[number][core]:
                    copy.wait()

    assert len(names.index) <= RECEIVES and len(outs.index) <= SENDS


def widen(target_in, gup_in, gdown_in, target_out, gup_out, gdown_out, target, narrow, wide, sems):
    target_come = pltpu.make_async_copy(target_in, target, sems.at[0])
    target_go = pltpu.make_async_copy(target, target_out, sems.at[1])
    comes = [
        pltpu.make_async_copy(source, narrow.at[at], sems.at[2 + at])
        for at, source in enumerate((gup_in, gdown_in))
    ]
    for come in comes:
        come.start()
    target_come.start()
    goes = []
    for at, out in enumerate((gup_out, gdown_out)):
        comes[at].wait()
        for half in range(2):
            low, rows = half * CHANNELS, pl.ds(half * CHANNELS, CHANNELS)
            for band in range(HIDDEN // 128):
                source = narrow[at, band * SHARD + low : band * SHARD + low + CHANNELS, :]
                wide[at, low : low + CHANNELS, band * 128 : (band + 1) * 128] = source.astype(F32)
            goes.append(
                pltpu.make_async_copy(wide.at[at, rows, :], out.at[rows, :], sems.at[4 + 2 * at + half])
            )
            goes[-1].start()
    target_come.wait()
    target_go.start()
    for go in goes:
        go.wait()
    target_go.wait()


def local(frames, masked, kept_counts, teacher_qkv, student_gain, w_up, w_down):
    wt = teacher_qkv.transpose(1, 2, 0).reshape(3 * CHANNELS, SHARD)
    vmem = pl.BlockSpec(memory_space=pltpu.VMEM)
    hbm = pl.BlockSpec(memory_space=pltpu.HBM)
    target, gup, gdown = pl.pallas_call(
        kernel,
        out_shape=(
            jax.ShapeDtypeStruct((CHANNELS, FRAMES), BF16),
            jax.ShapeDtypeStruct((STACK, 128), BF16),
            jax.ShapeDtypeStruct((STACK, 128), BF16),
        ),
        in_specs=[hbm, hbm, vmem, hbm, hbm, hbm, hbm],
        out_specs=(hbm, hbm, hbm),
        scratch_shapes=[
            pltpu.VMEM((CHANNELS, FRAMES), BF16),
            pltpu.VMEM((1, FRAMES), jnp.int32),
            pltpu.VMEM((D,), F32),
            pltpu.VMEM((FRAMES, D), BF16),
            pltpu.VMEM((NX, 3 * CHANNELS, SHARD), BF16),
            pltpu.VMEM((D, HIDDEN), BF16),
            pltpu.VMEM((D, HIDDEN), BF16),
            pltpu.VMEM((NY, 2, 2 * CHANNELS, FRAMES), BF16),
            pltpu.VMEM((SLOTS, D), BF16),
            pltpu.VMEM((D, SLOTS), BF16),
            pltpu.VMEM((SLOTS, HIDDEN), BF16),
            pltpu.VMEM((SLOTS, HIDDEN), F32),
            pltpu.VMEM((SLOTS, HIDDEN), BF16),
            pltpu.VMEM((D, SLOTS), BF16),
            pltpu.VMEM((NZ, CHANNELS, SLOTS), BF16),
            pltpu.VMEM((D, SLOTS), BF16),
            pltpu.VMEM((NT, 8, 128), F32),
            pltpu.VMEM((2 * NX, SHARD, SLOTS), BF16),
            pltpu.VMEM((2 * NX, SLOTS, HIDDEN), BF16),
            pltpu.VMEM((STACK, 128), F32),
            pltpu.VMEM((STACK, 128), BF16),
            pltpu.VMEM((NY + 1, PIECE, 128), BF16),
            pltpu.VMEM((STACK, 128), BF16),
            pltpu.VMEM((STACK, 128), BF16),
            pltpu.VMEM((METER, 128), BF16),
            pltpu.SemaphoreType.DMA((11,)),
            pltpu.SemaphoreType.DMA((SENDS,)),
            pltpu.SemaphoreType.DMA((RECEIVES,)),
        ],
        compiler_params=pltpu.CompilerParams(
            collective_id=0, has_side_effects=True, vmem_limit_bytes=60 * 1024 * 1024
        ),
    )(
        frames[0],
        masked,
        kept_counts,
        student_gain,
        wt,
        w_up,
        w_down,
    )
    target, gup, gdown = pl.pallas_call(
        widen,
        out_shape=(
            jax.ShapeDtypeStruct((CHANNELS, FRAMES), BF16),
            jax.ShapeDtypeStruct((SHARD, HIDDEN), F32),
            jax.ShapeDtypeStruct((SHARD, HIDDEN), F32),
        ),
        in_specs=[hbm] * 3,
        out_specs=(hbm, hbm, hbm),
        scratch_shapes=[
            pltpu.VMEM((CHANNELS, FRAMES), BF16),
            pltpu.VMEM((2, STACK, 128), BF16),
            pltpu.VMEM((2, SHARD, HIDDEN), F32),
            pltpu.SemaphoreType.DMA((8,)),
        ],
        compiler_params=pltpu.CompilerParams(vmem_limit_bytes=60 * 1024 * 1024),
    )(target, gup, gdown)
    return target.T[None], gup, gdown


def solution(mesh):
    placed = (
        P("dp", "tm", None),
        P("dp", "tm"),
        P("dp", "tm"),
        P("dp", None, "head"),
        P(),
        P("dp", "head"),
        P("dp", "head"),
    )
    return jax.shard_map(
        local,
        mesh=mesh,
        in_specs=placed,
        out_specs=(P("dp", "tm", "head"), P("dp", "head"), P("dp", "head")),
        check_vma=False,
    )
```
